32 devices in a mesh: grp: 4 (over y, x), blk: 8 (over z, core).
Axes of the slice: x: 2, y: 2, z: 4, core: 2. Of those that a mesh axis runs over, the one named last changes fastest.
Arguments:
- walkers: bfloat16 [128, 32, 768], P('blk', 'grp'), may hold values from -6 to 6
- one_body: bfloat16 [768, 768], replicated, may hold values from -0.21875 to 0.21875
- fields: float32 [32, 96], P('grp', 'blk'), may hold values from -6 to 6
- field_diag: float32 [96, 768], P('blk'), may hold values from -0.875 to 0.875
- chol: bfloat16 [96, 128, 768], P('blk'), may hold values from -0.25 to 0.25
- weights: float32 [32], P('grp'), may hold values from 0.25 to 12, as said below
- target: int32 [32], P('grp'), may hold values from 0 to 16, as said below
Outputs:
- fock: bfloat16 [128, 32, 768], P('blk', 'grp')
The draws below stay inside these ranges and needn't reach their ends.
Inputs may be any that keep to these rules, and one draw needn't show every extreme that they name: `target`: each list of 8 slots (the slots of one index of grp) holds its live walkers in its first slots. The live walkers of all lists, in order of list and slot, carry the numbers 0 to 15, each once; a dead slot holds 16. A list holds 0 to 8 live walkers, and some list holds exactly 8. `weights`: Positive.
All inputs are finite; a program needn't handle non-finite values.
Results may differ from the reference program's by a relative error of at most 0.018.
Values may be sent and summed in bfloat16 or wider, within the bound.
No kernel may reach another device: no remote copies, remote signals or barrier semaphores. Data moves between devices by JAX's collectives and lax.ppermute only.
A program may use at most 64 MiB of HBM per device.

```python
import math
import jax
import jax.numpy as jnp
from jax import lax

NOCC = 128
NORB = 768
SLOTS = 8
WALKERS = 32
LIVE = 16
NCHOL = 96


def draw_target(key, part):
    groups = WALKERS // SLOTS
    first_key, second_key = jax.random.split(jax.random.fold_in(key, 11))
    halves = jax.random.randint(first_key, (groups // 2,), 0, SLOTS + 1)
    halves = halves.at[0].set(SLOTS)
    counts = jnp.stack([halves, SLOTS - halves], axis=1).reshape(groups)
    counts = jax.random.permutation(second_key, counts)
    starts = jnp.cumsum(counts) - counts
    position = jnp.arange(SLOTS)
    target = jnp.where(position[None, :] < counts[:, None], starts[:, None] + position[None, :], LIVE)
    return target.reshape(WALKERS).astype(jnp.int32)


def draw_weights(key, part):
    groups = WALKERS // SLOTS
    sample_key = jax.random.fold_in(key, 23)
    sample = jnp.exp(jax.random.uniform(sample_key, (WALKERS,), jnp.float32, math.log(0.5), math.log(2.0)))
    rising = 3.0 ** (jnp.arange(WALKERS) // SLOTS / max(groups - 1, 1))
    return (sample * rising).astype(jnp.float32)


def levels(key, dims, pieces, smallest, high):
    loudness = 1.0
    for dim, blocks in pieces:
        heights = jax.random.uniform(jax.random.fold_in(jax.random.fold_in(key, 6), dim), (blocks,), jnp.float32, smallest / len(pieces), high / len(pieces))
        loudness = loudness * jnp.repeat(jnp.exp(heights), dims[dim] // blocks).reshape((-1,) + (1,) * (len(dims) - 1 - dim))
    return loudness


def noise(key, shape, spread, limit, cuts=(), held_as=jnp.bfloat16):
    gain = levels(key, shape, cuts, -0.22, 0.18) if cuts else 1.0
    drawn = jax.random.normal(key, shape, jnp.float32) * spread * gain
    return jnp.minimum(jnp.maximum(drawn, -limit), limit).astype(held_as)


def setup_inputs(seed: int = 0) -> dict:
    keys = jax.random.split(jax.random.key(seed), 8)
    walkers = noise(keys[0], (NOCC, WALKERS, NORB), 1.0, 6.0, ((0, 8), (1, 4)))
    one_body = noise(keys[1], (NORB, NORB), NORB ** -0.5, 0.21875)
    fields = noise(keys[2], (WALKERS, NCHOL), 1.0, 6.0, ((0, 4), (1, 8)), jnp.float32)
    field_diag = noise(keys[3], (NCHOL, NORB), (0.6 * NCHOL ** -0.5), 0.875, ((0, 8),), jnp.float32)
    chol = noise(keys[4], (NCHOL, NOCC, NORB), ((NORB * NOCC * NCHOL) ** -0.25), 0.25, ((0, 8),))
    weights = draw_weights(jax.random.fold_in(keys[7], 71), 0)
    target = draw_target(jax.random.fold_in(keys[7], 71), 0)
    return {"walkers": walkers, "one_body": one_body, "fields": fields, "field_diag": field_diag, "chol": chol, "weights": weights, "target": target}


def reference(walkers, one_body, fields, field_diag, chol, weights, target):
    exponent = jnp.dot(fields, field_diag, precision=lax.Precision.HIGHEST)
    scaled = (walkers.astype(jnp.float32) * jnp.exp(exponent)[None]).astype(jnp.bfloat16)
    propagated = jnp.dot(scaled.reshape(-1, NORB), one_body, preferred_element_type=jnp.float32)
    propagated = propagated.astype(jnp.bfloat16).reshape(NOCC, WALKERS, NORB)
    vectors = chol.reshape(NCHOL * NOCC, NORB)

    def measure(walker_block):
        coupling = lax.dot_general(walker_block, vectors, (((1,), (1,)), ((), ())), preferred_element_type=jnp.float32)
        coupling = coupling.astype(jnp.bfloat16).reshape(NOCC, NCHOL, NOCC)
        flipped = jnp.transpose(coupling, (2, 1, 0)).reshape(NOCC, NCHOL * NOCC)
        return jnp.dot(flipped, vectors, preferred_element_type=jnp.float32).astype(jnp.bfloat16)

    fock_raw = lax.map(measure, jnp.transpose(propagated, (1, 0, 2)))
    fock_raw = lax.optimization_barrier(jnp.transpose(fock_raw, (1, 0, 2)))
    active = target < LIVE
    weight_sum = jnp.sum(jnp.where(active, weights, jnp.float32(0.0)))
    factor = jnp.where(active, weights * LIVE / weight_sum, jnp.float32(0.0))
    return (fock_raw.astype(jnp.float32) * factor[None, :, None]).astype(jnp.bfloat16)
```

```python
import functools
import jax
import jax.numpy as jnp
from jax import lax
from jax.experimental import pallas as pl
from jax.experimental.pallas import tpu as pltpu
from jax.sharding import PartitionSpec as P

F32 = jnp.float32
BF16 = jnp.bfloat16


def pack_kernel(walkers_ref, fields_ref, diag_ref, out_ref, wide):
    rows, slots, orbitals = walkers_ref.shape
    vec_count = fields_ref.shape[1]
    half = slots // 2
    wide[...] = walkers_ref[...].astype(F32)
    part = fields_ref[:, 0:1] * diag_ref[0:1, :]
    for g in range(1, vec_count):
        part = part + fields_ref[:, g : g + 1] * diag_ref[g : g + 1, :]
    high = part.astype(BF16).astype(F32)
    low = part - high
    for h in range(2):
        pieces = [wide[:, h * half + w, :] for w in range(half)]
        pieces += [high[h * half : (h + 1) * half], low[h * half : (h + 1) * half]]
        out_ref[h] = jnp.concatenate(pieces, axis=0).astype(BF16)


def fock_kernel(rows, half, recv_ref, body_ref, own_ref, sib_ref, out_ref, prop, turned, coup):
    n = recv_ref.shape[0]
    vec_count, occupied, orbitals = own_ref.shape
    slab = rows * half
    exponent = jnp.zeros((half, orbitals), F32)
    for s in range(n):
        tail = recv_ref[s, slab:, :].astype(F32)
        exponent = exponent + (tail[:half] + tail[half:])
    growth = jnp.exp(exponent)
    for s in range(n):
        for w in range(half):
            block = recv_ref[s, w * rows : (w + 1) * rows, :].astype(F32)
            prop[w * occupied + s * rows : w * occupied + (s + 1) * rows, :] = (
                block * growth[w : w + 1]
            ).astype(BF16)
    for w in range(half):
        piece = prop[w * occupied : (w + 1) * occupied, :]
        done = jnp.dot(piece, body_ref[...], preferred_element_type=F32)
        turned[:, w * occupied : (w + 1) * occupied] = done.T.astype(BF16)
    pair = 2 if vec_count % 2 == 0 else 1
    for c, ref in enumerate((own_ref, sib_ref)):
        for g in range(0, vec_count, pair):
            left = ref[g : g + pair].reshape(pair * occupied, orbitals)
            s = jnp.dot(left, turned[...], preferred_element_type=F32).astype(BF16)
            for k in range(pair):
                for w in range(half):
                    coup[
                        w * occupied : (w + 1) * occupied,
                        (c * vec_count + g + k) * occupied : (c * vec_count + g + k + 1) * occupied,
                    ] = s[k * occupied : (k + 1) * occupied, w * occupied : (w + 1) * occupied]
    tile = 256 if orbitals % 256 == 0 else orbitals
    depth = vec_count * occupied
    for t in range(0, orbitals, tile):
        total = jnp.dot(
            coup[:, :depth],
            own_ref[:, :, t : t + tile].reshape(depth, tile),
            preferred_element_type=F32,
        )
        total = total + jnp.dot(
            coup[:, depth:],
            sib_ref[:, :, t : t + tile].reshape(depth, tile),
            preferred_element_type=F32,
        )
        total = total.astype(BF16)
        for s in range(n):
            for w in range(half):
                out_ref[s, w * rows : (w + 1) * rows, t : t + tile] = total[
                    w * occupied + s * rows : w * occupied + (s + 1) * rows, :
                ]


def sum_kernel(recv_ref, factor_ref, out_ref, wide):
    n = recv_ref.shape[0]
    rows, slots, orbitals = out_ref.shape
    half = slots // 2
    for h in range(2):
        total = recv_ref[h].astype(F32)
        for s in range(h + 2, n, 2):
            total = total + recv_ref[s].astype(F32)
        for w in range(half):
            slot = h * half + w
            raw = total[w * rows : (w + 1) * rows].astype(BF16).astype(F32)
            wide[:, slot, :] = raw * factor_ref[slot]
    out_ref[...] = wide[...].astype(BF16)


def axis_sum(value, name):
    size = lax.axis_size(name)
    if size & (size - 1) == 0:
        step = 1
        while step < size:
            value = value + lax.ppermute(value, name, [(i, i ^ step) for i in range(size)])
            step *= 2
        return value
    total = value
    for step in range(1, size):
        total = total + lax.ppermute(value, name, [(i, (i + step) % size) for i in range(size)])
    return total


def vmem():
    return pl.BlockSpec(memory_space=pltpu.VMEM)


def params():
    return pltpu.CompilerParams(vmem_limit_bytes=40 * 2**20)


def body(walkers, one_body, fields, field_diag, chol, weights, target):
    rows, slots, orbitals = walkers.shape
    vec_count, occupied, _ = chol.shape
    half = slots // 2
    n = lax.axis_size("blk")
    slab = rows * half
    packed = pl.pallas_call(
        pack_kernel,
        out_shape=jax.ShapeDtypeStruct((2, slab + slots, orbitals), BF16),
        in_specs=[vmem()] * 3,
        out_specs=vmem(),
        scratch_shapes=[pltpu.VMEM((rows, slots, orbitals), F32)],
        compiler_params=params(),
        name="pack",
    )(walkers, fields, field_diag)
    send = jnp.broadcast_to(packed[None], (n // 2,) + packed.shape).reshape((n,) + packed.shape[1:])
    sibling = lax.ppermute(chol, "blk", [(i, i ^ 1) for i in range(n)])
    recv = lax.all_to_all(send, "blk", 0, 0, tiled=True)
    live_total = slots // 2 * lax.axis_size("grp")
    active = target < live_total
    weight_sum = axis_sum(jnp.sum(jnp.where(active, weights, F32(0.0)), keepdims=True), "grp")
    factor = jnp.where(active, weights * live_total / weight_sum, F32(0.0))
    flops = 2 * n * slab * orbitals * (orbitals + 4 * vec_count * occupied)
    part = pl.pallas_call(
        functools.partial(fock_kernel, rows, half),
        out_shape=jax.ShapeDtypeStruct((n, slab, orbitals), BF16),
        in_specs=[vmem()] * 4,
        out_specs=vmem(),
        scratch_shapes=[
            pltpu.VMEM((half * occupied, orbitals), BF16),
            pltpu.VMEM((orbitals, half * occupied), BF16),
            pltpu.VMEM((half * occupied, 2 * vec_count * occupied), BF16),
        ],
        compiler_params=params(),
        cost_estimate=pl.CostEstimate(flops=flops, bytes_accessed=8 * 2**20, transcendentals=0),
        name="fock",
    )(recv, one_body, chol, sibling)
    back = lax.all_to_all(part, "blk", 0, 0, tiled=True)
    return pl.pallas_call(
        sum_kernel,
        out_shape=jax.ShapeDtypeStruct(walkers.shape, BF16),
        in_specs=[vmem(), pl.BlockSpec(memory_space=pltpu.SMEM)],
        out_specs=vmem(),
        scratch_shapes=[pltpu.VMEM(walkers.shape, F32)],
        compiler_params=params(),
        name="sum",
    )(back, factor)


def solution(mesh):
    in_specs = (
        P("blk", "grp", None),
        P(),
        P("grp", "blk"),
        P("blk", None),
        P("blk", None, None),
        P("grp"),
        P("grp"),
    )
    out_specs = P("blk", "grp", None)
    return jax.shard_map(body, mesh=mesh, in_specs=in_specs, out_specs=out_specs, check_vma=False)
```

```python
import functools
import jax
import jax.numpy as jnp
from jax import lax
from jax.experimental import pallas as pl
from jax.experimental.pallas import tpu as pltpu
from jax.sharding import PartitionSpec as P

F32 = jnp.float32
BF16 = jnp.bfloat16
LANES = 128


def terms(value, count):
    out = []
    for _ in range(count):
        term = value.astype(BF16).astype(F32)
        out.append(term)
        value = value - term
    return out


def padded(pieces, rows):
    have = sum(p.shape[0] for p in pieces)
    if have < rows:
        pieces = list(pieces) + [jnp.zeros((rows - have, pieces[0].shape[1]), F32)]
    return jnp.concatenate(pieces, axis=0)


def route_kernel(keep, me_ref, target_ref, weights_ref, walkers_ref, fields_ref, *refs):
    rows, slots, orbitals = walkers_ref.shape
    vec_count = fields_ref.shape[1]
    *outs, wide, blocks, lines = refs
    groups = len(outs)
    live = groups * keep
    wide[...] = walkers_ref[...].astype(F32)
    blocks[...] = jnp.zeros(blocks.shape, F32)
    lines[...] = jnp.zeros(lines.shape, F32)
    weight = F32(0.0)
    for slot in range(slots):
        t = jnp.minimum(target_ref[slot], live)
        weight = weight + jnp.where(t < live, weights_ref[slot], F32(0.0))
        blocks[t] = wide[:, slot, :]
        lines[t, :, 0:vec_count] = fields_ref[slot : slot + 1, :]
    sums = terms(jnp.full((1, LANES), weight, F32), 3)
    for s, out in enumerate(outs):
        base = lax.rem(me_ref[0] + s, groups) * keep
        out[:, 0:orbitals] = jnp.concatenate([blocks[base + k] for k in range(keep)], axis=0).astype(BF16)
        line = jnp.concatenate([lines[base + k] for k in range(keep)], axis=0)
        out[:, orbitals:] = padded(terms(line, 3) + sums, keep * rows).astype(BF16)


def merge_kernel(keep, groups, core_ref, diag_ref, *refs):
    ins, (same_ref, other_ref, weight_ref) = refs[:groups], refs[groups:]
    vec_count, orbitals = diag_ref.shape
    half = keep // 2
    slab = same_ref.shape[0]
    total = ins[0][...].astype(F32)
    for ref in ins[1:]:
        total = total + ref[...].astype(F32)
    tail = total[:, orbitals:]
    line = tail[0:keep] + tail[keep : 2 * keep] + tail[2 * keep : 3 * keep]
    weight = jnp.zeros((1, LANES), F32)
    for ref in ins:
        part = ref[:, orbitals:].astype(F32)
        weight = weight + (part[3 * keep : 3 * keep + 1] + part[3 * keep + 1 : 3 * keep + 2] + part[3 * keep + 2 : 3 * keep + 3])
    weight_ref[...] = jnp.broadcast_to(weight, weight_ref.shape)
    exponent = line[:, 0:1] * diag_ref[0:1, :]
    for g in range(1, vec_count):
        exponent = exponent + line[:, g : g + 1] * diag_ref[g : g + 1, :]
    full = []
    for h in range(2):
        pieces = []
        for term in terms(exponent[h * half : (h + 1) * half], 2):
            pieces += [term[k : k + 1, c : c + LANES] for k in range(half) for c in range(0, orbitals, LANES)]
        parts = [total[h * slab : (h + 1) * slab, 0:orbitals]]
        for b in range(0, len(pieces), slab):
            parts.append(padded(pieces[b : b + slab], slab))
        full.append(jnp.concatenate(parts, axis=1))
    first = core_ref[0] == 0
    same_ref[...] = jnp.where(first, full[0], full[1]).astype(BF16)
    other_ref[...] = jnp.where(first, full[1], full[0]).astype(BF16)


def hops(n):
    return [(s, e) for s in range(n // 2) for e in range(2)]


def partner(blk, s, e, n, sign):
    chip = lax.rem(lax.div(blk, 2) + (s if sign > 0 else n // 2 - s), n // 2)
    core = lax.rem(blk, 2)
    return 2 * chip + (core if e == 0 else 1 - core)


def fock_kernel(n, half, blk_ref, body_ref, own_ref, sib_ref, *refs):
    ins, outs = refs[:n], refs[n : 2 * n]
    prop, turned, coup, result = refs[2 * n :]
    vec_count, occupied, orbitals = own_ref.shape
    slab = outs[0].shape[0]
    rows = slab // half
    blocks = orbitals // LANES
    blk = blk_ref[0]
    exponent = jnp.zeros((2 * half * blocks, LANES), F32)
    for ref in ins:
        pieces = [ref[:, c : c + LANES].astype(F32) for c in range(orbitals, ref.shape[1], LANES)]
        exponent = exponent + jnp.concatenate(pieces, axis=0)[0 : 2 * half * blocks]
    growth = jnp.exp(exponent[0 : half * blocks] + exponent[half * blocks :])
    for ref, (s, e) in zip(ins, hops(n)):
        source = partner(blk, s, e, n, -1)
        for w in range(half):
            for c in range(blocks):
                piece = ref[w * rows : (w + 1) * rows, c * LANES : (c + 1) * LANES].astype(F32)
                prop[w, source, :, c * LANES : (c + 1) * LANES] = piece * growth[w * blocks + c : w * blocks + c + 1]
    for w in range(half):
        piece = jnp.concatenate([prop[w, i] for i in range(n)], axis=0).astype(BF16)
        done = jnp.dot(piece, body_ref[...], preferred_element_type=F32)
        turned[:, w * occupied : (w + 1) * occupied] = done.T.astype(BF16)
    pair = 2 if vec_count % 2 == 0 else 1
    for c, ref in enumerate((own_ref, sib_ref)):
        for g in range(0, vec_count, pair):
            left = ref[g : g + pair].reshape(pair * occupied, orbitals)
            s = jnp.dot(left, turned[...], preferred_element_type=F32).astype(BF16)
            for k in range(pair):
                at = (c * vec_count + g + k) * occupied
                for w in range(half):
                    coup[w * occupied : (w + 1) * occupied, at : at + occupied] = s[
                        k * occupied : (k + 1) * occupied, w * occupied : (w + 1) * occupied
                    ]
    tile = 256 if orbitals % 256 == 0 else orbitals
    depth = vec_count * occupied
    for t in range(0, orbitals, tile):
        total = jnp.dot(
            coup[:, :depth],
            own_ref[:, :, t : t + tile].reshape(depth, tile),
            preferred_element_type=F32,
        )
        total = total + jnp.dot(
            coup[:, depth:],
            sib_ref[:, :, t : t + tile].reshape(depth, tile),
            preferred_element_type=F32,
        )
        for w in range(half):
            for i in range(n):
                at = w * occupied + i * rows
                result[w, i, :, t : t + tile] = total[at : at + rows]
    for out, (s, e) in zip(outs, hops(n)):
        to = partner(blk, s, e, n, 1)
        for w in range(half):
            out[w * rows : (w + 1) * rows, :] = result[w, to].astype(BF16)


def sum_kernel(n, core_ref, *refs):
    ins, out_ref = refs[:n], refs[n]
    slab = ins[0].shape[0]
    halves = []
    for e in range(2):
        total = ins[e][...].astype(F32)
        for ref in ins[e + 2 :: 2]:
            total = total + ref[...].astype(F32)
        halves.append(total)
    first = core_ref[0] == 0
    out_ref[0:slab, :] = jnp.where(first, halves[0], halves[1]).astype(BF16)
    out_ref[slab:, :] = jnp.where(first, halves[1], halves[0]).astype(BF16)


def deal_kernel(keep, groups, me_ref, target_ref, weights_ref, total_ref, *refs):
    ins, (out_ref, blocks, wide) = refs[:groups], refs[groups:]
    rows, slots, orbitals = out_ref.shape
    live = groups * keep
    for s, ref in enumerate(ins):
        base = lax.rem(me_ref[0] + groups - s, groups) * keep
        for k in range(keep):
            blocks[base + k] = ref[k * rows : (k + 1) * rows, :].astype(F32)
    blocks[live] = jnp.zeros((rows, orbitals), F32)
    for slot in range(slots):
        t = jnp.minimum(target_ref[slot], live)
        weight = jnp.where(t < live, weights_ref[slot], F32(0.0))
        factor = jnp.full((1, LANES), weight * live, F32) / total_ref[0:1, :]
        wide[:, slot, :] = blocks[t] * factor[:, 0:1]
    out_ref[...] = wide[...].astype(BF16)


def call(kernel, outs, scalars, arrays, scratch, name, flops=0, vmem=40):
    smem = pl.BlockSpec(memory_space=pltpu.SMEM)
    full = pl.BlockSpec(memory_space=pltpu.VMEM)
    size = sum(x.size * x.dtype.itemsize for x in list(arrays) + list(outs))
    return pl.pallas_call(
        kernel,
        out_shape=outs,
        in_specs=[smem] * len(scalars) + [full] * len(arrays),
        out_specs=[full] * len(outs),
        scratch_shapes=scratch,
        compiler_params=pltpu.CompilerParams(vmem_limit_bytes=vmem * 2**20),
        cost_estimate=pl.CostEstimate(flops=flops, bytes_accessed=size, transcendentals=0),
        name=name,
    )(*scalars, *arrays)


def body(walkers, one_body, fields, field_diag, chol, weights, target):
    rows, slots, orbitals = walkers.shape
    vec_count, occupied, _ = chol.shape
    n, groups = lax.axis_size("blk"), lax.axis_size("grp")
    keep = slots // 2
    half = keep // 2
    slab = half * rows
    shape = jax.ShapeDtypeStruct
    grp = lax.axis_index("grp").reshape(1)
    blk = lax.axis_index("blk").reshape(1)
    core = lax.rem(blk, 2)

    def to_list(x, s):
        return lax.ppermute(x, "grp", [(i, (i + s) % groups) for i in range(groups)]) if s else x

    def to_block(x, s, e):
        if not s and not e:
            return x
        return lax.ppermute(x, "blk", [(i, (2 * (i // 2 + s) + (i % 2 ^ e)) % n) for i in range(n)])

    sibling = to_block(chol, 0, 1)
    routed = call(
        functools.partial(route_kernel, keep),
        [shape((keep * rows, orbitals + LANES), BF16)] * groups,
        [grp, target, weights],
        [walkers, fields],
        [
            pltpu.VMEM((rows, slots, orbitals), F32),
            pltpu.VMEM((groups * keep + 1, rows, orbitals), F32),
            pltpu.VMEM((groups * keep + 1, 1, LANES), F32),
        ],
        "route",
    )
    routed = [to_list(x, s) for s, x in enumerate(routed)]
    extra = -(-2 * half * (orbitals // LANES) // slab)
    payload = shape((slab, orbitals + extra * LANES), BF16)
    same, other, weight_sum = call(
        functools.partial(merge_kernel, keep, groups),
        [payload, payload, shape((8, LANES), F32)],
        [core],
        [field_diag] + routed,
        [],
        "merge",
    )
    gathered = [to_block(other if e else same, s, e) for s, e in hops(n)]
    parts = call(
        functools.partial(fock_kernel, n, half),
        [shape((slab, orbitals), BF16)] * n,
        [blk],
        [one_body, chol, sibling] + gathered,
        [
            pltpu.VMEM((half, n, rows, orbitals), F32),
            pltpu.VMEM((orbitals, half * occupied), BF16),
            pltpu.VMEM((half * occupied, 2 * vec_count * occupied), BF16),
            pltpu.VMEM((half, n, rows, orbitals), F32),
        ],
        "fock",
        flops=2 * n * slab * orbitals * (orbitals + 4 * vec_count * occupied),
    )
    parts = [to_block(x, s, e) for x, (s, e) in zip(parts, hops(n))]
    (raw,) = call(
        functools.partial(sum_kernel, n),
        [shape((keep * rows, orbitals), BF16)],
        [core],
        parts,
        [],
        "sum",
    )
    back = [to_list(raw, s) for s in range(groups)]
    (out,) = call(
        functools.partial(deal_kernel, keep, groups),
        [shape(walkers.shape, BF16)],
        [grp, target, weights],
        [weight_sum] + back,
        [pltpu.VMEM((groups * keep + 1, rows, orbitals), F32), pltpu.VMEM(walkers.shape, F32)],
        "deal",
    )
    return out


def solution(mesh):
    in_specs = (
        P("blk", "grp", None),
        P(),
        P("grp", "blk"),
        P("blk", None),
        P("blk", None, None),
        P("grp"),
        P("grp"),
    )
    out_specs = P("blk", "grp", None)
    return jax.shard_map(body, mesh=mesh, in_specs=in_specs, out_specs=out_specs, check_vma=False)
```

```python
import functools
import jax
import jax.numpy as jnp
from jax import lax
from jax.experimental import pallas as pl
from jax.experimental.pallas import tpu as pltpu
from jax.sharding import PartitionSpec as P

F32 = jnp.float32
BF16 = jnp.bfloat16
LANES = 128


def terms(value, count):
    out = []
    for _ in range(count):
        term = value.astype(BF16).astype(F32)
        out.append(term)
        value = value - term
    return out


def tail_blocks(count, slab):
    return -(-count // slab)


def write_tail(out_ref, start, lines):
    slab = out_ref.shape[0]
    for b in range(tail_blocks(lines.shape[0], slab)):
        part = lines[b * slab : (b + 1) * slab]
        if part.shape[0] < slab:
            part = jnp.concatenate([part, jnp.zeros((slab - part.shape[0], LANES), F32)], axis=0)
        out_ref[:, start + b * LANES : start + (b + 1) * LANES] = part.astype(BF16)


def read_tail(ref, start, count):
    parts = [ref[:, c : c + LANES].astype(F32) for c in range(start, ref.shape[1], LANES)]
    whole = parts[0] if len(parts) == 1 else jnp.concatenate(parts, axis=0)
    return whole[0:count]


def wide_mask(line, width):
    return jnp.concatenate([line] * (width // LANES), axis=1) > 0


def stage_kernel(*refs):
    count = (len(refs) - 1) // 2
    sems = refs[-1]
    copies = [pltpu.make_async_copy(refs[i], refs[count + i], sems.at[i]) for i in range(count)]
    for copy in copies:
        copy.start()
    for copy in copies:
        copy.wait()


def route_kernel(keep, cap, me_ref, target_any, weights_any, walkers_any, fields_any, *refs):
    *outs, target_ref, weights_ref, walkers_ref, fields_ref, wide, blocks, lines, sems = refs
    pairs = (
        (walkers_any, walkers_ref),
        (target_any, target_ref),
        (weights_any, weights_ref),
        (fields_any, fields_ref),
    )
    copies = [pltpu.make_async_copy(a, b, sems.at[i]) for i, (a, b) in enumerate(pairs)]
    for copy in copies:
        copy.start()
    rows, slots, orbitals = walkers_ref.shape
    vec_count = fields_ref.shape[1]
    groups = len(outs)
    live = groups * keep
    blocks[...] = jnp.zeros(blocks.shape, F32)
    lines[...] = jnp.zeros(lines.shape, F32)
    for copy in copies:
        copy.wait()
    wide[...] = walkers_ref[...].astype(F32)
    weight = F32(0.0)
    lane = lax.broadcasted_iota(jnp.int32, (1, LANES), 1)
    for slot in range(slots):
        t = target_ref[slot]
        alive = t < live
        weight = weight + jnp.where(alive, weights_ref[slot], F32(0.0))
        turn = lax.div(t, groups)
        at = jnp.where(alive, lax.rem(t, groups) * cap + lax.rem(turn, cap), groups * cap)
        blocks[at] = wide[:, slot, :]
        lines[at] = jnp.where(lane == LANES - 1, (turn + 1).astype(F32), F32(0.0))
        lines[at, :, 0:vec_count] = fields_ref[slot : slot + 1, :]
    sums = terms(jnp.full((1, LANES), weight, F32), 3)
    for s, out in enumerate(outs):
        base = lax.rem(me_ref[0] + s, groups) * cap
        out[:, 0:orbitals] = jnp.concatenate([blocks[base + k] for k in range(cap)], axis=0).astype(BF16)
        line = jnp.concatenate([lines[base + k] for k in range(cap)], axis=0)
        write_tail(out, orbitals, jnp.concatenate(terms(line, 3) + sums, axis=0))


def merge_kernel(keep, cap, groups, core_ref, diag_ref, *refs):
    ins, (same_ref, other_ref, weight_ref, pick_ref) = refs[:groups], refs[groups:]
    vec_count, orbitals = diag_ref.shape
    half = keep // 2
    rows = ins[0].shape[0] // cap
    slab = half * rows
    weight = jnp.zeros((1, LANES), F32)
    walker = [jnp.zeros((rows, orbitals), F32)] * keep
    line = [jnp.zeros((1, LANES), F32)] * keep
    for s, ref in enumerate(ins):
        tail = read_tail(ref, orbitals, 3 * cap + 3)
        weight = weight + (tail[3 * cap : 3 * cap + 1] + tail[3 * cap + 1 : 3 * cap + 2] + tail[3 * cap + 2 :])
        for k in range(cap):
            fields = tail[k : k + 1] + tail[cap + k : cap + k + 1] + tail[2 * cap + k : 2 * cap + k + 1]
            flag = jnp.broadcast_to(fields[:, LANES - 1 : LANES], (1, LANES))
            block = ref[k * rows : (k + 1) * rows, 0:orbitals].astype(F32)
            for m in range(k, keep, cap):
                mine = jnp.where(flag == m + 1, F32(1.0), F32(0.0))
                pick_ref[s * keep + m : s * keep + m + 1, :] = mine
                walker[m] = jnp.where(wide_mask(mine, orbitals), block, walker[m])
                line[m] = jnp.where(mine > 0, fields, line[m])
    weight_ref[...] = jnp.broadcast_to(weight, weight_ref.shape)
    fields = jnp.concatenate(line, axis=0)
    exponent = fields[:, 0:1] * diag_ref[0:1, :]
    for g in range(1, vec_count):
        exponent = exponent + fields[:, g : g + 1] * diag_ref[g : g + 1, :]
    first = core_ref[0] == 0
    high, low = terms(exponent, 2)
    for out, order in ((same_ref, (0, 1)), (other_ref, (1, 0))):
        for k in range(half):
            picked = jnp.where(first, walker[order[0] * half + k], walker[order[1] * half + k])
            out[k * rows : (k + 1) * rows, 0:orbitals] = picked.astype(BF16)
        pieces = []
        for term in (high, low):
            for k in range(half):
                a, b = order[0] * half + k, order[1] * half + k
                picked = jnp.where(first, term[a : a + 1], term[b : b + 1])
                pieces += [picked[:, c : c + LANES] for c in range(0, orbitals, LANES)]
        write_tail(out, orbitals, jnp.concatenate(pieces, axis=0))


def hops(n):
    return [(s, e) for s in range(n // 2) for e in range(2)]


def partner(blk, s, e, n, sign):
    chip = lax.rem(lax.div(blk, 2) + (s if sign > 0 else n // 2 - s), n // 2)
    core = lax.rem(blk, 2)
    return 2 * chip + (core if e == 0 else 1 - core)


def fock_kernel(n, half, blk_ref, body_ref, own_ref, sib_ref, *refs):
    ins, outs = refs[:n], refs[n : 2 * n]
    prop, turned, coup, result = refs[2 * n :]
    vec_count, occupied, orbitals = own_ref.shape
    slab = outs[0].shape[0]
    rows = slab // half
    blocks = orbitals // LANES
    blk = blk_ref[0]
    exponent = jnp.zeros((2 * half * blocks, LANES), F32)
    for ref in ins:
        exponent = exponent + read_tail(ref, orbitals, 2 * half * blocks)
    growth = jnp.exp(exponent[0 : half * blocks] + exponent[half * blocks :])
    for ref, (s, e) in zip(ins, hops(n)):
        source = partner(blk, s, e, n, -1)
        for w in range(half):
            for c in range(blocks):
                piece = ref[w * rows : (w + 1) * rows, c * LANES : (c + 1) * LANES].astype(F32)
                prop[w, source, :, c * LANES : (c + 1) * LANES] = piece * growth[w * blocks + c : w * blocks + c + 1]
    for w in range(half):
        piece = jnp.concatenate([prop[w, i] for i in range(n)], axis=0).astype(BF16)
        done = jnp.dot(piece, body_ref[...], preferred_element_type=F32)
        turned[:, w * occupied : (w + 1) * occupied] = done.T.astype(BF16)
    pair = 2 if vec_count % 2 == 0 else 1
    for c, ref in enumerate((own_ref, sib_ref)):
        for g in range(0, vec_count, pair):
            left = ref[g : g + pair].reshape(pair * occupied, orbitals)
            s = jnp.dot(left, turned[...], preferred_element_type=F32).astype(BF16)
            for k in range(pair):
                at = (c * vec_count + g + k) * occupied
                for w in range(half):
                    coup[w * occupied : (w + 1) * occupied, at : at + occupied] = s[
                        k * occupied : (k + 1) * occupied, w * occupied : (w + 1) * occupied
                    ]
    tile = 256 if orbitals % 256 == 0 else orbitals
    depth = vec_count * occupied
    for t in range(0, orbitals, tile):
        total = jnp.dot(
            coup[:, :depth],
            own_ref[:, :, t : t + tile].reshape(depth, tile),
            preferred_element_type=F32,
        )
        total = total + jnp.dot(
            coup[:, depth:],
            sib_ref[:, :, t : t + tile].reshape(depth, tile),
            preferred_element_type=F32,
        )
        for w in range(half):
            for i in range(n):
                at = w * occupied + i * rows
                result[w, i, :, t : t + tile] = total[at : at + rows]
    for out, (s, e) in zip(outs, hops(n)):
        to = partner(blk, s, e, n, 1)
        for w in range(half):
            out[w * rows : (w + 1) * rows, :] = result[w, to].astype(BF16)


def sum_kernel(n, keep, cap, groups, core_ref, pick_ref, *refs):
    ins, outs = refs[:n], refs[n:]
    slab, orbitals = ins[0].shape
    half = keep // 2
    rows = slab // half
    halves = []
    for e in range(2):
        total = ins[e][...].astype(F32)
        for ref in ins[e + 2 :: 2]:
            total = total + ref[...].astype(F32)
        halves.append(total)
    first = core_ref[0] == 0
    whole = [jnp.where(first, halves[0], halves[1]), jnp.where(first, halves[1], halves[0])]
    walker = [whole[m // half][(m % half) * rows : (m % half + 1) * rows] for m in range(keep)]
    for s, out in enumerate(outs):
        source = (groups - s) % groups
        for k in range(cap):
            value = jnp.zeros((rows, orbitals), F32)
            for m in range(k, keep, cap):
                mine = pick_ref[source * keep + m : source * keep + m + 1, :]
                value = jnp.where(wide_mask(mine, orbitals), walker[m], value)
            out[k * rows : (k + 1) * rows, :] = value.astype(BF16)


def deal_kernel(keep, cap, groups, me_ref, target_ref, weights_ref, total_ref, *refs):
    ins, (out_ref, blocks, wide) = refs[:groups], refs[groups:]
    rows, slots, orbitals = out_ref.shape
    live = groups * keep
    for s, ref in enumerate(ins):
        base = lax.rem(me_ref[0] + groups - s, groups) * cap
        for k in range(cap):
            blocks[base + k] = ref[k * rows : (k + 1) * rows, :].astype(F32)
    blocks[groups * cap] = jnp.zeros((rows, orbitals), F32)
    for slot in range(slots):
        t = target_ref[slot]
        alive = t < live
        at = jnp.where(alive, lax.rem(t, groups) * cap + lax.rem(lax.div(t, groups), cap), groups * cap)
        weight = jnp.where(alive, weights_ref[slot], F32(0.0))
        factor = jnp.full((1, LANES), weight * live, F32) / total_ref[0:1, :]
        wide[:, slot, :] = blocks[at] * factor[:, 0:1]
    out_ref[...] = wide[...].astype(BF16)


def call(kernel, outs, scalars, held, arrays, scratch, name, flops=0, vmem=40):
    smem = pl.BlockSpec(memory_space=pltpu.SMEM)
    full = pl.BlockSpec(memory_space=pltpu.VMEM)
    size = sum(x.size * x.dtype.itemsize for x in list(arrays) + list(outs))
    return pl.pallas_call(
        kernel,
        out_shape=outs,
        in_specs=[smem] * len(scalars) + [pl.BlockSpec(memory_space=pl.ANY)] * len(held) + [full] * len(arrays),
        out_specs=[full] * len(outs),
        scratch_shapes=scratch,
        compiler_params=pltpu.CompilerParams(vmem_limit_bytes=vmem * 2**20),
        cost_estimate=pl.CostEstimate(flops=flops, bytes_accessed=size, transcendentals=0),
        name=name,
    )(*scalars, *held, *arrays)


def body(walkers, one_body, fields, field_diag, chol, weights, target):
    rows, slots, orbitals = walkers.shape
    vec_count, occupied, _ = chol.shape
    n, groups = lax.axis_size("blk"), lax.axis_size("grp")
    keep = slots // 2
    half = keep // 2
    cap = -(-slots // groups)
    slab = half * rows
    shape = jax.ShapeDtypeStruct
    grp = lax.axis_index("grp").reshape(1)
    blk = lax.axis_index("blk").reshape(1)
    core = lax.rem(blk, 2)

    def to_list(x, s):
        return lax.ppermute(x, "grp", [(i, (i + s) % groups) for i in range(groups)]) if s else x

    def to_block(x, s, e):
        if not s and not e:
            return x
        return lax.ppermute(x, "blk", [(i, (2 * (i // 2 + s) + (i % 2 ^ e)) % n) for i in range(n)])

    sibling = to_block(chol, 0, 1)
    own, held_body, diag = call(
        stage_kernel,
        [shape(x.shape, x.dtype) for x in (chol, one_body, field_diag)],
        [],
        [chol, one_body, field_diag],
        [],
        [pltpu.SemaphoreType.DMA((3,))],
        "stage",
    )
    width = orbitals + tail_blocks(3 * cap + 3, cap * rows) * LANES
    routed = call(
        functools.partial(route_kernel, keep, cap),
        [shape((cap * rows, width), BF16)] * groups,
        [grp],
        [target, weights, walkers, fields],
        [],
        [
            pltpu.SMEM(target.shape, target.dtype),
            pltpu.SMEM(weights.shape, weights.dtype),
            pltpu.VMEM(walkers.shape, walkers.dtype),
            pltpu.VMEM(fields.shape, fields.dtype),
            pltpu.VMEM((rows, slots, orbitals), F32),
            pltpu.VMEM((groups * cap + 1, rows, orbitals), F32),
            pltpu.VMEM((groups * cap + 1, 1, LANES), F32),
            pltpu.SemaphoreType.DMA((4,)),
        ],
        "route",
        vmem=56,
    )
    routed = [to_list(x, s) for s, x in enumerate(routed)]
    payload = shape((slab, orbitals + tail_blocks(2 * half * (orbitals // LANES), slab) * LANES), BF16)
    same, other, weight_sum, pick = call(
        functools.partial(merge_kernel, keep, cap, groups),
        [payload, payload, shape((8, LANES), F32), shape((groups * keep, LANES), F32)],
        [core],
        [],
        [diag] + routed,
        [],
        "merge",
    )
    gathered = [to_block(other if e else same, s, e) for s, e in hops(n)]
    parts = call(
        functools.partial(fock_kernel, n, half),
        [shape((slab, orbitals), BF16)] * n,
        [blk],
        [],
        [held_body, own, sibling] + gathered,
        [
            pltpu.VMEM((half, n, rows, orbitals), F32),
            pltpu.VMEM((orbitals, half * occupied), BF16),
            pltpu.VMEM((half * occupied, 2 * vec_count * occupied), BF16),
            pltpu.VMEM((half, n, rows, orbitals), F32),
        ],
        "fock",
        flops=2 * n * slab * orbitals * (orbitals + 4 * vec_count * occupied),
    )
    parts = [to_block(x, s, e) for x, (s, e) in zip(parts, hops(n))]
    back = call(
        functools.partial(sum_kernel, n, keep, cap, groups),
        [shape((cap * rows, orbitals), BF16)] * groups,
        [core],
        [],
        [pick] + parts,
        [],
        "sum",
    )
    back = [to_list(x, s) for s, x in enumerate(back)]
    (out,) = call(
        functools.partial(deal_kernel, keep, cap, groups),
        [shape(walkers.shape, BF16)],
        [grp, target, weights],
        [],
        [weight_sum] + back,
        [pltpu.VMEM((groups * cap + 1, rows, orbitals), F32), pltpu.VMEM(walkers.shape, F32)],
        "deal",
    )
    return out


def solution(mesh):
    in_specs = (
        P("blk", "grp", None),
        P(),
        P("grp", "blk"),
        P("blk", None),
        P("blk", None, None),
        P("grp"),
        P("grp"),
    )
    out_specs = P("blk", "grp", None)
    return jax.shard_map(body, mesh=mesh, in_specs=in_specs, out_specs=out_specs, check_vma=False)
```

```python
import functools
import math
import jax
import jax.numpy as jnp
from jax import lax
from jax.experimental import pallas as pl
from jax.experimental.pallas import tpu as pltpu
from jax.sharding import PartitionSpec as P

F32 = jnp.float32
BF16 = jnp.bfloat16
LANES = 128


def terms(value, count):
    out = []
    for _ in range(count):
        term = value.astype(BF16).astype(F32)
        out.append(term)
        value = value - term
    return out


def tail_blocks(count, slab):
    return -(-count // slab)


def write_tail(out_ref, start, lines):
    slab = out_ref.shape[0]
    for b in range(tail_blocks(lines.shape[0], slab)):
        part = lines[b * slab : (b + 1) * slab]
        if part.shape[0] < slab:
            part = jnp.concatenate([part, jnp.zeros((slab - part.shape[0], LANES), F32)], axis=0)
        out_ref[:, start + b * LANES : start + (b + 1) * LANES] = part.astype(BF16)


def read_tail(ref, start, count):
    parts = [ref[:, c : c + LANES].astype(F32) for c in range(start, ref.shape[1], LANES)]
    whole = parts[0] if len(parts) == 1 else jnp.concatenate(parts, axis=0)
    return whole[0:count]


def wide_mask(line, width):
    return jnp.concatenate([line] * (width // LANES), axis=1) > 0


def stage_kernel(*refs):
    count = (len(refs) - 2) // 2
    sems = refs[-1]
    copies = [pltpu.make_async_copy(refs[i], refs[count + 1 + i], sems.at[i]) for i in range(count)]
    for copy in copies:
        copy.start()
    for copy in copies:
        copy.wait()


def route_kernel(keep, cap, me_ref, target_any, weights_any, walkers_any, fields_any, diag_any, *refs):
    *outs, target_ref, weights_ref, walkers_ref, fields_ref, diag_ref, wide, blocks, parts, lines, sems = refs
    pairs = (
        (walkers_any, walkers_ref),
        (target_any, target_ref),
        (weights_any, weights_ref),
        (fields_any, fields_ref),
        (diag_any, diag_ref),
    )
    copies = [pltpu.make_async_copy(a, b, sems.at[i]) for i, (a, b) in enumerate(pairs)]
    for copy in copies:
        copy.start()
    rows, slots, orbitals = walkers_ref.shape
    vec_count = fields_ref.shape[1]
    chunks = orbitals // LANES
    groups = len(outs)
    live = groups * keep
    blocks[...] = jnp.zeros(blocks.shape, F32)
    lines[...] = jnp.zeros(lines.shape, F32)
    for copy in copies:
        copy.wait()
    wide[...] = walkers_ref[...].astype(F32)
    exponent = fields_ref[:, 0:1] * diag_ref[0:1, :]
    for g in range(1, vec_count):
        exponent = exponent + fields_ref[:, g : g + 1] * diag_ref[g : g + 1, :]
    for i, term in enumerate(terms(exponent, 2)):
        for c in range(chunks):
            parts[:, i * chunks + c, :] = term[:, c * LANES : (c + 1) * LANES]
    weight = F32(0.0)
    for slot in range(slots):
        t = target_ref[slot]
        alive = t < live
        weight = weight + jnp.where(alive, weights_ref[slot], F32(0.0))
        turn = lax.div(t, groups)
        at = jnp.where(alive, lax.rem(t, groups) * cap + lax.rem(turn, cap), groups * cap)
        blocks[at] = wide[:, slot, :]
        parts[slot, 2 * chunks : 2 * chunks + 1, :] = jnp.full((1, LANES), (turn + 1).astype(F32), F32)
        lines[at] = parts[slot]
    sums = terms(jnp.full((1, LANES), weight, F32), 3)
    for s, out in enumerate(outs):
        base = lax.rem(me_ref[0] + s, groups) * cap
        out[:, 0:orbitals] = jnp.concatenate([blocks[base + k] for k in range(cap)], axis=0).astype(BF16)
        tail = [lines[base + k][0 : 2 * chunks + 1] for k in range(cap)]
        write_tail(out, orbitals, jnp.concatenate(tail + sums, axis=0))


def merge_kernel(keep, cap, groups, orbitals, core_ref, *refs):
    ins, (same_ref, other_ref, weight_ref, pick_ref) = refs[:groups], refs[groups:]
    half = keep // 2
    rows = ins[0].shape[0] // cap
    slab = half * rows
    chunks = orbitals // LANES
    each = 2 * chunks + 1
    weight = jnp.zeros((1, LANES), F32)
    walker = [jnp.zeros((rows, orbitals), F32)] * keep
    line = [jnp.zeros((2 * chunks, LANES), F32)] * keep
    for s, ref in enumerate(ins):
        tail = read_tail(ref, orbitals, cap * each + 3)
        weight = weight + (tail[cap * each : cap * each + 1] + tail[cap * each + 1 : cap * each + 2] + tail[cap * each + 2 :])
        for k in range(cap):
            flag = tail[(k + 1) * each - 1 : (k + 1) * each]
            block = ref[k * rows : (k + 1) * rows, 0:orbitals].astype(F32)
            part = tail[k * each : (k + 1) * each - 1]
            for m in range(k, keep, cap):
                mine = jnp.where(flag == m + 1, F32(1.0), F32(0.0))
                pick_ref[s * keep + m : s * keep + m + 1, :] = mine
                walker[m] = jnp.where(wide_mask(mine, orbitals), block, walker[m])
                line[m] = jnp.where(mine > 0, part, line[m])
    weight_ref[...] = jnp.broadcast_to(weight, weight_ref.shape)
    first = core_ref[0] == 0
    for out, order in ((same_ref, (0, 1)), (other_ref, (1, 0))):
        picked = []
        for k in range(half):
            a, b = order[0] * half + k, order[1] * half + k
            picked.append(jnp.where(first, line[a], line[b]))
            block = jnp.where(first, walker[a], walker[b])
            for c in range(chunks):
                at = c * slab + k * rows
                out[at : at + rows, :] = block[:, c * LANES : (c + 1) * LANES].astype(BF16)
        tail = [p[i * chunks : (i + 1) * chunks] for i in range(2) for p in picked]
        out[chunks * slab :, :] = jnp.concatenate(tail, axis=0).astype(BF16)


def hops(n):
    return [(s, e) for s in range(n // 2) for e in range(2)]


def partner(blk, s, e, n, sign):
    chip = lax.rem(lax.div(blk, 2) + (s if sign > 0 else n // 2 - s), n // 2)
    core = lax.rem(blk, 2)
    return 2 * chip + (core if e == 0 else 1 - core)


def fock_kernel(n, half, blk_ref, body_ref, own_ref, sib_ref, *refs):
    ins, outs = refs[:n], refs[n : 2 * n]
    prop, turned, coup, result = refs[2 * n :]
    vec_count, occupied, orbitals = own_ref.shape
    slab = outs[0].shape[0]
    rows = slab // half
    chunks = orbitals // LANES
    blk = blk_ref[0]
    exponent = jnp.zeros((2 * half * chunks, LANES), F32)
    for ref in ins:
        exponent = exponent + ref[chunks * slab :, :].astype(F32)
    growth = jnp.exp(exponent[0 : half * chunks] + exponent[half * chunks :])
    for ref, (s, e) in zip(ins, hops(n)):
        source = partner(blk, s, e, n, -1)
        for w in range(half):
            for c in range(chunks):
                piece = ref[c * slab + w * rows : c * slab + (w + 1) * rows, :].astype(F32)
                piece = piece * growth[w * chunks + c : w * chunks + c + 1]
                prop[w, source, :, c * LANES : (c + 1) * LANES] = piece.astype(prop.dtype)
    scaled = jnp.concatenate([prop[w, i] for w in range(half) for i in range(n)], axis=0).astype(BF16)
    turned[...] = jnp.dot(scaled, body_ref[...], preferred_element_type=F32).T.astype(BF16)
    batch = math.gcd(vec_count, 4)
    for c, ref in enumerate((own_ref, sib_ref)):
        for g in range(0, vec_count, batch):
            left = ref[g : g + batch].reshape(batch * occupied, orbitals)
            s = jnp.dot(left, turned[...], preferred_element_type=F32).astype(BF16)
            for k in range(batch):
                at = (c * vec_count + g + k) * occupied
                for w in range(half):
                    coup[w * occupied : (w + 1) * occupied, at : at + occupied] = s[
                        k * occupied : (k + 1) * occupied, w * occupied : (w + 1) * occupied
                    ]
    tile = 256 if orbitals % 256 == 0 else orbitals
    depth = vec_count * occupied
    for t in range(0, orbitals, tile):
        total = jnp.dot(
            coup[:, :depth],
            own_ref[:, :, t : t + tile].reshape(depth, tile),
            preferred_element_type=F32,
        )
        total = total + jnp.dot(
            coup[:, depth:],
            sib_ref[:, :, t : t + tile].reshape(depth, tile),
            preferred_element_type=F32,
        )
        for w in range(half):
            for i in range(n):
                at = w * occupied + i * rows
                result[w, i, :, t : t + tile] = total[at : at + rows].astype(result.dtype)
    for out, (s, e) in zip(outs, hops(n)):
        to = partner(blk, s, e, n, 1)
        for w in range(half):
            out[w * rows : (w + 1) * rows, :] = result[w, to].astype(BF16)


def sum_kernel(n, keep, cap, groups, core_ref, pick_ref, *refs):
    ins, outs = refs[:n], refs[n:]
    slab, orbitals = ins[0].shape
    half = keep // 2
    rows = slab // half
    halves = []
    for e in range(2):
        total = ins[e][...].astype(F32)
        for ref in ins[e + 2 :: 2]:
            total = total + ref[...].astype(F32)
        halves.append(total)
    first = core_ref[0] == 0
    whole = [jnp.where(first, halves[0], halves[1]), jnp.where(first, halves[1], halves[0])]
    walker = [whole[m // half][(m % half) * rows : (m % half + 1) * rows] for m in range(keep)]
    for s, out in enumerate(outs):
        source = (groups - s) % groups
        for k in range(cap):
            value = jnp.zeros((rows, orbitals), F32)
            for m in range(k, keep, cap):
                mine = pick_ref[source * keep + m : source * keep + m + 1, :]
                value = jnp.where(wide_mask(mine, orbitals), walker[m], value)
            out[k * rows : (k + 1) * rows, :] = value.astype(BF16)


def deal_kernel(keep, cap, groups, me_ref, target_ref, weights_ref, total_ref, *refs):
    ins, (out_ref, blocks, wide) = refs[:groups], refs[groups:]
    rows, slots, orbitals = out_ref.shape
    live = groups * keep
    for s, ref in enumerate(ins):
        base = lax.rem(me_ref[0] + groups - s, groups) * cap
        for k in range(cap):
            blocks[base + k] = ref[k * rows : (k + 1) * rows, :].astype(F32)
    blocks[groups * cap] = jnp.zeros((rows, orbitals), F32)
    for slot in range(slots):
        t = target_ref[slot]
        alive = t < live
        at = jnp.where(alive, lax.rem(t, groups) * cap + lax.rem(lax.div(t, groups), cap), groups * cap)
        weight = jnp.where(alive, weights_ref[slot], F32(0.0))
        factor = jnp.full((1, LANES), weight * live, F32) / total_ref[0:1, :]
        wide[:, slot, :] = blocks[at] * factor[:, 0:1]
    out_ref[...] = wide[...].astype(BF16)


def call(kernel, outs, scalars, held, arrays, scratch, name, flops=0, vmem=40):
    smem = pl.BlockSpec(memory_space=pltpu.SMEM)
    full = pl.BlockSpec(memory_space=pltpu.VMEM)
    size = sum(x.size * x.dtype.itemsize for x in list(arrays) + list(outs))
    return pl.pallas_call(
        kernel,
        out_shape=outs,
        in_specs=[smem] * len(scalars) + [pl.BlockSpec(memory_space=pl.ANY)] * len(held) + [full] * len(arrays),
        out_specs=[full] * len(outs),
        scratch_shapes=scratch,
        compiler_params=pltpu.CompilerParams(vmem_limit_bytes=vmem * 2**20),
        cost_estimate=pl.CostEstimate(flops=flops, bytes_accessed=size, transcendentals=0),
        name=name,
    )(*scalars, *held, *arrays)


def body(walkers, one_body, fields, field_diag, chol, weights, target):
    rows, slots, orbitals = walkers.shape
    vec_count, occupied, _ = chol.shape
    n, groups = lax.axis_size("blk"), lax.axis_size("grp")
    keep = slots // 2
    half = keep // 2
    cap = -(-slots // groups)
    slab = half * rows
    shape = jax.ShapeDtypeStruct
    grp = lax.axis_index("grp").reshape(1)
    blk = lax.axis_index("blk").reshape(1)
    core = lax.rem(blk, 2)

    def to_list(x, s):
        return lax.ppermute(x, "grp", [(i, (i + s) % groups) for i in range(groups)]) if s else x

    def to_block(x, s, e):
        if not s and not e:
            return x
        return lax.ppermute(x, "blk", [(i, (2 * (i // 2 + s) + (i % 2 ^ e)) % n) for i in range(n)])

    chunks = orbitals // LANES
    sibling = to_block(chol, 0, 1)
    width = orbitals + tail_blocks(cap * (2 * chunks + 1) + 3, cap * rows) * LANES
    routed = call(
        functools.partial(route_kernel, keep, cap),
        [shape((cap * rows, width), BF16)] * groups,
        [grp],
        [target, weights, walkers, fields, field_diag],
        [],
        [
            pltpu.SMEM(target.shape, target.dtype),
            pltpu.SMEM(weights.shape, weights.dtype),
            pltpu.VMEM(walkers.shape, walkers.dtype),
            pltpu.VMEM(fields.shape, fields.dtype),
            pltpu.VMEM(field_diag.shape, field_diag.dtype),
            pltpu.VMEM((rows, slots, orbitals), F32),
            pltpu.VMEM((groups * cap + 1, rows, orbitals), F32),
            pltpu.VMEM((slots, 2 * chunks + 4, LANES), F32),
            pltpu.VMEM((groups * cap + 1, 2 * chunks + 4, LANES), F32),
            pltpu.SemaphoreType.DMA((5,)),
        ],
        "route",
        vmem=56,
    )
    routed = [to_list(x, s) for s, x in enumerate(routed)]
    payload = shape((chunks * slab + 2 * half * chunks, LANES), BF16)
    same, other, weight_sum, pick = call(
        functools.partial(merge_kernel, keep, cap, groups, orbitals),
        [payload, payload, shape((8, LANES), F32), shape((groups * keep, LANES), F32)],
        [core],
        [],
        routed,
        [],
        "merge",
    )
    own, held_body = call(
        stage_kernel,
        [shape(x.shape, x.dtype) for x in (chol, one_body)],
        [],
        [chol, one_body, weight_sum],
        [],
        [pltpu.SemaphoreType.DMA((2,))],
        "stage",
        vmem=48,
    )
    gathered = [to_block(other if e else same, s, e) for s, e in hops(n)]
    held = F32 if rows % 16 else BF16
    parts = call(
        functools.partial(fock_kernel, n, half),
        [shape((slab, orbitals), BF16)] * n,
        [blk],
        [],
        [held_body, own, sibling] + gathered,
        [
            pltpu.VMEM((half, n, rows, orbitals), held),
            pltpu.VMEM((orbitals, half * occupied), BF16),
            pltpu.VMEM((half * occupied, 2 * vec_count * occupied), BF16),
            pltpu.VMEM((half, n, rows, orbitals), held),
        ],
        "fock",
        flops=2 * n * slab * orbitals * (orbitals + 4 * vec_count * occupied),
    )
    parts = [to_block(x, s, e) for x, (s, e) in zip(parts, hops(n))]
    back = call(
        functools.partial(sum_kernel, n, keep, cap, groups),
        [shape((cap * rows, orbitals), BF16)] * groups,
        [core],
        [],
        [pick] + parts,
        [],
        "sum",
    )
    back = [to_list(x, s) for s, x in enumerate(back)]
    (out,) = call(
        functools.partial(deal_kernel, keep, cap, groups),
        [shape(walkers.shape, BF16)],
        [grp, target, weights],
        [],
        [weight_sum] + back,
        [pltpu.VMEM((groups * cap + 1, rows, orbitals), F32), pltpu.VMEM(walkers.shape, F32)],
        "deal",
    )
    return out


def solution(mesh):
    in_specs = (
        P("blk", "grp", None),
        P(),
        P("grp", "blk"),
        P("blk", None),
        P("blk", None, None),
        P("grp"),
        P("grp"),
    )
    out_specs = P("blk", "grp", None)
    return jax.shard_map(body, mesh=mesh, in_specs=in_specs, out_specs=out_specs, check_vma=False)
```

```python
import functools
import math
import jax
import jax.numpy as jnp
from jax import lax
from jax.experimental import pallas as pl
from jax.experimental.pallas import tpu as pltpu
from jax.sharding import PartitionSpec as P

F32 = jnp.float32
BF16 = jnp.bfloat16
LANES = 128
PARTS = 1
ROUTE_VMEM = 56
STAGE_VMEM = 48


def power(size):
    return size & (size - 1) == 0


def target_of(me, s, size):
    return lax.bitwise_xor(me, jnp.int32(s)) if power(size) else lax.rem(me + s, size)


def source_of(me, s, size):
    return lax.bitwise_xor(me, jnp.int32(s)) if power(size) else lax.rem(me + size - s, size)


def back_of(s, size):
    return s if power(size) else (size - s) % size


def terms(value, count):
    out = []
    for _ in range(count):
        term = value.astype(BF16).astype(F32)
        out.append(term)
        value = value - term
    return out


def round_up(x, unit):
    return -(-x // unit) * unit


def write_lines(out, start, pieces):
    have = sum(p.shape[0] for p in pieces)
    rest = out.shape[0] - start - have
    if rest:
        pieces = list(pieces) + [jnp.zeros((rest, LANES), F32)]
    out[start:, :] = jnp.concatenate(pieces, axis=0).astype(BF16)


def wide_mask(line, width):
    return jnp.concatenate([line] * (width // LANES), axis=1) > 0


def stage_kernel(*refs):
    sems = refs[-1]
    count = sems.shape[0]
    copies = [pltpu.make_async_copy(refs[i], refs[i - count - 1], sems.at[i]) for i in range(count)]
    for copy in copies:
        copy.start()
    for copy in copies:
        copy.wait()


def route_kernel(keep, cap, core_ref, grp_ref, *refs):
    anys, refs = refs[:5], refs[5:]
    mine_ref, twin_ref, target_ref, weights_ref, own_ref, fields_ref, diag_ref, wide, blocks, parts, lines, sems = refs
    held = (target_ref, weights_ref, own_ref, fields_ref, diag_ref)
    copies = [pltpu.make_async_copy(a, b, sems.at[i]) for i, (a, b) in enumerate(zip(anys, held))]
    for copy in copies:
        copy.start()
    grp, core = grp_ref[0], core_ref[0]
    rows, slots, orbitals = own_ref.shape
    vec_count = fields_ref.shape[1]
    chunks = orbitals // LANES
    spots = (blocks.shape[0] - 1) // 2
    groups = spots // cap
    live = groups * keep
    blocks[...] = jnp.zeros(blocks.shape, F32)
    lines[...] = jnp.zeros(lines.shape, F32)
    for copy in copies:
        copy.wait()
    wide[...] = own_ref[...].astype(F32)
    exponent = fields_ref[:, 0:1] * diag_ref[0:1, :]
    for g in range(1, vec_count):
        exponent = exponent + fields_ref[:, g : g + 1] * diag_ref[g : g + 1, :]
    for i, term in enumerate(terms(exponent, 2)):
        for c in range(chunks):
            parts[:, i * chunks + c, :] = term[:, c * LANES : (c + 1) * LANES]
    weight = F32(0.0)
    for slot in range(slots):
        t = target_ref[slot]
        alive = t < live
        weight = weight + jnp.where(alive, weights_ref[slot], F32(0.0))
        turn = lax.div(t, groups)
        other = jnp.where(lax.rem(turn, 2) == core, 0, 1)
        turn = lax.div(turn, 2)
        at = (other * groups + lax.rem(t, groups)) * cap + lax.rem(turn, cap)
        at = jnp.where(alive, at, 2 * spots)
        blocks[at] = wide[:, slot, :]
        parts[slot, 2 * chunks : 2 * chunks + 1, :] = jnp.full((1, LANES), (turn + 1).astype(F32), F32)
        lines[at] = parts[slot]
    sums = terms(jnp.full((1, LANES), weight, F32), 3)
    for other, out in enumerate((mine_ref, twin_ref)):
        tail = []
        for s in range(groups):
            base = (other * groups + target_of(grp, s, groups)) * cap
            for k in range(cap):
                block = blocks[base + k]
                for c in range(chunks):
                    at = ((s * cap + k) * chunks + c) * rows
                    out[at : at + rows, :] = block[:, c * LANES : (c + 1) * LANES].astype(BF16)
                tail.append(lines[base + k][0 : 2 * chunks + 1])
        write_lines(out, spots * chunks * rows, tail + sums)


def pair_kernel(cap, chunks, rows, core_ref, mine_ref, twin_ref, *outs):
    spots = len(outs) * cap
    each = 2 * chunks + 1
    first = core_ref[0] == 0
    start = spots * chunks * rows
    tail_mine, tail_twin = mine_ref[start:, :].astype(F32), twin_ref[start:, :].astype(F32)
    sums = [tail_mine[spots * each : spots * each + 3]]
    for s, out in enumerate(outs):
        tail = []
        for k in range(cap):
            spot = s * cap + k
            for c in range(chunks):
                at = (spot * chunks + c) * rows
                a, b = mine_ref[at : at + rows, :].astype(F32), twin_ref[at : at + rows, :].astype(F32)
                both = jnp.concatenate([jnp.where(first, a, b), jnp.where(first, b, a)], axis=0)
                to = (k * chunks + c) * 2 * rows
                out[to : to + 2 * rows, :] = both.astype(BF16)
            at = spot * each
            a, b = tail_mine[at : at + 2 * chunks], tail_twin[at : at + 2 * chunks]
            total = (a[0:chunks] + b[0:chunks]) + (a[chunks:] + b[chunks:])
            tail += terms(total, 2) + [tail_mine[at + 2 * chunks : at + each]]
        write_lines(out, cap * chunks * 2 * rows, tail + sums)


def merge_kernel(order, half, cap, rows, chunks, *refs):
    ins, (*outs, weight_ref, pick_ref) = refs[: len(order)], refs[len(order) :]
    each = 2 * chunks + 1
    start = cap * chunks * rows
    weight = jnp.zeros((1, LANES), F32)
    walker = [[jnp.zeros((rows, LANES), F32)] * chunks for _ in range(half)]
    line = [jnp.zeros((2 * chunks, LANES), F32)] * half
    for s, ref in zip(order, ins):
        tail = ref[start:, :].astype(F32)
        total = tail[cap * each : cap * each + 1] + tail[cap * each + 1 : cap * each + 2]
        weight = weight + (total + tail[cap * each + 2 : cap * each + 3])
        for k in range(cap):
            flag = tail[(k + 1) * each - 1 : (k + 1) * each]
            part = tail[k * each : (k + 1) * each - 1]
            for u in range(k, half, cap):
                mine = jnp.where(flag == u + 1, F32(1.0), F32(0.0))
                pick_ref[s * half + u : s * half + u + 1, :] = mine
                line[u] = jnp.where(mine > 0, part, line[u])
                for c in range(chunks):
                    at = (k * chunks + c) * rows
                    block = ref[at : at + rows, :].astype(F32)
                    walker[u][c] = jnp.where(mine > 0, block, walker[u][c])
    weight_ref[...] = jnp.broadcast_to(weight, weight_ref.shape)
    count = half // len(outs)
    for p, out in enumerate(outs):
        for w in range(count):
            for c in range(chunks):
                at = (w * chunks + c) * rows
                out[at : at + rows, :] = walker[p * count + w][c].astype(BF16)
        write_lines(out, count * chunks * rows, line[p * count : (p + 1) * count])


def fock_kernel(order, send_order, count, rows, chip_ref, body_ref, own_ref, twin_ref, *refs):
    n = len(order)
    ins, outs = refs[:n], refs[n : 2 * n]
    prop, turned, coup, result = refs[2 * n :]
    vec_count, occupied, orbitals = own_ref.shape
    chunks = orbitals // LANES
    chip = chip_ref[0]
    start = count * chunks * rows
    exponent = jnp.zeros((2 * count * chunks, LANES), F32)
    for ref in ins:
        exponent = exponent + ref[start : start + 2 * count * chunks, :].astype(F32)
    growth = []
    for w in range(count):
        at = 2 * w * chunks
        growth.append(jnp.exp(exponent[at : at + chunks] + exponent[at + chunks : at + 2 * chunks]))
    for ref, s in zip(ins, order):
        source = source_of(chip, s, n)
        for w in range(count):
            for c in range(chunks):
                at = (w * chunks + c) * rows
                piece = ref[at : at + rows, :].astype(F32) * growth[w][c : c + 1]
                prop[w, source, :, c * LANES : (c + 1) * LANES] = piece.astype(prop.dtype)
    scaled = jnp.concatenate([prop[w, i] for w in range(count) for i in range(n)], axis=0).astype(BF16)
    turned[...] = jnp.dot(scaled, body_ref[...], preferred_element_type=F32).T.astype(BF16)
    batch = math.gcd(vec_count, 4)
    for c, ref in enumerate((own_ref, twin_ref)):
        for g in range(0, vec_count, batch):
            left = ref[g : g + batch].reshape(batch * occupied, orbitals)
            s = jnp.dot(left, turned[...], preferred_element_type=F32).astype(BF16)
            for k in range(batch):
                at = (c * vec_count + g + k) * occupied
                for w in range(count):
                    coup[w * occupied : (w + 1) * occupied, at : at + occupied] = s[
                        k * occupied : (k + 1) * occupied, w * occupied : (w + 1) * occupied
                    ]
    tile = 256 if orbitals % 256 == 0 else orbitals
    depth = vec_count * occupied
    for t in range(0, orbitals, tile):
        total = jnp.dot(
            coup[:, :depth],
            own_ref[:, :, t : t + tile].reshape(depth, tile),
            preferred_element_type=F32,
        )
        total = total + jnp.dot(
            coup[:, depth:],
            twin_ref[:, :, t : t + tile].reshape(depth, tile),
            preferred_element_type=F32,
        )
        for w in range(count):
            for i in range(n):
                at = w * occupied + i * rows
                result[w, i, :, t : t + tile] = total[at : at + rows].astype(result.dtype)
    for out, s in zip(outs, send_order):
        to = target_of(chip, s, n)
        for w in range(count):
            out[w * rows : (w + 1) * rows, :] = result[w, to].astype(BF16)


def sum_kernel(n, first, half, cap, groups, core_ref, pick_ref, *refs):
    ins, (mine_ref, twin_ref) = refs[:n], refs[n:]
    orbitals = mine_ref.shape[1]
    rows = mine_ref.shape[0] // (groups * cap)
    total = ins[0][...].astype(F32)
    for ref in ins[1:]:
        total = total + ref[...].astype(F32)
    count = total.shape[0] // (2 * rows)
    core = core_ref[0]
    for s in range(groups):
        source = back_of(s, groups)
        for k in range(cap):
            value = jnp.zeros((2 * rows, orbitals), F32)
            for w in range(count):
                u = first + w
                if u % cap == k:
                    mine = pick_ref[source * half + u : source * half + u + 1, :]
                    value = jnp.where(wide_mask(mine, orbitals), total[2 * w * rows : 2 * (w + 1) * rows], value)
            at = (s * cap + k) * rows
            low, high = value[0:rows], value[rows:]
            mine_ref[at : at + rows, :] = jnp.where(core == 0, low, high).astype(BF16)
            twin_ref[at : at + rows, :] = jnp.where(core == 0, high, low).astype(BF16)


def join_kernel(parts, core_ref, *refs):
    mine, twin, outs = refs[:parts], refs[parts : 2 * parts], refs[2 * parts :]
    block = outs[0].shape[0] // 2
    core = core_ref[0]
    for s, out in enumerate(outs):
        at = slice(s * block, (s + 1) * block)
        a, b = mine[0][at, :].astype(F32), twin[0][at, :].astype(F32)
        for p in range(1, parts):
            a, b = a + mine[p][at, :].astype(F32), b + twin[p][at, :].astype(F32)
        out[0:block, :] = jnp.where(core == 0, a, b).astype(BF16)
        out[block:, :] = jnp.where(core == 0, b, a).astype(BF16)


def deal_kernel(keep, cap, order, grp_ref, target_ref, weights_ref, total_ref, *refs):
    groups = len(order)
    ins, (out_ref, blocks, wide) = refs[:groups], refs[groups:]
    rows, slots, orbitals = out_ref.shape
    live = groups * keep
    for s, ref in zip(order, ins):
        base = source_of(grp_ref[0], s, groups) * 2 * cap
        for k in range(2 * cap):
            blocks[base + k] = ref[k * rows : (k + 1) * rows, :].astype(F32)
    blocks[groups * 2 * cap] = jnp.zeros((rows, orbitals), F32)
    for slot in range(slots):
        t = target_ref[slot]
        alive = t < live
        turn = lax.div(t, groups)
        at = (lax.rem(t, groups) * 2 + lax.rem(turn, 2)) * cap + lax.rem(lax.div(turn, 2), cap)
        at = jnp.where(alive, at, groups * 2 * cap)
        weight = jnp.where(alive, weights_ref[slot], F32(0.0))
        factor = jnp.full((1, LANES), weight * live, F32) / total_ref[0:1, :]
        wide[:, slot, :] = blocks[at] * factor[:, 0:1]
    out_ref[...] = wide[...].astype(BF16)


def call(kernel, outs, scalars, held, arrays, scratch, name, flops=0, vmem=40):
    smem = pl.BlockSpec(memory_space=pltpu.SMEM)
    full = pl.BlockSpec(memory_space=pltpu.VMEM)
    size = sum(x.size * x.dtype.itemsize for x in list(arrays) + list(outs))
    return pl.pallas_call(
        kernel,
        out_shape=outs,
        in_specs=[smem] * len(scalars) + [pl.BlockSpec(memory_space=pl.ANY)] * len(held) + [full] * len(arrays),
        out_specs=[full] * len(outs),
        scratch_shapes=scratch,
        compiler_params=pltpu.CompilerParams(vmem_limit_bytes=vmem * 2**20),
        cost_estimate=pl.CostEstimate(flops=flops, bytes_accessed=size, transcendentals=0),
        name=name,
    )(*scalars, *held, *arrays)


def body(walkers, one_body, fields, field_diag, chol, weights, target):
    rows, slots, orbitals = walkers.shape
    vec_count, occupied, _ = chol.shape
    n, groups = lax.axis_size("blk"), lax.axis_size("grp")
    chips = n // 2
    keep = slots // 2
    half = keep // 2
    count = half // PARTS
    cap = -(-slots // (2 * groups))
    chunks = orbitals // LANES
    shape = jax.ShapeDtypeStruct
    blk = lax.axis_index("blk")
    grp = lax.axis_index("grp").reshape(1)
    core, chip = lax.rem(blk, 2).reshape(1), lax.div(blk, 2).reshape(1)

    def to_twin(x):
        return lax.ppermute(x, "blk", [(i, i ^ 1) for i in range(n)])

    def to_list(x, s):
        to = [(i, i ^ s if power(groups) else (i + s) % groups) for i in range(groups)]
        return lax.ppermute(x, "grp", to) if s else x

    def to_chip(x, s):
        to = [(i, 2 * (i // 2 ^ s if power(chips) else (i // 2 + s) % chips) + i % 2) for i in range(n)]
        return lax.ppermute(x, "blk", to) if s else x

    send_order = [0] + list(range(chips // 2, chips)) + list(range(1, chips // 2))
    chip_order = [0] + send_order[:0:-1]
    list_order = [0] + sorted(range(1, groups), key=lambda s: -bin(s).count("1"))

    chol_twin = to_twin(chol)
    lines = groups * cap * (chunks * rows + 2 * chunks + 1) + 3
    scalars = [pltpu.SMEM(x.shape, x.dtype) for x in (target, weights)]
    mine, twin = call(
        functools.partial(route_kernel, keep, cap),
        [shape((round_up(lines, 16), LANES), BF16)] * 2,
        [core, grp],
        [target, weights, walkers, fields, field_diag],
        [],
        scalars
        + [pltpu.VMEM(x.shape, x.dtype) for x in (walkers, fields, field_diag)]
        + [
            pltpu.VMEM((rows, slots, orbitals), F32),
            pltpu.VMEM((2 * groups * cap + 1, rows, orbitals), F32),
            pltpu.VMEM((slots, 2 * chunks + 4, LANES), F32),
            pltpu.VMEM((2 * groups * cap + 1, 2 * chunks + 4, LANES), F32),
            pltpu.SemaphoreType.DMA((5,)),
        ],
        "route",
        vmem=ROUTE_VMEM,
    )
    lines = cap * (chunks * 2 * rows + 2 * chunks + 1) + 3
    twin = to_twin(twin)
    (mine,) = call(
        stage_kernel,
        [shape(mine.shape, mine.dtype)],
        [],
        [mine],
        [],
        [pltpu.SemaphoreType.DMA((1,))],
        "hold",
    )
    routed = call(
        functools.partial(pair_kernel, cap, chunks, rows),
        [shape((round_up(lines, 16), LANES), BF16)] * groups,
        [core],
        [],
        [mine, twin],
        [],
        "pair",
    )
    routed = [to_list(routed[s], s) for s in list_order]
    payload = shape((count * chunks * 2 * rows + round_up(2 * count * chunks, 8), LANES), BF16)
    *payloads, weight_sum, pick = call(
        functools.partial(merge_kernel, list_order, half, cap, 2 * rows, chunks),
        [payload] * PARTS + [shape((8, LANES), F32), shape((groups * half, LANES), F32)],
        [],
        [],
        routed,
        [],
        "merge",
    )
    own, held_body = call(
        stage_kernel,
        [shape(x.shape, x.dtype) for x in (chol, one_body)],
        [],
        [chol, one_body, weight_sum],
        [],
        [pltpu.SemaphoreType.DMA((2,))],
        "stage",
        vmem=STAGE_VMEM,
    )
    gathered = [[to_chip(x, s) for s in chip_order] for x in payloads]
    held = F32 if rows % 8 else BF16
    mine, twin = [], []
    for p in range(PARTS):
        out = call(
            functools.partial(fock_kernel, chip_order, send_order, count, 2 * rows),
            [shape((count * 2 * rows, orbitals), BF16)] * chips,
            [chip],
            [],
            [held_body, own, chol_twin] + gathered[p],
            [
                pltpu.VMEM((count, chips, 2 * rows, orbitals), held),
                pltpu.VMEM((orbitals, count * occupied), BF16),
                pltpu.VMEM((count * occupied, 2 * vec_count * occupied), BF16),
                pltpu.VMEM((count, chips, 2 * rows, orbitals), held),
            ],
            "fock",
            flops=2 * count * occupied * orbitals * (orbitals + 4 * vec_count * occupied),
        )
        out = [to_chip(x, s) for s, x in zip(send_order, out)]
        a, b = call(
            functools.partial(sum_kernel, chips, p * count, half, cap, groups),
            [shape((groups * cap * rows, orbitals), BF16)] * 2,
            [core],
            [],
            [pick] + out,
            [],
            "sum",
        )
        mine.append(a)
        twin.append(to_twin(b))
    back = call(
        functools.partial(join_kernel, PARTS),
        [shape((2 * cap * rows, orbitals), BF16)] * groups,
        [core],
        [],
        mine + twin,
        [],
        "join",
    )
    back = [to_list(back[s], s) for s in list_order]
    (out,) = call(
        functools.partial(deal_kernel, keep, cap, list_order),
        [shape(walkers.shape, BF16)],
        [grp, target, weights],
        [],
        [weight_sum] + back,
        [pltpu.VMEM((groups * 2 * cap + 1, rows, orbitals), F32), pltpu.VMEM(walkers.shape, F32)],
        "deal",
    )
    return out


def solution(mesh):
    in_specs = (
        P("blk", "grp", None),
        P(),
        P("grp", "blk"),
        P("blk", None),
        P("blk", None, None),
        P("grp"),
        P("grp"),
    )
    out_specs = P("blk", "grp", None)
    return jax.shard_map(body, mesh=mesh, in_specs=in_specs, out_specs=out_specs, check_vma=False)
```

```python
import functools
import math
import jax
import jax.numpy as jnp
from jax import lax
from jax.experimental import pallas as pl
from jax.experimental.pallas import tpu as pltpu
from jax.sharding import PartitionSpec as P

F32 = jnp.float32
BF16 = jnp.bfloat16
LANES = 128
PARTS = 2
ROUTE_VMEM = 56
STAGE_VMEM = 48


def power(size):
    return size & (size - 1) == 0


def target_of(me, s, size):
    return lax.bitwise_xor(me, jnp.int32(s)) if power(size) else lax.rem(me + s, size)


def source_of(me, s, size):
    return lax.bitwise_xor(me, jnp.int32(s)) if power(size) else lax.rem(me + size - s, size)


def back_of(s, size):
    return s if power(size) else (size - s) % size


def terms(value, count):
    out = []
    for _ in range(count):
        term = value.astype(BF16).astype(F32)
        out.append(term)
        value = value - term
    return out


def round_up(x, unit):
    return -(-x // unit) * unit


def write_lines(out, start, pieces):
    have = sum(p.shape[0] for p in pieces)
    rest = out.shape[0] - start - have
    if rest:
        pieces = list(pieces) + [jnp.zeros((rest, LANES), F32)]
    out[start:, :] = jnp.concatenate(pieces, axis=0).astype(BF16)


def wide_mask(line, width):
    return jnp.concatenate([line] * (width // LANES), axis=1) > 0


def stage_kernel(*refs):
    sems = refs[-1]
    count = sems.shape[0]
    copies = [pltpu.make_async_copy(refs[i], refs[i - count - 1], sems.at[i]) for i in range(count)]
    for copy in copies:
        copy.start()
    for copy in copies:
        copy.wait()


def route_kernel(keep, cap, core_ref, grp_ref, *refs):
    anys, refs = refs[:5], refs[5:]
    mine_ref, twin_ref, target_ref, weights_ref, own_ref, fields_ref, diag_ref, wide, blocks, parts, lines, sems = refs
    held = (target_ref, weights_ref, own_ref, fields_ref, diag_ref)
    copies = [pltpu.make_async_copy(a, b, sems.at[i]) for i, (a, b) in enumerate(zip(anys, held))]
    for copy in copies:
        copy.start()
    grp, core = grp_ref[0], core_ref[0]
    rows, slots, orbitals = own_ref.shape
    vec_count = fields_ref.shape[1]
    chunks = orbitals // LANES
    spots = (blocks.shape[0] - 1) // 2
    groups = spots // cap
    live = groups * keep
    blocks[...] = jnp.zeros(blocks.shape, F32)
    lines[...] = jnp.zeros(lines.shape, F32)
    for copy in copies:
        copy.wait()
    wide[...] = own_ref[...].astype(F32)
    exponent = fields_ref[:, 0:1] * diag_ref[0:1, :]
    for g in range(1, vec_count):
        exponent = exponent + fields_ref[:, g : g + 1] * diag_ref[g : g + 1, :]
    for i, term in enumerate(terms(exponent, 2)):
        for c in range(chunks):
            parts[:, i * chunks + c, :] = term[:, c * LANES : (c + 1) * LANES]
    weight = F32(0.0)
    for slot in range(slots):
        t = target_ref[slot]
        alive = t < live
        weight = weight + jnp.where(alive, weights_ref[slot], F32(0.0))
        turn = lax.div(t, groups)
        other = jnp.where(lax.rem(turn, 2) == core, 0, 1)
        turn = lax.div(turn, 2)
        at = (other * groups + lax.rem(t, groups)) * cap + lax.rem(turn, cap)
        at = jnp.where(alive, at, 2 * spots)
        blocks[at] = wide[:, slot, :]
        parts[slot, 2 * chunks : 2 * chunks + 1, :] = jnp.full((1, LANES), (turn + 1).astype(F32), F32)
        lines[at] = parts[slot]
    sums = terms(jnp.full((1, LANES), weight, F32), 3)
    for other, out in enumerate((mine_ref, twin_ref)):
        tail = []
        for s in range(groups):
            base = (other * groups + target_of(grp, s, groups)) * cap
            for k in range(cap):
                block = blocks[base + k]
                for c in range(chunks):
                    at = ((s * cap + k) * chunks + c) * rows
                    out[at : at + rows, :] = block[:, c * LANES : (c + 1) * LANES].astype(BF16)
                tail.append(lines[base + k][0 : 2 * chunks + 1])
        write_lines(out, spots * chunks * rows, tail + sums)


def pair_kernel(cap, chunks, rows, core_ref, mine_ref, twin_ref, *outs):
    spots = len(outs) * cap
    each = 2 * chunks + 1
    first = core_ref[0] == 0
    start = spots * chunks * rows
    tail_mine, tail_twin = mine_ref[start:, :].astype(F32), twin_ref[start:, :].astype(F32)
    sums = [tail_mine[spots * each : spots * each + 3]]
    for s, out in enumerate(outs):
        tail = []
        for k in range(cap):
            spot = s * cap + k
            for c in range(chunks):
                at = (spot * chunks + c) * rows
                a, b = mine_ref[at : at + rows, :].astype(F32), twin_ref[at : at + rows, :].astype(F32)
                both = jnp.concatenate([jnp.where(first, a, b), jnp.where(first, b, a)], axis=0)
                to = (k * chunks + c) * 2 * rows
                out[to : to + 2 * rows, :] = both.astype(BF16)
            at = spot * each
            a, b = tail_mine[at : at + 2 * chunks], tail_twin[at : at + 2 * chunks]
            total = (a[0:chunks] + b[0:chunks]) + (a[chunks:] + b[chunks:])
            tail += terms(total, 2) + [tail_mine[at + 2 * chunks : at + each]]
        write_lines(out, cap * chunks * 2 * rows, tail + sums)


def merge_kernel(order, half, cap, rows, chunks, when, *refs):
    ins, (*outs, weight_ref, pick_ref) = refs[: len(order)], refs[len(order) :]
    each = 2 * chunks + 1
    start = cap * chunks * rows
    weight = jnp.zeros((1, LANES), F32)
    walker = [[jnp.zeros((rows, LANES), F32)] * chunks for _ in range(half)]
    line = [jnp.zeros((2 * chunks, LANES), F32)] * half
    for s, ref in zip(order, ins):
        tail = ref[start:, :].astype(F32)
        total = tail[cap * each : cap * each + 1] + tail[cap * each + 1 : cap * each + 2]
        weight = weight + (total + tail[cap * each + 2 : cap * each + 3])
        for k in range(cap):
            flag = tail[(k + 1) * each - 1 : (k + 1) * each]
            part = tail[k * each : (k + 1) * each - 1]
            for u in range(k, half, cap):
                mine = jnp.where(flag == u + 1, F32(1.0), F32(0.0))
                pick_ref[s * half + u : s * half + u + 1, :] = mine
                line[u] = jnp.where(mine > 0, part, line[u])
                for c in range(chunks):
                    at = (k * chunks + c) * rows
                    block = ref[at : at + rows, :].astype(F32)
                    walker[u][c] = jnp.where(mine > 0, block, walker[u][c])
    weight_ref[...] = jnp.broadcast_to(weight, weight_ref.shape)
    count = half // len(outs)
    for p, out in enumerate(outs):
        for w in range(count):
            for c in range(chunks):
                at = (w * chunks + c) * rows
                out[at : at + rows, :] = walker[p * count + w][c].astype(BF16)
        write_lines(out, count * chunks * rows, line[p * count : (p + 1) * count])


def fock_kernel(order, send_order, count, rows, chip_ref, body_ref, own_ref, twin_ref, *refs):
    n = len(order)
    ins, outs = refs[:n], refs[n : 2 * n]
    prop, turned, coup, result = refs[2 * n :]
    vec_count, occupied, orbitals = own_ref.shape
    chunks = orbitals // LANES
    chip = chip_ref[0]
    start = count * chunks * rows
    exponent = jnp.zeros((2 * count * chunks, LANES), F32)
    for ref in ins:
        exponent = exponent + ref[start : start + 2 * count * chunks, :].astype(F32)
    growth = []
    for w in range(count):
        at = 2 * w * chunks
        growth.append(jnp.exp(exponent[at : at + chunks] + exponent[at + chunks : at + 2 * chunks]))
    for ref, s in zip(ins, order):
        source = source_of(chip, s, n)
        for w in range(count):
            for c in range(chunks):
                at = (w * chunks + c) * rows
                piece = ref[at : at + rows, :].astype(F32) * growth[w][c : c + 1]
                prop[w, source, :, c * LANES : (c + 1) * LANES] = piece.astype(prop.dtype)
    scaled = jnp.concatenate([prop[w, i] for w in range(count) for i in range(n)], axis=0).astype(BF16)
    turned[...] = jnp.dot(scaled, body_ref[...], preferred_element_type=F32).T.astype(BF16)
    batch = math.gcd(vec_count, 4)
    for c, ref in enumerate((own_ref, twin_ref)):
        for g in range(0, vec_count, batch):
            left = ref[g : g + batch].reshape(batch * occupied, orbitals)
            s = jnp.dot(left, turned[...], preferred_element_type=F32).astype(BF16)
            for k in range(batch):
                at = (c * vec_count + g + k) * occupied
                for w in range(count):
                    coup[w * occupied : (w + 1) * occupied, at : at + occupied] = s[
                        k * occupied : (k + 1) * occupied, w * occupied : (w + 1) * occupied
                    ]
    tile = 256 if orbitals % 256 == 0 else orbitals
    depth = vec_count * occupied
    for t in range(0, orbitals, tile):
        total = jnp.dot(
            coup[:, :depth],
            own_ref[:, :, t : t + tile].reshape(depth, tile),
            preferred_element_type=F32,
        )
        total = total + jnp.dot(
            coup[:, depth:],
            twin_ref[:, :, t : t + tile].reshape(depth, tile),
            preferred_element_type=F32,
        )
        for w in range(count):
            for i in range(n):
                at = w * occupied + i * rows
                result[w, i, :, t : t + tile] = total[at : at + rows].astype(result.dtype)
    for out, s in zip(outs, send_order):
        to = target_of(chip, s, n)
        for w in range(count):
            out[w * rows : (w + 1) * rows, :] = result[w, to].astype(BF16)


def sum_kernel(n, first, half, cap, groups, core_ref, pick_ref, *refs):
    ins, (mine_ref, twin_ref) = refs[:n], refs[n:]
    orbitals = mine_ref.shape[1]
    rows = mine_ref.shape[0] // (groups * cap)
    total = ins[0][...].astype(F32)
    for ref in ins[1:]:
        total = total + ref[...].astype(F32)
    count = total.shape[0] // (2 * rows)
    core = core_ref[0]
    for s in range(groups):
        source = back_of(s, groups)
        for k in range(cap):
            value = jnp.zeros((2 * rows, orbitals), F32)
            for w in range(count):
                u = first + w
                if u % cap == k:
                    mine = pick_ref[source * half + u : source * half + u + 1, :]
                    value = jnp.where(wide_mask(mine, orbitals), total[2 * w * rows : 2 * (w + 1) * rows], value)
            at = (s * cap + k) * rows
            low, high = value[0:rows], value[rows:]
            mine_ref[at : at + rows, :] = jnp.where(core == 0, low, high).astype(BF16)
            twin_ref[at : at + rows, :] = jnp.where(core == 0, high, low).astype(BF16)


def join_kernel(parts, core_ref, *refs):
    mine, twin, outs = refs[:parts], refs[parts : 2 * parts], refs[2 * parts :]
    block = outs[0].shape[0] // 2
    core = core_ref[0]
    for s, out in enumerate(outs):
        at = slice(s * block, (s + 1) * block)
        a, b = mine[0][at, :].astype(F32), twin[0][at, :].astype(F32)
        for p in range(1, parts):
            a, b = a + mine[p][at, :].astype(F32), b + twin[p][at, :].astype(F32)
        out[0:block, :] = jnp.where(core == 0, a, b).astype(BF16)
        out[block:, :] = jnp.where(core == 0, b, a).astype(BF16)


def deal_kernel(keep, cap, order, grp_ref, target_ref, weights_ref, total_ref, *refs):
    groups = len(order)
    ins, (out_ref, blocks, wide) = refs[:groups], refs[groups:]
    rows, slots, orbitals = out_ref.shape
    live = groups * keep
    for s, ref in zip(order, ins):
        base = source_of(grp_ref[0], s, groups) * 2 * cap
        for k in range(2 * cap):
            blocks[base + k] = ref[k * rows : (k + 1) * rows, :].astype(F32)
    blocks[groups * 2 * cap] = jnp.zeros((rows, orbitals), F32)
    for slot in range(slots):
        t = target_ref[slot]
        alive = t < live
        turn = lax.div(t, groups)
        at = (lax.rem(t, groups) * 2 + lax.rem(turn, 2)) * cap + lax.rem(lax.div(turn, 2), cap)
        at = jnp.where(alive, at, groups * 2 * cap)
        weight = jnp.where(alive, weights_ref[slot], F32(0.0))
        factor = jnp.full((1, LANES), weight * live, F32) / total_ref[0:1, :]
        wide[:, slot, :] = blocks[at] * factor[:, 0:1]
    out_ref[...] = wide[...].astype(BF16)


def call(kernel, outs, scalars, held, arrays, scratch, name, flops=0, vmem=40):
    smem = pl.BlockSpec(memory_space=pltpu.SMEM)
    full = pl.BlockSpec(memory_space=pltpu.VMEM)
    size = sum(x.size * x.dtype.itemsize for x in list(arrays) + list(outs))
    return pl.pallas_call(
        kernel,
        out_shape=outs,
        in_specs=[smem] * len(scalars) + [pl.BlockSpec(memory_space=pl.ANY)] * len(held) + [full] * len(arrays),
        out_specs=[full] * len(outs),
        scratch_shapes=scratch,
        compiler_params=pltpu.CompilerParams(vmem_limit_bytes=vmem * 2**20),
        cost_estimate=pl.CostEstimate(flops=flops, bytes_accessed=size, transcendentals=0),
        name=name,
    )(*scalars, *held, *arrays)


def body(walkers, one_body, fields, field_diag, chol, weights, target):
    rows, slots, orbitals = walkers.shape
    vec_count, occupied, _ = chol.shape
    n, groups = lax.axis_size("blk"), lax.axis_size("grp")
    chips = n // 2
    keep = slots // 2
    half = keep // 2
    count = half // PARTS
    cap = -(-slots // (2 * groups))
    chunks = orbitals // LANES
    shape = jax.ShapeDtypeStruct
    blk = lax.axis_index("blk")
    grp = lax.axis_index("grp").reshape(1)
    core, chip = lax.rem(blk, 2).reshape(1), lax.div(blk, 2).reshape(1)

    def to_twin(x):
        return lax.ppermute(x, "blk", [(i, i ^ 1) for i in range(n)])

    def to_list(x, s):
        to = [(i, i ^ s if power(groups) else (i + s) % groups) for i in range(groups)]
        return lax.ppermute(x, "grp", to) if s else x

    def to_chip(x, s):
        to = [(i, 2 * (i // 2 ^ s if power(chips) else (i // 2 + s) % chips) + i % 2) for i in range(n)]
        return lax.ppermute(x, "blk", to) if s else x

    send_order = [0] + list(range(chips // 2, chips)) + list(range(1, chips // 2))
    chip_order = [0] + send_order[:0:-1]
    list_order = [0] + sorted(range(1, groups), key=lambda s: -bin(s).count("1"))

    chol_twin = to_twin(chol)
    lines = groups * cap * (chunks * rows + 2 * chunks + 1) + 3
    scalars = [pltpu.SMEM(x.shape, x.dtype) for x in (target, weights)]
    mine, twin = call(
        functools.partial(route_kernel, keep, cap),
        [shape((round_up(lines, 16), LANES), BF16)] * 2,
        [core, grp],
        [target, weights, walkers, fields, field_diag],
        [],
        scalars
        + [pltpu.VMEM(x.shape, x.dtype) for x in (walkers, fields, field_diag)]
        + [
            pltpu.VMEM((rows, slots, orbitals), F32),
            pltpu.VMEM((2 * groups * cap + 1, rows, orbitals), F32),
            pltpu.VMEM((slots, 2 * chunks + 4, LANES), F32),
            pltpu.VMEM((2 * groups * cap + 1, 2 * chunks + 4, LANES), F32),
            pltpu.SemaphoreType.DMA((5,)),
        ],
        "route",
        vmem=ROUTE_VMEM,
    )
    lines = cap * (chunks * 2 * rows + 2 * chunks + 1) + 3
    twin = to_twin(twin)
    (mine,) = call(
        stage_kernel,
        [shape(mine.shape, mine.dtype)],
        [],
        [mine],
        [],
        [pltpu.SemaphoreType.DMA((1,))],
        "hold",
    )
    routed = call(
        functools.partial(pair_kernel, cap, chunks, rows),
        [shape((round_up(lines, 16), LANES), BF16)] * groups,
        [core],
        [],
        [mine, twin],
        [],
        "pair",
    )
    own, held_body = call(
        stage_kernel,
        [shape(x.shape, x.dtype) for x in (chol, one_body)],
        [],
        [chol, one_body, routed[0]],
        [],
        [pltpu.SemaphoreType.DMA((2,))],
        "stage",
        vmem=STAGE_VMEM,
    )
    routed = [to_list(routed[s], s) for s in list_order]
    payload = shape((count * chunks * 2 * rows + round_up(2 * count * chunks, 8), LANES), BF16)
    *payloads, weight_sum, pick = call(
        functools.partial(merge_kernel, list_order, half, cap, 2 * rows, chunks),
        [payload] * PARTS + [shape((8, LANES), F32), shape((groups * half, LANES), F32)],
        [],
        [own],
        routed,
        [],
        "merge",
    )
    gathered = [[to_chip(x, s) for s in chip_order] for x in payloads]
    held = F32 if rows % 8 else BF16
    mine, twin = [], []
    for p in range(PARTS):
        out = call(
            functools.partial(fock_kernel, chip_order, send_order, count, 2 * rows),
            [shape((count * 2 * rows, orbitals), BF16)] * chips,
            [chip],
            [],
            [held_body, own, chol_twin] + gathered[p],
            [
                pltpu.VMEM((count, chips, 2 * rows, orbitals), held),
                pltpu.VMEM((orbitals, count * occupied), BF16),
                pltpu.VMEM((count * occupied, 2 * vec_count * occupied), BF16),
                pltpu.VMEM((count, chips, 2 * rows, orbitals), held),
            ],
            "fock",
            flops=2 * count * occupied * orbitals * (orbitals + 4 * vec_count * occupied),
        )
        out = [to_chip(x, s) for s, x in zip(send_order, out)]
        a, b = call(
            functools.partial(sum_kernel, chips, p * count, half, cap, groups),
            [shape((groups * cap * rows, orbitals), BF16)] * 2,
            [core],
            [],
            [pick] + out,
            [],
            "sum",
        )
        mine.append(a)
        twin.append(to_twin(b))
    back = call(
        functools.partial(join_kernel, PARTS),
        [shape((2 * cap * rows, orbitals), BF16)] * groups,
        [core],
        [],
        mine + twin,
        [],
        "join",
    )
    back = [to_list(back[s], s) for s in list_order]
    (out,) = call(
        functools.partial(deal_kernel, keep, cap, list_order),
        [shape(walkers.shape, BF16)],
        [grp, target, weights],
        [],
        [weight_sum] + back,
        [pltpu.VMEM((groups * 2 * cap + 1, rows, orbitals), F32), pltpu.VMEM(walkers.shape, F32)],
        "deal",
    )
    return out


def solution(mesh):
    in_specs = (
        P("blk", "grp", None),
        P(),
        P("grp", "blk"),
        P("blk", None),
        P("blk", None, None),
        P("grp"),
        P("grp"),
    )
    out_specs = P("blk", "grp", None)
    return jax.shard_map(body, mesh=mesh, in_specs=in_specs, out_specs=out_specs, check_vma=False)
```

```python
import functools
import math
import jax
import jax.numpy as jnp
from jax import lax
from jax.experimental import pallas as pl
from jax.experimental.pallas import tpu as pltpu
from jax.sharding import PartitionSpec as P

F32 = jnp.float32
BF16 = jnp.bfloat16
LANES = 128
PARTS = 1
VMEM = 24
ROUTE_VMEM = 56
STAGE_VMEM = 48


def power(size):
    return size & (size - 1) == 0


def target_of(me, s, size):
    return lax.bitwise_xor(me, jnp.int32(s)) if power(size) else lax.rem(me + s, size)


def source_of(me, s, size):
    return lax.bitwise_xor(me, jnp.int32(s)) if power(size) else lax.rem(me + size - s, size)


def back_of(s, size):
    return s if power(size) else (size - s) % size


def terms(value, count):
    out = []
    for _ in range(count):
        term = value.astype(BF16).astype(F32)
        out.append(term)
        value = value - term
    return out


def round_up(x, unit):
    return -(-x // unit) * unit


def write_lines(out, start, pieces):
    have = sum(p.shape[0] for p in pieces)
    rest = out.shape[0] - start - have
    if rest:
        pieces = list(pieces) + [jnp.zeros((rest, LANES), F32)]
    out[start:, :] = jnp.concatenate(pieces, axis=0).astype(BF16)


def wide_mask(line, width):
    return jnp.concatenate([line] * (width // LANES), axis=1) > 0


def stage_kernel(*refs):
    sems = refs[-1]
    count = sems.shape[0]
    copies = [pltpu.make_async_copy(refs[i], refs[i - count - 1], sems.at[i]) for i in range(count)]
    for copy in copies:
        copy.start()
    for copy in copies:
        copy.wait()


def route_kernel(keep, cap, core_ref, grp_ref, *refs):
    anys, refs = refs[:5], refs[5:]
    mine_ref, twin_ref, target_ref, weights_ref, own_ref, fields_ref, diag_ref, wide, blocks, parts, lines, sems = refs
    held = (target_ref, weights_ref, own_ref, fields_ref, diag_ref)
    copies = [pltpu.make_async_copy(a, b, sems.at[i]) for i, (a, b) in enumerate(zip(anys, held))]
    for copy in copies:
        copy.start()
    grp, core = grp_ref[0], core_ref[0]
    rows, slots, orbitals = own_ref.shape
    vec_count = fields_ref.shape[1]
    chunks = orbitals // LANES
    spots = (blocks.shape[0] - 1) // 2
    groups = spots // cap
    live = groups * keep
    blocks[...] = jnp.zeros(blocks.shape, F32)
    lines[...] = jnp.zeros(lines.shape, F32)
    for copy in copies:
        copy.wait()
    wide[...] = own_ref[...].astype(F32)
    exponent = fields_ref[:, 0:1] * diag_ref[0:1, :]
    for g in range(1, vec_count):
        exponent = exponent + fields_ref[:, g : g + 1] * diag_ref[g : g + 1, :]
    for i, term in enumerate(terms(exponent, 2)):
        for c in range(chunks):
            parts[:, i * chunks + c, :] = term[:, c * LANES : (c + 1) * LANES]
    weight = F32(0.0)
    for slot in range(slots):
        t = target_ref[slot]
        alive = t < live
        weight = weight + jnp.where(alive, weights_ref[slot], F32(0.0))
        turn = lax.div(t, groups)
        other = jnp.where(lax.rem(turn, 2) == core, 0, 1)
        turn = lax.div(turn, 2)
        at = (other * groups + lax.rem(t, groups)) * cap + lax.rem(turn, cap)
        at = jnp.where(alive, at, 2 * spots)
        blocks[at] = wide[:, slot, :]
        parts[slot, 2 * chunks : 2 * chunks + 1, :] = jnp.full((1, LANES), (turn + 1).astype(F32), F32)
        lines[at] = parts[slot]
    sums = terms(jnp.full((1, LANES), weight, F32), 3)
    for other, out in enumerate((mine_ref, twin_ref)):
        tail = []
        for s in range(groups):
            base = (other * groups + target_of(grp, s, groups)) * cap
            for k in range(cap):
                block = blocks[base + k]
                for c in range(chunks):
                    at = ((s * cap + k) * chunks + c) * rows
                    out[at : at + rows, :] = block[:, c * LANES : (c + 1) * LANES].astype(BF16)
                tail.append(lines[base + k][0 : 2 * chunks + 1])
        write_lines(out, spots * chunks * rows, tail + sums)


def pair_kernel(cap, chunks, rows, core_ref, mine_ref, twin_ref, *outs):
    spots = len(outs) * cap
    each = 2 * chunks + 1
    first = core_ref[0] == 0
    start = spots * chunks * rows
    tail_mine, tail_twin = mine_ref[start:, :].astype(F32), twin_ref[start:, :].astype(F32)
    sums = [tail_mine[spots * each : spots * each + 3]]
    for s, out in enumerate(outs):
        tail = []
        for k in range(cap):
            spot = s * cap + k
            for c in range(chunks):
                at = (spot * chunks + c) * rows
                a, b = mine_ref[at : at + rows, :].astype(F32), twin_ref[at : at + rows, :].astype(F32)
                both = jnp.concatenate([jnp.where(first, a, b), jnp.where(first, b, a)], axis=0)
                to = (k * chunks + c) * 2 * rows
                out[to : to + 2 * rows, :] = both.astype(BF16)
            at = spot * each
            a, b = tail_mine[at : at + 2 * chunks], tail_twin[at : at + 2 * chunks]
            total = (a[0:chunks] + b[0:chunks]) + (a[chunks:] + b[chunks:])
            tail += terms(total, 2) + [tail_mine[at + 2 * chunks : at + each]]
        write_lines(out, cap * chunks * 2 * rows, tail + sums)


def fold(body_ref, own_ref, twin_ref, out_ref):
    vec_count, occupied, orbitals = own_ref.shape
    batch = math.gcd(vec_count, 2)
    for c, ref in enumerate((own_ref, twin_ref)):

        @pl.loop(0, vec_count // batch)
        def _(i):
            left = ref[pl.ds(i * batch, batch)].reshape(batch * occupied, orbitals)
            done = lax.dot_general(left, body_ref[...], (((1,), (1,)), ((), ())), preferred_element_type=F32)
            out_ref[pl.ds(c * vec_count + i * batch, batch)] = done.astype(BF16).reshape(batch, occupied, orbitals)


def fold_kernel(core_ref, body_ref, own_ref, twin_ref, early_ref, out_ref):
    core = core_ref[0]

    @pl.when(core == 0)
    def _():
        out_ref[...] = early_ref[...]

    @pl.when(core != 0)
    def _():
        fold(body_ref, own_ref, twin_ref, out_ref)


def merge_kernel(order, half, cap, rows, chunks, core_ref, body_ref, own_ref, chol_ref, *refs):
    ins, (*outs, weight_ref, pick_ref, early_ref) = refs[: len(order)], refs[len(order) :]
    each = 2 * chunks + 1
    start = cap * chunks * rows
    weight = jnp.zeros((1, LANES), F32)
    walker = [[jnp.zeros((rows, LANES), F32)] * chunks for _ in range(half)]
    line = [jnp.zeros((2 * chunks, LANES), F32)] * half
    for s, ref in zip(order, ins):
        tail = ref[start:, :].astype(F32)
        total = tail[cap * each : cap * each + 1] + tail[cap * each + 1 : cap * each + 2]
        weight = weight + (total + tail[cap * each + 2 : cap * each + 3])
        for k in range(cap):
            flag = tail[(k + 1) * each - 1 : (k + 1) * each]
            part = tail[k * each : (k + 1) * each - 1]
            for u in range(k, half, cap):
                mine = jnp.where(flag == u + 1, F32(1.0), F32(0.0))
                pick_ref[s * half + u : s * half + u + 1, :] = mine
                line[u] = jnp.where(mine > 0, part, line[u])
                for c in range(chunks):
                    at = (k * chunks + c) * rows
                    block = ref[at : at + rows, :].astype(F32)
                    walker[u][c] = jnp.where(mine > 0, block, walker[u][c])
    weight_ref[...] = jnp.broadcast_to(weight, weight_ref.shape)
    count = half // len(outs)
    for p, out in enumerate(outs):
        for w in range(count):
            for c in range(chunks):
                at = (w * chunks + c) * rows
                out[at : at + rows, :] = walker[p * count + w][c].astype(BF16)
        write_lines(out, count * chunks * rows, line[p * count : (p + 1) * count])

    @pl.when(core_ref[0] == 0)
    def _():
        fold(body_ref, own_ref, chol_ref, early_ref)


def fock_kernel(order, send_order, count, rows, chip_ref, folded_ref, own_ref, twin_ref, *refs):
    n = len(order)
    ins, outs = refs[:n], refs[n : 2 * n]
    prop, turned, coup, result = refs[2 * n :]
    vec_count, occupied, orbitals = own_ref.shape
    chunks = orbitals // LANES
    chip = chip_ref[0]
    start = count * chunks * rows
    exponent = jnp.zeros((2 * count * chunks, LANES), F32)
    for ref in ins:
        exponent = exponent + ref[start : start + 2 * count * chunks, :].astype(F32)
    growth = []
    for w in range(count):
        at = 2 * w * chunks
        growth.append(jnp.exp(exponent[at : at + chunks] + exponent[at + chunks : at + 2 * chunks]))
    for ref, s in zip(ins, order):
        source = source_of(chip, s, n)
        for w in range(count):
            for c in range(chunks):
                at = (w * chunks + c) * rows
                piece = ref[at : at + rows, :].astype(F32) * growth[w][c : c + 1]
                prop[w, source, :, c * LANES : (c + 1) * LANES] = piece.astype(prop.dtype)
    scaled = jnp.concatenate([prop[w, i] for w in range(count) for i in range(n)], axis=0).astype(BF16)
    turned[...] = scaled.astype(F32).T.astype(BF16)
    batch = math.gcd(vec_count, 4)
    for g in range(0, 2 * vec_count, batch):
        left = folded_ref[g : g + batch].reshape(batch * occupied, orbitals)
        s = jnp.dot(left, turned[...], preferred_element_type=F32).astype(BF16)
        for k in range(batch):
            at = (g + k) * occupied
            for w in range(count):
                coup[w * occupied : (w + 1) * occupied, at : at + occupied] = s[
                    k * occupied : (k + 1) * occupied, w * occupied : (w + 1) * occupied
                ]
    tile = 256 if orbitals % 256 == 0 else orbitals
    depth = vec_count * occupied
    for t in range(0, orbitals, tile):
        total = jnp.dot(
            coup[:, :depth],
            own_ref[:, :, t : t + tile].reshape(depth, tile),
            preferred_element_type=F32,
        )
        total = total + jnp.dot(
            coup[:, depth:],
            twin_ref[:, :, t : t + tile].reshape(depth, tile),
            preferred_element_type=F32,
        )
        for w in range(count):
            for i in range(n):
                at = w * occupied + i * rows
                result[w, i, :, t : t + tile] = total[at : at + rows].astype(result.dtype)
    for out, s in zip(outs, send_order):
        to = target_of(chip, s, n)
        for w in range(count):
            out[w * rows : (w + 1) * rows, :] = result[w, to].astype(BF16)


def sum_kernel(n, first, half, cap, groups, core_ref, pick_ref, *refs):
    ins, (mine_ref, twin_ref) = refs[:n], refs[n:]
    orbitals = mine_ref.shape[1]
    rows = mine_ref.shape[0] // (groups * cap)
    total = ins[0][...].astype(F32)
    for ref in ins[1:]:
        total = total + ref[...].astype(F32)
    count = total.shape[0] // (2 * rows)
    core = core_ref[0]
    for s in range(groups):
        source = back_of(s, groups)
        for k in range(cap):
            value = jnp.zeros((2 * rows, orbitals), F32)
            for w in range(count):
                u = first + w
                if u % cap == k:
                    mine = pick_ref[source * half + u : source * half + u + 1, :]
                    value = jnp.where(wide_mask(mine, orbitals), total[2 * w * rows : 2 * (w + 1) * rows], value)
            at = (s * cap + k) * rows
            low, high = value[0:rows], value[rows:]
            mine_ref[at : at + rows, :] = jnp.where(core == 0, low, high).astype(BF16)
            twin_ref[at : at + rows, :] = jnp.where(core == 0, high, low).astype(BF16)


def join_kernel(parts, core_ref, *refs):
    mine, twin, outs = refs[:parts], refs[parts : 2 * parts], refs[2 * parts :]
    block = outs[0].shape[0] // 2
    core = core_ref[0]
    for s, out in enumerate(outs):
        at = slice(s * block, (s + 1) * block)
        a, b = mine[0][at, :].astype(F32), twin[0][at, :].astype(F32)
        for p in range(1, parts):
            a, b = a + mine[p][at, :].astype(F32), b + twin[p][at, :].astype(F32)
        out[0:block, :] = jnp.where(core == 0, a, b).astype(BF16)
        out[block:, :] = jnp.where(core == 0, b, a).astype(BF16)


def deal_kernel(keep, cap, order, grp_ref, target_ref, weights_ref, total_ref, *refs):
    groups = len(order)
    ins, (out_ref, blocks, wide) = refs[:groups], refs[groups:]
    rows, slots, orbitals = out_ref.shape
    live = groups * keep
    for s, ref in zip(order, ins):
        base = source_of(grp_ref[0], s, groups) * 2 * cap
        for k in range(2 * cap):
            blocks[base + k] = ref[k * rows : (k + 1) * rows, :].astype(F32)
    blocks[groups * 2 * cap] = jnp.zeros((rows, orbitals), F32)
    for slot in range(slots):
        t = target_ref[slot]
        alive = t < live
        turn = lax.div(t, groups)
        at = (lax.rem(t, groups) * 2 + lax.rem(turn, 2)) * cap + lax.rem(lax.div(turn, 2), cap)
        at = jnp.where(alive, at, groups * 2 * cap)
        weight = jnp.where(alive, weights_ref[slot], F32(0.0))
        factor = jnp.full((1, LANES), weight * live, F32) / total_ref[0:1, :]
        wide[:, slot, :] = blocks[at] * factor[:, 0:1]
    out_ref[...] = wide[...].astype(BF16)


def call(kernel, outs, scalars, held, arrays, scratch, name, flops=0, vmem=VMEM):
    smem = pl.BlockSpec(memory_space=pltpu.SMEM)
    full = pl.BlockSpec(memory_space=pltpu.VMEM)
    size = sum(x.size * x.dtype.itemsize for x in list(arrays) + list(outs))
    return pl.pallas_call(
        kernel,
        out_shape=outs,
        in_specs=[smem] * len(scalars) + [pl.BlockSpec(memory_space=pl.ANY)] * len(held) + [full] * len(arrays),
        out_specs=[full] * len(outs),
        scratch_shapes=scratch,
        compiler_params=pltpu.CompilerParams(vmem_limit_bytes=vmem * 2**20),
        cost_estimate=pl.CostEstimate(flops=flops, bytes_accessed=size, transcendentals=0),
        name=name,
    )(*scalars, *held, *arrays)


def body(walkers, one_body, fields, field_diag, chol, weights, target):
    rows, slots, orbitals = walkers.shape
    vec_count, occupied, _ = chol.shape
    n, groups = lax.axis_size("blk"), lax.axis_size("grp")
    chips = n // 2
    keep = slots // 2
    half = keep // 2
    count = half // PARTS
    cap = -(-slots // (2 * groups))
    chunks = orbitals // LANES
    shape = jax.ShapeDtypeStruct
    blk = lax.axis_index("blk")
    grp = lax.axis_index("grp").reshape(1)
    core, chip = lax.rem(blk, 2).reshape(1), lax.div(blk, 2).reshape(1)

    def to_twin(x):
        return lax.ppermute(x, "blk", [(i, i ^ 1) for i in range(n)])

    def to_list(x, s):
        to = [(i, i ^ s if power(groups) else (i + s) % groups) for i in range(groups)]
        return lax.ppermute(x, "grp", to) if s else x

    def to_chip(x, s):
        to = [(i, 2 * (i // 2 ^ s if power(chips) else (i // 2 + s) % chips) + i % 2) for i in range(n)]
        return lax.ppermute(x, "blk", to) if s else x

    send_order = [0] + list(range(chips // 2, chips)) + list(range(1, chips // 2))
    chip_order = send_order
    list_order = [0] + sorted(range(1, groups), key=lambda s: -bin(s).count("1"))

    chol_twin = to_twin(chol)
    lines = groups * cap * (chunks * rows + 2 * chunks + 1) + 3
    scalars = [pltpu.SMEM(x.shape, x.dtype) for x in (target, weights)]
    mine, twin = call(
        functools.partial(route_kernel, keep, cap),
        [shape((round_up(lines, 16), LANES), BF16)] * 2,
        [core, grp],
        [target, weights, walkers, fields, field_diag],
        [],
        scalars
        + [pltpu.VMEM(x.shape, x.dtype) for x in (walkers, fields, field_diag)]
        + [
            pltpu.VMEM((rows, slots, orbitals), F32),
            pltpu.VMEM((2 * groups * cap + 1, rows, orbitals), F32),
            pltpu.VMEM((slots, 2 * chunks + 4, LANES), F32),
            pltpu.VMEM((2 * groups * cap + 1, 2 * chunks + 4, LANES), F32),
            pltpu.SemaphoreType.DMA((5,)),
        ],
        "route",
        vmem=ROUTE_VMEM,
    )
    lines = cap * (chunks * 2 * rows + 2 * chunks + 1) + 3
    twin = to_twin(twin)
    (mine,) = call(
        stage_kernel,
        [shape(mine.shape, mine.dtype)],
        [],
        [mine],
        [],
        [pltpu.SemaphoreType.DMA((1,))],
        "hold",
    )
    routed = call(
        functools.partial(pair_kernel, cap, chunks, rows),
        [shape((round_up(lines, 16), LANES), BF16)] * groups,
        [core],
        [],
        [mine, twin],
        [],
        "pair",
    )
    own, held_body = call(
        stage_kernel,
        [shape(x.shape, x.dtype) for x in (chol, one_body)],
        [],
        [chol, one_body, routed[0]],
        [],
        [pltpu.SemaphoreType.DMA((2,))],
        "stage",
        vmem=STAGE_VMEM,
    )
    routed = [to_list(routed[s], s) for s in list_order]
    folded_shape = shape((2 * vec_count, occupied, orbitals), BF16)
    payload = shape((count * chunks * 2 * rows + round_up(2 * count * chunks, 8), LANES), BF16)
    *payloads, weight_sum, pick, early = call(
        functools.partial(merge_kernel, list_order, half, cap, 2 * rows, chunks),
        [payload] * PARTS + [shape((8, LANES), F32), shape((groups * half, LANES), F32), folded_shape],
        [core],
        [],
        [held_body, own, chol_twin] + routed,
        [],
        "merge",
        flops=4 * vec_count * occupied * orbitals * orbitals,
    )
    (folded,) = call(
        fold_kernel,
        [folded_shape],
        [core],
        [],
        [held_body, own, chol_twin, early],
        [],
        "fold",
        flops=4 * vec_count * occupied * orbitals * orbitals,
    )
    gathered = [[to_chip(x, s) for s in chip_order] for x in payloads]
    held = F32 if rows % 8 else BF16
    mine, twin = [], []
    for p in range(PARTS):
        out = call(
            functools.partial(fock_kernel, chip_order, send_order, count, 2 * rows),
            [shape((count * 2 * rows, orbitals), BF16)] * chips,
            [chip],
            [],
            [folded, own, chol_twin] + gathered[p],
            [
                pltpu.VMEM((count, chips, 2 * rows, orbitals), held),
                pltpu.VMEM((orbitals, count * occupied), BF16),
                pltpu.VMEM((count * occupied, 2 * vec_count * occupied), BF16),
                pltpu.VMEM((count, chips, 2 * rows, orbitals), held),
            ],
            "fock",
            flops=2 * count * occupied * orbitals * 4 * vec_count * occupied,
        )
        out = [to_chip(x, s) for s, x in zip(send_order, out)]
        a, b = call(
            functools.partial(sum_kernel, chips, p * count, half, cap, groups),
            [shape((groups * cap * rows, orbitals), BF16)] * 2,
            [core],
            [],
            [pick] + out,
            [],
            "sum",
        )
        mine.append(a)
        twin.append(to_twin(b))
    back = call(
        functools.partial(join_kernel, PARTS),
        [shape((2 * cap * rows, orbitals), BF16)] * groups,
        [core],
        [],
        mine + twin,
        [],
        "join",
    )
    back = [to_list(back[s], s) for s in list_order]
    (out,) = call(
        functools.partial(deal_kernel, keep, cap, list_order),
        [shape(walkers.shape, BF16)],
        [grp, target, weights],
        [],
        [weight_sum] + back,
        [pltpu.VMEM((groups * 2 * cap + 1, rows, orbitals), F32), pltpu.VMEM(walkers.shape, F32)],
        "deal",
    )
    return out


def solution(mesh):
    in_specs = (
        P("blk", "grp", None),
        P(),
        P("grp", "blk"),
        P("blk", None),
        P("blk", None, None),
        P("grp"),
        P("grp"),
    )
    out_specs = P("blk", "grp", None)
    return jax.shard_map(body, mesh=mesh, in_specs=in_specs, out_specs=out_specs, check_vma=False)
```

```python
import functools
import math
import jax
import jax.numpy as jnp
from jax import lax
from jax.experimental import pallas as pl
from jax.experimental.pallas import tpu as pltpu
from jax.sharding import PartitionSpec as P

F32 = jnp.float32
BF16 = jnp.bfloat16
LANES = 128
ROUTE_VMEM = 56
STAGE_VMEM = 48


def power(size):
    return size & (size - 1) == 0


def target_of(me, s, size):
    return lax.bitwise_xor(me, jnp.int32(s)) if power(size) else lax.rem(me + s, size)


def source_of(me, s, size):
    return lax.bitwise_xor(me, jnp.int32(s)) if power(size) else lax.rem(me + size - s, size)


def terms(value, count):
    out = []
    for _ in range(count):
        term = value.astype(BF16).astype(F32)
        out.append(term)
        value = value - term
    return out


def round_up(x, unit):
    return -(-x // unit) * unit


def write_lines(out, start, pieces):
    have = sum(p.shape[0] for p in pieces)
    rest = out.shape[0] - start - have
    if rest:
        pieces = list(pieces) + [jnp.zeros((rest, LANES), F32)]
    out[start:, :] = jnp.concatenate(pieces, axis=0).astype(BF16)


def wide_mask(line, width):
    return jnp.concatenate([line] * (width // LANES), axis=1) > 0


def stage_kernel(*refs):
    sems = refs[-1]
    count = sems.shape[0]
    copies = [pltpu.make_async_copy(refs[i], refs[i - count - 1], sems.at[i]) for i in range(count)]
    for copy in copies:
        copy.start()
    for copy in copies:
        copy.wait()


def route_kernel(keep, cap, *refs):
    anys, refs = refs[:5], refs[5:]
    out, target_ref, weights_ref, own_ref, fields_ref, diag_ref, wide, blocks, parts, lines, sems = refs
    held = (target_ref, weights_ref, own_ref, fields_ref, diag_ref)
    copies = [pltpu.make_async_copy(a, b, sems.at[i]) for i, (a, b) in enumerate(zip(anys, held))]
    for copy in copies:
        copy.start()
    rows, slots, orbitals = own_ref.shape
    vec_count = fields_ref.shape[1]
    chunks = orbitals // LANES
    spots = blocks.shape[0] - 1
    groups = spots // cap // 2
    live = groups * keep
    blocks[...] = jnp.zeros(blocks.shape, F32)
    lines[...] = jnp.zeros(lines.shape, F32)
    for copy in copies:
        copy.wait()
    wide[...] = own_ref[...].astype(F32)
    exponent = fields_ref[:, 0:1] * diag_ref[0:1, :]
    for g in range(1, vec_count):
        exponent = exponent + fields_ref[:, g : g + 1] * diag_ref[g : g + 1, :]
    for i, term in enumerate(terms(exponent, 2)):
        for c in range(chunks):
            parts[:, i * chunks + c, :] = term[:, c * LANES : (c + 1) * LANES]
    weight = F32(0.0)
    for slot in range(slots):
        t = target_ref[slot]
        alive = t < live
        weight = weight + jnp.where(alive, weights_ref[slot], F32(0.0))
        turn = lax.div(t, groups)
        at = (lax.rem(t, groups) * 2 + lax.rem(turn, 2)) * cap
        turn = lax.div(turn, 2)
        at = jnp.where(alive, at + lax.rem(turn, cap), spots)
        blocks[at] = wide[:, slot, :]
        parts[slot, 2 * chunks : 2 * chunks + 1, :] = jnp.full((1, LANES), (turn + 1).astype(F32), F32)
        lines[at] = parts[slot]
    sums = terms(jnp.full((1, LANES), weight, F32), 3)
    for d in range(2 * groups):
        for k in range(cap):
            block = blocks[d * cap + k]
            for c in range(chunks):
                at = (k * chunks + c) * rows
                out[d, at : at + rows, :] = block[:, c * LANES : (c + 1) * LANES].astype(BF16)
        tail = [lines[d * cap + k][0 : 2 * chunks + 1] for k in range(cap)]
        write_lines(out.at[d], cap * chunks * rows, tail + sums)


def merge_kernel(half, cap, rows, chunks, routed_ref, out, weight_ref, pick_ref):
    each = 2 * chunks + 1
    start = cap * chunks * rows
    weight = jnp.zeros((1, LANES), F32)
    walker = [[jnp.zeros((2 * rows, LANES), F32)] * chunks for _ in range(half)]
    line = [jnp.zeros((2 * chunks, LANES), F32)] * half
    for q in range(routed_ref.shape[0] // 2):
        tails = [routed_ref[2 * q + e, start:, :].astype(F32) for e in range(2)]
        total = tails[0][cap * each : cap * each + 1] + tails[0][cap * each + 1 : cap * each + 2]
        weight = weight + (total + tails[0][cap * each + 2 : cap * each + 3])
        for k in range(cap):
            flag = tails[0][(k + 1) * each - 1 : (k + 1) * each]
            a, b = [tail[k * each : (k + 1) * each - 1] for tail in tails]
            both = (a[0:chunks] + b[0:chunks]) + (a[chunks:] + b[chunks:])
            part = jnp.concatenate(terms(both, 2), axis=0)
            for u in range(k, half, cap):
                mine = jnp.where(flag == u + 1, F32(1.0), F32(0.0))
                pick_ref[q * half + u : q * half + u + 1, :] = mine
                line[u] = jnp.where(mine > 0, part, line[u])
                for c in range(chunks):
                    at = (k * chunks + c) * rows
                    block = [routed_ref[2 * q + e, at : at + rows, :].astype(F32) for e in range(2)]
                    walker[u][c] = jnp.where(mine > 0, jnp.concatenate(block, axis=0), walker[u][c])
    weight_ref[...] = jnp.broadcast_to(weight, weight_ref.shape)
    for u in range(half):
        for c in range(chunks):
            at = (u * chunks + c) * 2 * rows
            out[at : at + 2 * rows, :] = walker[u][c].astype(BF16)
    write_lines(out, half * chunks * 2 * rows, line)


def fock_kernel(order, send_order, count, rows, chip_ref, body_ref, own_ref, twin_ref, *refs):
    n = len(order)
    ins, outs = refs[:n], refs[n : 2 * n]
    prop, turned, coup, result = refs[2 * n :]
    vec_count, occupied, orbitals = own_ref.shape
    chunks = orbitals // LANES
    chip = chip_ref[0]
    start = count * chunks * rows
    exponent = jnp.zeros((2 * count * chunks, LANES), F32)
    for ref in ins:
        exponent = exponent + ref[start : start + 2 * count * chunks, :].astype(F32)
    growth = []
    for w in range(count):
        at = 2 * w * chunks
        growth.append(jnp.exp(exponent[at : at + chunks] + exponent[at + chunks : at + 2 * chunks]))
    for ref, s in zip(ins, order):
        source = source_of(chip, s, n)
        for w in range(count):
            for c in range(chunks):
                at = (w * chunks + c) * rows
                piece = ref[at : at + rows, :].astype(F32) * growth[w][c : c + 1]
                prop[w, source, :, c * LANES : (c + 1) * LANES] = piece.astype(prop.dtype)
    scaled = jnp.concatenate([prop[w, i] for w in range(count) for i in range(n)], axis=0).astype(BF16)
    turned[...] = jnp.dot(scaled, body_ref[...], preferred_element_type=F32).T.astype(BF16)
    batch = math.gcd(vec_count, 4)
    for c, ref in enumerate((own_ref, twin_ref)):
        for g in range(0, vec_count, batch):
            left = ref[g : g + batch].reshape(batch * occupied, orbitals)
            s = jnp.dot(left, turned[...], preferred_element_type=F32).astype(BF16)
            for k in range(batch):
                at = (c * vec_count + g + k) * occupied
                for w in range(count):
                    coup[w * occupied : (w + 1) * occupied, at : at + occupied] = s[
                        k * occupied : (k + 1) * occupied, w * occupied : (w + 1) * occupied
                    ]
    tile = 256 if orbitals % 256 == 0 else orbitals
    depth = vec_count * occupied
    for t in range(0, orbitals, tile):
        total = jnp.dot(
            coup[:, :depth],
            own_ref[:, :, t : t + tile].reshape(depth, tile),
            preferred_element_type=F32,
        )
        total = total + jnp.dot(
            coup[:, depth:],
            twin_ref[:, :, t : t + tile].reshape(depth, tile),
            preferred_element_type=F32,
        )
        for w in range(count):
            for i in range(n):
                at = w * occupied + i * rows
                result[w, i, :, t : t + tile] = total[at : at + rows].astype(result.dtype)
    for out, s in zip(outs, send_order):
        to = target_of(chip, s, n)
        for w in range(count):
            out[w * rows : (w + 1) * rows, :] = result[w, to].astype(BF16)


def sum_kernel(half, cap, rows, pick_ref, *refs):
    ins, out = refs[:-1], refs[-1]
    orbitals = out.shape[2]
    total = ins[0][...].astype(F32)
    for ref in ins[1:]:
        total = total + ref[...].astype(F32)
    for q in range(out.shape[0] // cap // 2):
        for k in range(cap):
            value = jnp.zeros((2 * rows, orbitals), F32)
            for u in range(k, half, cap):
                mine = pick_ref[q * half + u : q * half + u + 1, :]
                value = jnp.where(wide_mask(mine, orbitals), total[2 * u * rows : 2 * (u + 1) * rows], value)
            for e in range(2):
                out[(2 * q + e) * cap + k] = value[e * rows : (e + 1) * rows].astype(BF16)


def deal_kernel(keep, cap, target_ref, weights_ref, total_ref, back_ref, out_ref, wide):
    rows, slots, orbitals = out_ref.shape
    groups = back_ref.shape[0] // cap // 2
    live = groups * keep
    for slot in range(slots):
        t = target_ref[slot]
        alive = t < live
        turn = lax.div(t, groups)
        at = (lax.rem(t, groups) * 2 + lax.rem(turn, 2)) * cap + lax.rem(lax.div(turn, 2), cap)
        block = back_ref[jnp.where(alive, at, 0)].astype(F32)
        weight = jnp.where(alive, weights_ref[slot], F32(0.0))
        factor = jnp.full((1, LANES), weight * live, F32) / total_ref[0:1, :]
        wide[:, slot, :] = jnp.where(alive, block * factor[:, 0:1], F32(0.0))
    out_ref[...] = wide[...].astype(BF16)


def call(kernel, outs, scalars, held, arrays, scratch, name, flops=0, vmem=40):
    smem = pl.BlockSpec(memory_space=pltpu.SMEM)
    full = pl.BlockSpec(memory_space=pltpu.VMEM)
    size = sum(x.size * x.dtype.itemsize for x in list(arrays) + list(outs))
    return pl.pallas_call(
        kernel,
        out_shape=outs,
        in_specs=[smem] * len(scalars) + [pl.BlockSpec(memory_space=pl.ANY)] * len(held) + [full] * len(arrays),
        out_specs=[full] * len(outs),
        scratch_shapes=scratch,
        compiler_params=pltpu.CompilerParams(vmem_limit_bytes=vmem * 2**20),
        cost_estimate=pl.CostEstimate(flops=flops, bytes_accessed=size, transcendentals=0),
        name=name,
    )(*scalars, *held, *arrays)


def body(walkers, one_body, fields, field_diag, chol, weights, target):
    rows, slots, orbitals = walkers.shape
    vec_count, occupied, _ = chol.shape
    chips, groups = lax.axis_size("chip"), lax.axis_size("grp")
    keep = slots // 2
    half = keep // 2
    cap = -(-slots // (2 * groups))
    chunks = orbitals // LANES
    shape = jax.ShapeDtypeStruct
    chip = lax.axis_index("chip").reshape(1)

    def to_chip(x, s):
        to = [(i, i ^ s if power(chips) else (i + s) % chips) for i in range(chips)]
        return lax.ppermute(x, "chip", to) if s else x

    def exchange(x):
        return lax.all_to_all(x, ("grp", "core"), 0, 0, tiled=True)

    send_order = [0] + list(range(chips // 2, chips)) + list(range(1, chips // 2))
    chip_order = [0] + send_order[:0:-1]
    chol_twin = lax.ppermute(chol, "core", [(0, 1), (1, 0)])
    lines = cap * (chunks * rows + 2 * chunks + 1) + 3
    routed = call(
        functools.partial(route_kernel, keep, cap),
        [shape((2 * groups, round_up(lines, 16), LANES), BF16)],
        [],
        [target, weights, walkers, fields, field_diag],
        [],
        [pltpu.SMEM(x.shape, x.dtype) for x in (target, weights)]
        + [pltpu.VMEM(x.shape, x.dtype) for x in (walkers, fields, field_diag)]
        + [
            pltpu.VMEM((rows, slots, orbitals), F32),
            pltpu.VMEM((2 * groups * cap + 1, rows, orbitals), F32),
            pltpu.VMEM((slots, 2 * chunks + 4, LANES), F32),
            pltpu.VMEM((2 * groups * cap + 1, 2 * chunks + 4, LANES), F32),
            pltpu.SemaphoreType.DMA((5,)),
        ],
        "route",
        vmem=ROUTE_VMEM,
    )
    routed = [exchange(routed[0])]
    payload = shape((half * chunks * 2 * rows + round_up(2 * half * chunks, 8), LANES), BF16)
    payload, weight_sum, pick = call(
        functools.partial(merge_kernel, half, cap, rows, chunks),
        [payload, shape((8, LANES), F32), shape((groups * half, LANES), F32)],
        [],
        [],
        routed,
        [],
        "merge",
    )
    own, held_body = call(
        stage_kernel,
        [shape(x.shape, x.dtype) for x in (chol, one_body)],
        [],
        [chol, one_body, weight_sum],
        [],
        [pltpu.SemaphoreType.DMA((2,))],
        "stage",
        vmem=STAGE_VMEM,
    )
    gathered = [to_chip(payload, s) for s in chip_order]
    held = F32 if rows % 8 else BF16
    parts = call(
        functools.partial(fock_kernel, chip_order, send_order, half, 2 * rows),
        [shape((half * 2 * rows, orbitals), BF16)] * chips,
        [chip],
        [],
        [held_body, own, chol_twin] + gathered,
        [
            pltpu.VMEM((half, chips, 2 * rows, orbitals), held),
            pltpu.VMEM((orbitals, half * occupied), BF16),
            pltpu.VMEM((half * occupied, 2 * vec_count * occupied), BF16),
            pltpu.VMEM((half, chips, 2 * rows, orbitals), held),
        ],
        "fock",
        flops=2 * half * occupied * orbitals * (orbitals + 4 * vec_count * occupied),
    )
    parts = [to_chip(x, s) for s, x in zip(send_order, parts)]
    (back,) = call(
        functools.partial(sum_kernel, half, cap, rows),
        [shape((2 * groups * cap, rows, orbitals), BF16)],
        [],
        [],
        [pick] + parts,
        [],
        "sum",
    )
    (out,) = call(
        functools.partial(deal_kernel, keep, cap),
        [shape(walkers.shape, BF16)],
        [target, weights],
        [],
        [weight_sum, exchange(back)],
        [pltpu.VMEM(walkers.shape, F32)],
        "deal",
    )
    return out


def solution(mesh):
    groups, n = mesh.shape["grp"], mesh.shape["blk"]
    split = jax.sharding.Mesh(mesh.devices.reshape(groups, n // 2, 2), ("grp", "chip", "core"))
    blk = ("chip", "core")
    in_specs = (
        P(blk, "grp", None),
        P(),
        P("grp", blk),
        P(blk, None),
        P(blk, None, None),
        P("grp"),
        P("grp"),
    )
    out_specs = P(blk, "grp", None)
    return jax.shard_map(body, mesh=split, in_specs=in_specs, out_specs=out_specs, check_vma=False)
```

```python
import functools
import math
import jax
import jax.numpy as jnp
from jax import lax
from jax.experimental import pallas as pl
from jax.experimental.pallas import tpu as pltpu
from jax.sharding import PartitionSpec as P

F32 = jnp.float32
BF16 = jnp.bfloat16
LANES = 128
VMEM = 24
ROUTE_VMEM = 56
STAGE_VMEM = 48


def terms(value, count):
    out = []
    for _ in range(count):
        term = value.astype(BF16).astype(F32)
        out.append(term)
        value = value - term
    return out


def tail_blocks(count, slab):
    return -(-count // slab)


def write_tail(out_ref, start, lines):
    slab = out_ref.shape[0]
    for b in range(tail_blocks(lines.shape[0], slab)):
        part = lines[b * slab : (b + 1) * slab]
        if part.shape[0] < slab:
            part = jnp.concatenate([part, jnp.zeros((slab - part.shape[0], LANES), F32)], axis=0)
        out_ref[:, start + b * LANES : start + (b + 1) * LANES] = part.astype(BF16)


def read_tail(ref, start, count):
    parts = [ref[:, c : c + LANES].astype(F32) for c in range(start, ref.shape[1], LANES)]
    whole = parts[0] if len(parts) == 1 else jnp.concatenate(parts, axis=0)
    return whole[0:count]


def wide_mask(line, width):
    return jnp.concatenate([line] * (width // LANES), axis=1) > 0


def stage_kernel(*refs):
    sems = refs[-1]
    count = sems.shape[0]
    copies = [pltpu.make_async_copy(refs[i], refs[i - count - 1], sems.at[i]) for i in range(count)]
    for copy in copies:
        copy.start()
    for copy in copies:
        copy.wait()


def route_kernel(keep, cap, me_ref, target_any, weights_any, walkers_any, fields_any, diag_any, *refs):
    *outs, target_ref, weights_ref, walkers_ref, fields_ref, diag_ref, wide, blocks, parts, lines, sems = refs
    pairs = (
        (walkers_any, walkers_ref),
        (target_any, target_ref),
        (weights_any, weights_ref),
        (fields_any, fields_ref),
        (diag_any, diag_ref),
    )
    copies = [pltpu.make_async_copy(a, b, sems.at[i]) for i, (a, b) in enumerate(pairs)]
    for copy in copies:
        copy.start()
    rows, slots, orbitals = walkers_ref.shape
    vec_count = fields_ref.shape[1]
    chunks = orbitals // LANES
    groups = len(outs)
    live = groups * keep
    blocks[...] = jnp.zeros(blocks.shape, F32)
    lines[...] = jnp.zeros(lines.shape, F32)
    for copy in copies:
        copy.wait()
    wide[...] = walkers_ref[...].astype(F32)
    exponent = fields_ref[:, 0:1] * diag_ref[0:1, :]
    for g in range(1, vec_count):
        exponent = exponent + fields_ref[:, g : g + 1] * diag_ref[g : g + 1, :]
    for i, term in enumerate(terms(exponent, 2)):
        for c in range(chunks):
            parts[:, i * chunks + c, :] = term[:, c * LANES : (c + 1) * LANES]
    weight = F32(0.0)
    for slot in range(slots):
        t = target_ref[slot]
        alive = t < live
        weight = weight + jnp.where(alive, weights_ref[slot], F32(0.0))
        turn = lax.div(t, groups)
        at = jnp.where(alive, lax.rem(t, groups) * cap + lax.rem(turn, cap), groups * cap)
        blocks[at] = wide[:, slot, :]
        parts[slot, 2 * chunks : 2 * chunks + 1, :] = jnp.full((1, LANES), (turn + 1).astype(F32), F32)
        lines[at] = parts[slot]
    sums = terms(jnp.full((1, LANES), weight, F32), 3)
    for s, out in enumerate(outs):
        base = moved(me_ref[0], s, groups, 1) * cap
        out[:, 0:orbitals] = jnp.concatenate([blocks[base + k] for k in range(cap)], axis=0).astype(BF16)
        tail = [lines[base + k][0 : 2 * chunks + 1] for k in range(cap)]
        write_tail(out, orbitals, jnp.concatenate(tail + sums, axis=0))


def merge_kernel(order, keep, cap, orbitals, core_ref, when, *refs):
    ins, (same_ref, other_ref, weight_ref, pick_ref) = refs[: len(order)], refs[len(order) :]
    half = keep // 2
    rows = ins[0].shape[0] // cap
    slab = half * rows
    chunks = orbitals // LANES
    each = 2 * chunks + 1
    weight = jnp.zeros((1, LANES), F32)
    walker = [jnp.zeros((rows, orbitals), F32)] * keep
    line = [jnp.zeros((2 * chunks, LANES), F32)] * keep
    for s, ref in zip(order, ins):
        tail = read_tail(ref, orbitals, cap * each + 3)
        weight = weight + (tail[cap * each : cap * each + 1] + tail[cap * each + 1 : cap * each + 2] + tail[cap * each + 2 :])
        for k in range(cap):
            flag = tail[(k + 1) * each - 1 : (k + 1) * each]
            block = ref[k * rows : (k + 1) * rows, 0:orbitals].astype(F32)
            part = tail[k * each : (k + 1) * each - 1]
            for m in range(k, keep, cap):
                mine = jnp.where(flag == m + 1, F32(1.0), F32(0.0))
                pick_ref[s * keep + m : s * keep + m + 1, :] = mine
                walker[m] = jnp.where(wide_mask(mine, orbitals), block, walker[m])
                line[m] = jnp.where(mine > 0, part, line[m])
    weight_ref[...] = jnp.broadcast_to(weight, weight_ref.shape)
    first = core_ref[0] == 0
    for out, order in ((same_ref, (0, 1)), (other_ref, (1, 0))):
        picked = []
        for k in range(half):
            a, b = order[0] * half + k, order[1] * half + k
            picked.append(jnp.where(first, line[a], line[b]))
            block = jnp.where(first, walker[a], walker[b])
            for c in range(chunks):
                at = c * slab + k * rows
                out[at : at + rows, :] = block[:, c * LANES : (c + 1) * LANES].astype(BF16)
        tail = [p[i * chunks : (i + 1) * chunks] for i in range(2) for p in picked]
        out[chunks * slab :, :] = jnp.concatenate(tail, axis=0).astype(BF16)


def power(size):
    return size & (size - 1) == 0


def moved(me, s, size, sign):
    if power(size):
        return me ^ s if isinstance(me, int) else lax.bitwise_xor(me, jnp.int32(s))
    at = me + (s if sign > 0 else size - s)
    return at % size if isinstance(me, int) else lax.rem(at, size)


def hops(n):
    chips = n // 2
    far = list(range(chips // 2, chips)) + list(range(1, chips // 2))
    return [(0, 0)] + [(s, e) for s in far for e in range(2)] + [(0, 1)]


def arrivals(n):
    return hops(n)[:1] + hops(n)[:0:-1]


def partner(blk, s, e, n, sign):
    chip = moved(lax.div(blk, 2), s, n // 2, sign)
    core = lax.rem(blk, 2)
    return 2 * chip + (core if e == 0 else 1 - core)


def fock_kernel(n, half, blk_ref, body_ref, own_ref, sib_ref, *refs):
    ins, outs = refs[:n], refs[n : 2 * n]
    prop, turned, coup, result = refs[2 * n :]
    vec_count, occupied, orbitals = own_ref.shape
    slab = outs[0].shape[0]
    rows = slab // half
    chunks = orbitals // LANES
    blk = blk_ref[0]
    exponent = jnp.zeros((2 * half * chunks, LANES), F32)
    for ref in ins:
        exponent = exponent + ref[chunks * slab :, :].astype(F32)
    growth = jnp.exp(exponent[0 : half * chunks] + exponent[half * chunks :])
    for ref, (s, e) in zip(ins, arrivals(n)):
        source = partner(blk, s, e, n, -1)
        for w in range(half):
            for c in range(chunks):
                piece = ref[c * slab + w * rows : c * slab + (w + 1) * rows, :].astype(F32)
                piece = piece * growth[w * chunks + c : w * chunks + c + 1]
                prop[w, source, :, c * LANES : (c + 1) * LANES] = piece.astype(prop.dtype)
    scaled = jnp.concatenate([prop[w, i] for w in range(half) for i in range(n)], axis=0).astype(BF16)
    turned[...] = jnp.dot(scaled, body_ref[...], preferred_element_type=F32).T.astype(BF16)
    batch = math.gcd(vec_count, 4)
    for c, ref in enumerate((own_ref, sib_ref)):
        for g in range(0, vec_count, batch):
            left = ref[g : g + batch].reshape(batch * occupied, orbitals)
            s = jnp.dot(left, turned[...], preferred_element_type=F32).astype(BF16)
            for k in range(batch):
                at = (c * vec_count + g + k) * occupied
                for w in range(half):
                    coup[w * occupied : (w + 1) * occupied, at : at + occupied] = s[
                        k * occupied : (k + 1) * occupied, w * occupied : (w + 1) * occupied
                    ]
    tile = 256 if orbitals % 256 == 0 else orbitals
    depth = vec_count * occupied
    for t in range(0, orbitals, tile):
        total = jnp.dot(
            coup[:, :depth],
            own_ref[:, :, t : t + tile].reshape(depth, tile),
            preferred_element_type=F32,
        )
        total = total + jnp.dot(
            coup[:, depth:],
            sib_ref[:, :, t : t + tile].reshape(depth, tile),
            preferred_element_type=F32,
        )
        for w in range(half):
            for i in range(n):
                at = w * occupied + i * rows
                result[w, i, :, t : t + tile] = total[at : at + rows].astype(result.dtype)
    for out, (s, e) in zip(outs, hops(n)):
        to = partner(blk, s, e, n, 1)
        for w in range(half):
            out[w * rows : (w + 1) * rows, :] = result[w, to].astype(BF16)


def sum_kernel(n, keep, cap, groups, core_ref, pick_ref, *refs):
    ins, outs = refs[:n], refs[n:]
    slab, orbitals = ins[0].shape
    half = keep // 2
    rows = slab // half
    halves = []
    for e in range(2):
        same = [ref for ref, (_, other) in zip(ins, hops(n)) if other == e]
        total = same[0][...].astype(F32)
        for ref in same[1:]:
            total = total + ref[...].astype(F32)
        halves.append(total)
    first = core_ref[0] == 0
    whole = [jnp.where(first, halves[0], halves[1]), jnp.where(first, halves[1], halves[0])]
    walker = [whole[m // half][(m % half) * rows : (m % half + 1) * rows] for m in range(keep)]
    for s, out in enumerate(outs):
        source = s if power(groups) else (groups - s) % groups
        for k in range(cap):
            value = jnp.zeros((rows, orbitals), F32)
            for m in range(k, keep, cap):
                mine = pick_ref[source * keep + m : source * keep + m + 1, :]
                value = jnp.where(wide_mask(mine, orbitals), walker[m], value)
            out[k * rows : (k + 1) * rows, :] = value.astype(BF16)


def deal_kernel(order, keep, cap, me_ref, target_ref, weights_ref, total_ref, *refs):
    groups = len(order)
    ins, (out_ref, blocks, wide) = refs[:groups], refs[groups:]
    rows, slots, orbitals = out_ref.shape
    live = groups * keep
    for s, ref in zip(order, ins):
        base = moved(me_ref[0], s, groups, -1) * cap
        for k in range(cap):
            blocks[base + k] = ref[k * rows : (k + 1) * rows, :].astype(F32)
    blocks[groups * cap] = jnp.zeros((rows, orbitals), F32)
    for slot in range(slots):
        t = target_ref[slot]
        alive = t < live
        at = jnp.where(alive, lax.rem(t, groups) * cap + lax.rem(lax.div(t, groups), cap), groups * cap)
        weight = jnp.where(alive, weights_ref[slot], F32(0.0))
        factor = jnp.full((1, LANES), weight * live, F32) / total_ref[0:1, :]
        wide[:, slot, :] = blocks[at] * factor[:, 0:1]
    out_ref[...] = wide[...].astype(BF16)


def call(kernel, outs, scalars, held, arrays, scratch, name, flops=0, vmem=VMEM):
    smem = pl.BlockSpec(memory_space=pltpu.SMEM)
    full = pl.BlockSpec(memory_space=pltpu.VMEM)
    size = sum(x.size * x.dtype.itemsize for x in list(arrays) + list(outs))
    return pl.pallas_call(
        kernel,
        out_shape=outs,
        in_specs=[smem] * len(scalars) + [pl.BlockSpec(memory_space=pl.ANY)] * len(held) + [full] * len(arrays),
        out_specs=[full] * len(outs),
        scratch_shapes=scratch,
        compiler_params=pltpu.CompilerParams(vmem_limit_bytes=vmem * 2**20),
        cost_estimate=pl.CostEstimate(flops=flops, bytes_accessed=size, transcendentals=0),
        name=name,
    )(*scalars, *held, *arrays)


def body(walkers, one_body, fields, field_diag, chol, weights, target):
    rows, slots, orbitals = walkers.shape
    vec_count, occupied, _ = chol.shape
    n, groups = lax.axis_size("blk"), lax.axis_size("grp")
    keep = slots // 2
    half = keep // 2
    cap = -(-slots // groups)
    slab = half * rows
    shape = jax.ShapeDtypeStruct
    grp = lax.axis_index("grp").reshape(1)
    blk = lax.axis_index("blk").reshape(1)
    core = lax.rem(blk, 2)

    def to_list(x, s):
        return lax.ppermute(x, "grp", [(i, moved(i, s, groups, 1)) for i in range(groups)]) if s else x

    def to_block(x, s, e):
        if not s and not e:
            return x
        return lax.ppermute(x, "blk", [(i, 2 * moved(i // 2, s, n // 2, 1) + (i % 2 ^ e)) for i in range(n)])

    order = [0] + sorted(range(1, groups), key=lambda s: -bin(s).count("1"))
    chunks = orbitals // LANES
    sibling = to_block(chol, 0, 1)
    width = orbitals + tail_blocks(cap * (2 * chunks + 1) + 3, cap * rows) * LANES
    routed = call(
        functools.partial(route_kernel, keep, cap),
        [shape((cap * rows, width), BF16)] * groups,
        [grp],
        [target, weights, walkers, fields, field_diag],
        [],
        [
            pltpu.SMEM(target.shape, target.dtype),
            pltpu.SMEM(weights.shape, weights.dtype),
            pltpu.VMEM(walkers.shape, walkers.dtype),
            pltpu.VMEM(fields.shape, fields.dtype),
            pltpu.VMEM(field_diag.shape, field_diag.dtype),
            pltpu.VMEM((rows, slots, orbitals), F32),
            pltpu.VMEM((groups * cap + 1, rows, orbitals), F32),
            pltpu.VMEM((slots, 2 * chunks + 4, LANES), F32),
            pltpu.VMEM((groups * cap + 1, 2 * chunks + 4, LANES), F32),
            pltpu.SemaphoreType.DMA((5,)),
        ],
        "route",
        vmem=ROUTE_VMEM,
    )
    (kept,) = call(
        stage_kernel,
        [shape(routed[0].shape, BF16)],
        [],
        [routed[0]],
        [],
        [pltpu.SemaphoreType.DMA((1,))],
        "keep",
    )
    (own,) = call(
        stage_kernel,
        [shape(chol.shape, chol.dtype)],
        [],
        [chol, kept],
        [],
        [pltpu.SemaphoreType.DMA((1,))],
        "stage",
        vmem=STAGE_VMEM,
    )
    routed = [to_list(routed[s], s) if s else kept for s in order]
    payload = shape((chunks * slab + 2 * half * chunks, LANES), BF16)
    same, other, weight_sum, pick = call(
        functools.partial(merge_kernel, order, keep, cap, orbitals),
        [payload, payload, shape((8, LANES), F32), shape((groups * keep, LANES), F32)],
        [core],
        [own],
        routed,
        [],
        "merge",
    )
    (held_body,) = call(
        stage_kernel,
        [shape(one_body.shape, one_body.dtype)],
        [],
        [one_body, weight_sum],
        [],
        [pltpu.SemaphoreType.DMA((1,))],
        "hold",
    )
    gathered = [to_block(other if e else same, s, e) for s, e in arrivals(n)]
    held = F32 if rows % 16 else BF16
    parts = call(
        functools.partial(fock_kernel, n, half),
        [shape((slab, orbitals), BF16)] * n,
        [blk],
        [],
        [held_body, own, sibling] + gathered,
        [
            pltpu.VMEM((half, n, rows, orbitals), held),
            pltpu.VMEM((orbitals, half * occupied), BF16),
            pltpu.VMEM((half * occupied, 2 * vec_count * occupied), BF16),
            pltpu.VMEM((half, n, rows, orbitals), held),
        ],
        "fock",
        flops=2 * n * slab * orbitals * (orbitals + 4 * vec_count * occupied),
    )
    parts = [to_block(x, s, e) for x, (s, e) in zip(parts, hops(n))]
    back = call(
        functools.partial(sum_kernel, n, keep, cap, groups),
        [shape((cap * rows, orbitals), BF16)] * groups,
        [core],
        [],
        [pick] + parts,
        [],
        "sum",
    )
    back = [to_list(back[s], s) for s in order]
    (out,) = call(
        functools.partial(deal_kernel, order, keep, cap),
        [shape(walkers.shape, BF16)],
        [grp, target, weights],
        [],
        [weight_sum] + back,
        [pltpu.VMEM((groups * cap + 1, rows, orbitals), F32), pltpu.VMEM(walkers.shape, F32)],
        "deal",
    )
    return out


def solution(mesh):
    in_specs = (
        P("blk", "grp", None),
        P(),
        P("grp", "blk"),
        P("blk", None),
        P("blk", None, None),
        P("grp"),
        P("grp"),
    )
    out_specs = P("blk", "grp", None)
    return jax.shard_map(body, mesh=mesh, in_specs=in_specs, out_specs=out_specs, check_vma=False)
```

```python
import functools
import math
import jax
import jax.numpy as jnp
from jax import lax
from jax.experimental import pallas as pl
from jax.experimental.pallas import tpu as pltpu
from jax.sharding import PartitionSpec as P

F32 = jnp.float32
BF16 = jnp.bfloat16
LANES = 128
VMEM = 24
ROUTE_VMEM = 56
STAGE_VMEM = 48


def terms(value, count):
    out = []
    for _ in range(count):
        term = value.astype(BF16).astype(F32)
        out.append(term)
        value = value - term
    return out


def tail_blocks(count, slab):
    return -(-count // slab)


def write_tail(out_ref, start, lines):
    slab = out_ref.shape[0]
    for b in range(tail_blocks(lines.shape[0], slab)):
        part = lines[b * slab : (b + 1) * slab]
        if part.shape[0] < slab:
            part = jnp.concatenate([part, jnp.zeros((slab - part.shape[0], LANES), F32)], axis=0)
        out_ref[:, start + b * LANES : start + (b + 1) * LANES] = part.astype(BF16)


def read_tail(ref, start, count):
    parts = [ref[:, c : c + LANES].astype(F32) for c in range(start, ref.shape[1], LANES)]
    whole = parts[0] if len(parts) == 1 else jnp.concatenate(parts, axis=0)
    return whole[0:count]


def wide_mask(line, width):
    return jnp.concatenate([line] * (width // LANES), axis=1) > 0


def stage_kernel(*refs):
    sems = refs[-1]
    count = sems.shape[0]
    copies = [pltpu.make_async_copy(refs[i], refs[i - count - 1], sems.at[i]) for i in range(count)]
    for copy in copies:
        copy.start()
    for copy in copies:
        copy.wait()


def route_kernel(keep, cap, me_ref, target_any, weights_any, walkers_any, fields_any, diag_any, *refs):
    *outs, target_ref, weights_ref, walkers_ref, fields_ref, diag_ref, wide, blocks, parts, lines, sems = refs
    pairs = (
        (walkers_any, walkers_ref),
        (target_any, target_ref),
        (weights_any, weights_ref),
        (fields_any, fields_ref),
        (diag_any, diag_ref),
    )
    copies = [pltpu.make_async_copy(a, b, sems.at[i]) for i, (a, b) in enumerate(pairs)]
    for copy in copies:
        copy.start()
    rows, slots, orbitals = walkers_ref.shape
    vec_count = fields_ref.shape[1]
    chunks = orbitals // LANES
    groups = len(outs)
    live = groups * keep
    blocks[...] = jnp.zeros(blocks.shape, F32)
    lines[...] = jnp.zeros(lines.shape, F32)
    for copy in copies:
        copy.wait()
    wide[...] = walkers_ref[...].astype(F32)
    exponent = fields_ref[:, 0:1] * diag_ref[0:1, :]
    for g in range(1, vec_count):
        exponent = exponent + fields_ref[:, g : g + 1] * diag_ref[g : g + 1, :]
    for i, term in enumerate(terms(exponent, 2)):
        for c in range(chunks):
            parts[:, i * chunks + c, :] = term[:, c * LANES : (c + 1) * LANES]
    weight = F32(0.0)
    for slot in range(slots):
        t = target_ref[slot]
        alive = t < live
        weight = weight + jnp.where(alive, weights_ref[slot], F32(0.0))
        turn = lax.div(t, groups)
        at = jnp.where(alive, lax.rem(t, groups) * cap + lax.rem(turn, cap), groups * cap)
        blocks[at] = wide[:, slot, :]
        parts[slot, 2 * chunks : 2 * chunks + 1, :] = jnp.full((1, LANES), (turn + 1).astype(F32), F32)
        lines[at] = parts[slot]
    sums = terms(jnp.full((1, LANES), weight, F32), 3)
    for s, out in enumerate(outs):
        base = moved(me_ref[0], s, groups, 1) * cap
        out[:, 0:orbitals] = jnp.concatenate([blocks[base + k] for k in range(cap)], axis=0).astype(BF16)
        tail = [lines[base + k][0 : 2 * chunks + 1] for k in range(cap)]
        write_tail(out, orbitals, jnp.concatenate(tail + sums, axis=0))


def merge_kernel(order, keep, cap, orbitals, core_ref, when, *refs):
    ins, (same_ref, other_ref, weight_ref, pick_ref) = refs[: len(order)], refs[len(order) :]
    half = keep // 2
    rows = ins[0].shape[0] // cap
    slab = half * rows
    chunks = orbitals // LANES
    each = 2 * chunks + 1
    weight = jnp.zeros((1, LANES), F32)
    walker = [jnp.zeros((rows, orbitals), F32)] * keep
    line = [jnp.zeros((2 * chunks, LANES), F32)] * keep
    for s, ref in zip(order, ins):
        tail = read_tail(ref, orbitals, cap * each + 3)
        weight = weight + (tail[cap * each : cap * each + 1] + tail[cap * each + 1 : cap * each + 2] + tail[cap * each + 2 :])
        for k in range(cap):
            flag = tail[(k + 1) * each - 1 : (k + 1) * each]
            block = ref[k * rows : (k + 1) * rows, 0:orbitals].astype(F32)
            part = tail[k * each : (k + 1) * each - 1]
            for m in range(k, keep, cap):
                mine = jnp.where(flag == m + 1, F32(1.0), F32(0.0))
                pick_ref[s * keep + m : s * keep + m + 1, :] = mine
                walker[m] = jnp.where(wide_mask(mine, orbitals), block, walker[m])
                line[m] = jnp.where(mine > 0, part, line[m])
    weight_ref[...] = jnp.broadcast_to(weight, weight_ref.shape)
    first = core_ref[0] == 0
    for out, order in ((same_ref, (0, 1)), (other_ref, (1, 0))):
        picked = []
        for k in range(half):
            a, b = order[0] * half + k, order[1] * half + k
            picked.append(jnp.where(first, line[a], line[b]))
            block = jnp.where(first, walker[a], walker[b])
            for c in range(chunks):
                at = c * slab + k * rows
                out[at : at + rows, :] = block[:, c * LANES : (c + 1) * LANES].astype(BF16)
        tail = [p[i * chunks : (i + 1) * chunks] for i in range(2) for p in picked]
        out[chunks * slab :, :] = jnp.concatenate(tail, axis=0).astype(BF16)


def power(size):
    return size & (size - 1) == 0


def moved(me, s, size, sign):
    if power(size):
        return me ^ s if isinstance(me, int) else lax.bitwise_xor(me, jnp.int32(s))
    at = me + (s if sign > 0 else size - s)
    return at % size if isinstance(me, int) else lax.rem(at, size)


def hops(n):
    chips = n // 2
    far = list(range(chips // 2, chips)) + list(range(1, chips // 2))
    return [(0, 0)] + [(s, e) for s in far for e in range(2)] + [(0, 1)]


def arrivals(n):
    return hops(n)[:1] + hops(n)[:0:-1]


def leading(s, chips):
    top = 1 << (s.bit_length() - 1) if s else 0
    return top if power(chips) else s


def returns(n):
    return [(s, e) for s, e in hops(n) if leading(s, n // 2) == s]


def add_kernel(count, *refs):
    outs = refs[len(refs) - 1 - count :]
    ins = refs[: len(refs) - 1 - count]
    total = ins[count][...].astype(F32)
    for ref in ins[count + 1 :]:
        total = total + ref[...].astype(F32)
    outs[0][...] = total.astype(BF16)
    for i in range(count):
        outs[1 + i][...] = ins[i][...]


def partner(blk, s, e, n, sign):
    chip = moved(lax.div(blk, 2), s, n // 2, sign)
    core = lax.rem(blk, 2)
    return 2 * chip + (core if e == 0 else 1 - core)


def fock_kernel(n, half, blk_ref, body_ref, own_ref, sib_ref, *refs):
    ins, outs = refs[:n], refs[n : 2 * n]
    prop, turned, coup, result = refs[2 * n :]
    vec_count, occupied, orbitals = own_ref.shape
    slab = outs[0].shape[0]
    rows = slab // half
    chunks = orbitals // LANES
    blk = blk_ref[0]
    exponent = jnp.zeros((2 * half * chunks, LANES), F32)
    for ref in ins:
        exponent = exponent + ref[chunks * slab :, :].astype(F32)
    growth = jnp.exp(exponent[0 : half * chunks] + exponent[half * chunks :])
    for ref, (s, e) in zip(ins, arrivals(n)):
        source = partner(blk, s, e, n, -1)
        for w in range(half):
            for c in range(chunks):
                piece = ref[c * slab + w * rows : c * slab + (w + 1) * rows, :].astype(F32)
                piece = piece * growth[w * chunks + c : w * chunks + c + 1]
                prop[w, source, :, c * LANES : (c + 1) * LANES] = piece.astype(prop.dtype)
    scaled = jnp.concatenate([prop[w, i] for w in range(half) for i in range(n)], axis=0).astype(BF16)
    turned[...] = jnp.dot(scaled, body_ref[...], preferred_element_type=F32).T.astype(BF16)
    batch = math.gcd(vec_count, 4)
    for c, ref in enumerate((own_ref, sib_ref)):
        for g in range(0, vec_count, batch):
            left = ref[g : g + batch].reshape(batch * occupied, orbitals)
            s = jnp.dot(left, turned[...], preferred_element_type=F32).astype(BF16)
            for k in range(batch):
                at = (c * vec_count + g + k) * occupied
                for w in range(half):
                    coup[w * occupied : (w + 1) * occupied, at : at + occupied] = s[
                        k * occupied : (k + 1) * occupied, w * occupied : (w + 1) * occupied
                    ]
    tile = 256 if orbitals % 256 == 0 else orbitals
    depth = vec_count * occupied
    for t in range(0, orbitals, tile):
        total = jnp.dot(
            coup[:, :depth],
            own_ref[:, :, t : t + tile].reshape(depth, tile),
            preferred_element_type=F32,
        )
        total = total + jnp.dot(
            coup[:, depth:],
            sib_ref[:, :, t : t + tile].reshape(depth, tile),
            preferred_element_type=F32,
        )
        for w in range(half):
            for i in range(n):
                at = w * occupied + i * rows
                result[w, i, :, t : t + tile] = total[at : at + rows].astype(result.dtype)
    for out, (s, e) in zip(outs, hops(n)):
        to = partner(blk, s, e, n, 1)
        for w in range(half):
            out[w * rows : (w + 1) * rows, :] = result[w, to].astype(BF16)


def sum_kernel(n, keep, cap, groups, core_ref, pick_ref, *refs):
    known = returns(n)
    ins, outs = refs[: len(known)], refs[len(known) :]
    slab, orbitals = ins[0].shape
    half = keep // 2
    rows = slab // half
    halves = []
    for e in range(2):
        same = [ref for ref, (_, other) in zip(ins, known) if other == e]
        total = same[0][...].astype(F32)
        for ref in same[1:]:
            total = total + ref[...].astype(F32)
        halves.append(total)
    first = core_ref[0] == 0
    whole = [jnp.where(first, halves[0], halves[1]), jnp.where(first, halves[1], halves[0])]
    walker = [whole[m // half][(m % half) * rows : (m % half + 1) * rows] for m in range(keep)]
    for s, out in enumerate(outs):
        source = s if power(groups) else (groups - s) % groups
        for k in range(cap):
            value = jnp.zeros((rows, orbitals), F32)
            for m in range(k, keep, cap):
                mine = pick_ref[source * keep + m : source * keep + m + 1, :]
                value = jnp.where(wide_mask(mine, orbitals), walker[m], value)
            out[k * rows : (k + 1) * rows, :] = value.astype(BF16)


def deal_kernel(order, keep, cap, me_ref, target_ref, weights_ref, total_ref, *refs):
    groups = len(order)
    ins, (out_ref, blocks, wide) = refs[:groups], refs[groups:]
    rows, slots, orbitals = out_ref.shape
    live = groups * keep
    for s, ref in zip(order, ins):
        base = moved(me_ref[0], s, groups, -1) * cap
        for k in range(cap):
            blocks[base + k] = ref[k * rows : (k + 1) * rows, :].astype(F32)
    blocks[groups * cap] = jnp.zeros((rows, orbitals), F32)
    for slot in range(slots):
        t = target_ref[slot]
        alive = t < live
        at = jnp.where(alive, lax.rem(t, groups) * cap + lax.rem(lax.div(t, groups), cap), groups * cap)
        weight = jnp.where(alive, weights_ref[slot], F32(0.0))
        factor = jnp.full((1, LANES), weight * live, F32) / total_ref[0:1, :]
        wide[:, slot, :] = blocks[at] * factor[:, 0:1]
    out_ref[...] = wide[...].astype(BF16)


def call(kernel, outs, scalars, held, arrays, scratch, name, flops=0, vmem=VMEM):
    smem = pl.BlockSpec(memory_space=pltpu.SMEM)
    full = pl.BlockSpec(memory_space=pltpu.VMEM)
    size = sum(x.size * x.dtype.itemsize for x in list(arrays) + list(outs))
    return pl.pallas_call(
        kernel,
        out_shape=outs,
        in_specs=[smem] * len(scalars) + [pl.BlockSpec(memory_space=pl.ANY)] * len(held) + [full] * len(arrays),
        out_specs=[full] * len(outs),
        scratch_shapes=scratch,
        compiler_params=pltpu.CompilerParams(vmem_limit_bytes=vmem * 2**20),
        cost_estimate=pl.CostEstimate(flops=flops, bytes_accessed=size, transcendentals=0),
        name=name,
    )(*scalars, *held, *arrays)


def body(walkers, one_body, fields, field_diag, chol, weights, target):
    rows, slots, orbitals = walkers.shape
    vec_count, occupied, _ = chol.shape
    n, groups = lax.axis_size("blk"), lax.axis_size("grp")
    keep = slots // 2
    half = keep // 2
    cap = -(-slots // groups)
    slab = half * rows
    shape = jax.ShapeDtypeStruct
    grp = lax.axis_index("grp").reshape(1)
    blk = lax.axis_index("blk").reshape(1)
    core = lax.rem(blk, 2)

    def to_list(x, s):
        return lax.ppermute(x, "grp", [(i, moved(i, s, groups, 1)) for i in range(groups)]) if s else x

    def to_block(x, s, e):
        if not s and not e:
            return x
        return lax.ppermute(x, "blk", [(i, 2 * moved(i // 2, s, n // 2, 1) + (i % 2 ^ e)) for i in range(n)])

    order = [0] + sorted(range(1, groups), key=lambda s: -bin(s).count("1"))
    chunks = orbitals // LANES
    sibling = to_block(chol, 0, 1)
    width = orbitals + tail_blocks(cap * (2 * chunks + 1) + 3, cap * rows) * LANES
    routed = call(
        functools.partial(route_kernel, keep, cap),
        [shape((cap * rows, width), BF16)] * groups,
        [grp],
        [target, weights, walkers, fields, field_diag],
        [],
        [
            pltpu.SMEM(target.shape, target.dtype),
            pltpu.SMEM(weights.shape, weights.dtype),
            pltpu.VMEM(walkers.shape, walkers.dtype),
            pltpu.VMEM(fields.shape, fields.dtype),
            pltpu.VMEM(field_diag.shape, field_diag.dtype),
            pltpu.VMEM((rows, slots, orbitals), F32),
            pltpu.VMEM((groups * cap + 1, rows, orbitals), F32),
            pltpu.VMEM((slots, 2 * chunks + 4, LANES), F32),
            pltpu.VMEM((groups * cap + 1, 2 * chunks + 4, LANES), F32),
            pltpu.SemaphoreType.DMA((5,)),
        ],
        "route",
        vmem=ROUTE_VMEM,
    )
    (kept,) = call(
        stage_kernel,
        [shape(routed[0].shape, BF16)],
        [],
        [routed[0]],
        [],
        [pltpu.SemaphoreType.DMA((1,))],
        "keep",
    )
    (own,) = call(
        stage_kernel,
        [shape(chol.shape, chol.dtype)],
        [],
        [chol, kept],
        [],
        [pltpu.SemaphoreType.DMA((1,))],
        "stage",
        vmem=STAGE_VMEM,
    )
    routed = [to_list(routed[s], s) if s else kept for s in order]
    payload = shape((chunks * slab + 2 * half * chunks, LANES), BF16)
    same, other, weight_sum, pick = call(
        functools.partial(merge_kernel, order, keep, cap, orbitals),
        [payload, payload, shape((8, LANES), F32), shape((groups * keep, LANES), F32)],
        [core],
        [own],
        routed,
        [],
        "merge",
    )
    (held_body,) = call(
        stage_kernel,
        [shape(one_body.shape, one_body.dtype)],
        [],
        [one_body, weight_sum],
        [],
        [pltpu.SemaphoreType.DMA((1,))],
        "hold",
    )
    gathered = {}
    for s, e in arrivals(n):
        if leading(s, n // 2) == s:
            gathered[s, e] = to_block(other if e else same, s, e)
    for s, e in arrivals(n):
        top = leading(s, n // 2)
        if top != s:
            gathered[s, e] = to_block(gathered[top, e], s ^ top, 0)
    gathered = [gathered[hop] for hop in arrivals(n)]
    held = F32 if rows % 16 else BF16
    parts = call(
        functools.partial(fock_kernel, n, half),
        [shape((slab, orbitals), BF16)] * n,
        [blk],
        [],
        [held_body, own, sibling] + gathered,
        [
            pltpu.VMEM((half, n, rows, orbitals), held),
            pltpu.VMEM((orbitals, half * occupied), BF16),
            pltpu.VMEM((half * occupied, 2 * vec_count * occupied), BF16),
            pltpu.VMEM((half, n, rows, orbitals), held),
        ],
        "fock",
        flops=2 * n * slab * orbitals * (orbitals + 4 * vec_count * occupied),
    )
    parts = dict(zip(hops(n), parts))
    for s, e in returns(n):
        via = [hop for hop in hops(n) if hop[1] == e and hop[0] != s and leading(hop[0], n // 2) == s]
        if via:
            later = [hop for hop in returns(n) if 0 < hop[0] < s and hop[1] == e] + [(0, 1)] * e
            terms_in = [parts[s, e]] + [to_block(parts[hop], hop[0] ^ s, 0) for hop in via]
            out = call(
                functools.partial(add_kernel, len(later)),
                [shape((slab, orbitals), BF16)] * (1 + len(later)),
                [],
                [],
                [parts[hop] for hop in later] + terms_in,
                [],
                "add",
            )
            parts.update(zip([(s, e)] + later, out))
    backs = [to_block(parts[hop], *hop) for hop in returns(n)]
    back = call(
        functools.partial(sum_kernel, n, keep, cap, groups),
        [shape((cap * rows, orbitals), BF16)] * groups,
        [core],
        [],
        [pick] + backs,
        [],
        "sum",
    )
    back = [to_list(back[s], s) for s in order]
    (out,) = call(
        functools.partial(deal_kernel, order, keep, cap),
        [shape(walkers.shape, BF16)],
        [grp, target, weights],
        [],
        [weight_sum] + back,
        [pltpu.VMEM((groups * cap + 1, rows, orbitals), F32), pltpu.VMEM(walkers.shape, F32)],
        "deal",
    )
    return out


def solution(mesh):
    in_specs = (
        P("blk", "grp", None),
        P(),
        P("grp", "blk"),
        P("blk", None),
        P("blk", None, None),
        P("grp"),
        P("grp"),
    )
    out_specs = P("blk", "grp", None)
    return jax.shard_map(body, mesh=mesh, in_specs=in_specs, out_specs=out_specs, check_vma=False)
```

```python
import functools
import math
import jax
import jax.numpy as jnp
from jax import lax
from jax.experimental import pallas as pl
from jax.experimental.pallas import tpu as pltpu
from jax.sharding import PartitionSpec as P

F32 = jnp.float32
BF16 = jnp.bfloat16
LANES = 128
VMEM = 24
ROUTE_VMEM = 56
STAGE_VMEM = 48


def terms(value, count):
    out = []
    for _ in range(count):
        term = value.astype(BF16).astype(F32)
        out.append(term)
        value = value - term
    return out


def tail_blocks(count, slab):
    return -(-count // slab)


def write_tail(out_ref, start, lines):
    slab = out_ref.shape[0]
    for b in range(tail_blocks(lines.shape[0], slab)):
        part = lines[b * slab : (b + 1) * slab]
        if part.shape[0] < slab:
            part = jnp.concatenate([part, jnp.zeros((slab - part.shape[0], LANES), F32)], axis=0)
        out_ref[:, start + b * LANES : start + (b + 1) * LANES] = part.astype(BF16)


def read_tail(ref, start, count):
    parts = [ref[:, c : c + LANES].astype(F32) for c in range(start, ref.shape[1], LANES)]
    whole = parts[0] if len(parts) == 1 else jnp.concatenate(parts, axis=0)
    return whole[0:count]


def wide_mask(line, width):
    return jnp.concatenate([line] * (width // LANES), axis=1) > 0


def stage_kernel(*refs):
    sems = refs[-1]
    count = sems.shape[0]
    copies = [pltpu.make_async_copy(refs[i], refs[i - count - 1], sems.at[i]) for i in range(count)]
    for copy in copies:
        copy.start()
    for copy in copies:
        copy.wait()


def route_kernel(keep, cap, me_ref, target_any, weights_any, walkers_any, fields_any, diag_any, *refs):
    *outs, target_ref, weights_ref, walkers_ref, fields_ref, diag_ref, wide, blocks, parts, lines, sems = refs
    pairs = (
        (walkers_any, walkers_ref),
        (target_any, target_ref),
        (weights_any, weights_ref),
        (fields_any, fields_ref),
        (diag_any, diag_ref),
    )
    copies = [pltpu.make_async_copy(a, b, sems.at[i]) for i, (a, b) in enumerate(pairs)]
    for copy in copies:
        copy.start()
    rows, slots, orbitals = walkers_ref.shape
    vec_count = fields_ref.shape[1]
    chunks = orbitals // LANES
    groups = len(outs)
    live = groups * keep
    blocks[...] = jnp.zeros(blocks.shape, F32)
    lines[...] = jnp.zeros(lines.shape, F32)
    for copy in copies:
        copy.wait()
    wide[...] = walkers_ref[...].astype(F32)
    exponent = fields_ref[:, 0:1] * diag_ref[0:1, :]
    for g in range(1, vec_count):
        exponent = exponent + fields_ref[:, g : g + 1] * diag_ref[g : g + 1, :]
    for i, term in enumerate(terms(exponent, 2)):
        for c in range(chunks):
            parts[:, i * chunks + c, :] = term[:, c * LANES : (c + 1) * LANES]
    weight = F32(0.0)
    for slot in range(slots):
        t = target_ref[slot]
        alive = t < live
        weight = weight + jnp.where(alive, weights_ref[slot], F32(0.0))
        turn = lax.div(t, groups)
        at = jnp.where(alive, lax.rem(t, groups) * cap + lax.rem(turn, cap), groups * cap)
        blocks[at] = wide[:, slot, :]
        parts[slot, 2 * chunks : 2 * chunks + 1, :] = jnp.full((1, LANES), (turn + 1).astype(F32), F32)
        lines[at] = parts[slot]
    sums = terms(jnp.full((1, LANES), weight, F32), 3)
    for s, out in enumerate(outs):
        base = moved(me_ref[0], s, groups, 1) * cap
        out[:, 0:orbitals] = jnp.concatenate([blocks[base + k] for k in range(cap)], axis=0).astype(BF16)
        tail = [lines[base + k][0 : 2 * chunks + 1] for k in range(cap)]
        write_tail(out, orbitals, jnp.concatenate(tail + sums, axis=0))


def merge_kernel(order, keep, cap, orbitals, core_ref, when, *refs):
    ins, (same_ref, other_ref, weight_ref, pick_ref) = refs[: len(order)], refs[len(order) :]
    half = keep // 2
    rows = ins[0].shape[0] // cap
    slab = half * rows
    chunks = orbitals // LANES
    each = 2 * chunks + 1
    weight = jnp.zeros((1, LANES), F32)
    walker = [jnp.zeros((rows, orbitals), F32)] * keep
    line = [jnp.zeros((2 * chunks, LANES), F32)] * keep
    for s, ref in zip(order, ins):
        tail = read_tail(ref, orbitals, cap * each + 3)
        weight = weight + (tail[cap * each : cap * each + 1] + tail[cap * each + 1 : cap * each + 2] + tail[cap * each + 2 :])
        for k in range(cap):
            flag = tail[(k + 1) * each - 1 : (k + 1) * each]
            block = ref[k * rows : (k + 1) * rows, 0:orbitals].astype(F32)
            part = tail[k * each : (k + 1) * each - 1]
            for m in range(k, keep, cap):
                mine = jnp.where(flag == m + 1, F32(1.0), F32(0.0))
                pick_ref[s * keep + m : s * keep + m + 1, :] = mine
                walker[m] = jnp.where(wide_mask(mine, orbitals), block, walker[m])
                line[m] = jnp.where(mine > 0, part, line[m])
    weight_ref[...] = jnp.broadcast_to(weight, weight_ref.shape)
    first = core_ref[0] == 0
    for out, order in ((same_ref, (0, 1)), (other_ref, (1, 0))):
        picked = []
        for k in range(half):
            a, b = order[0] * half + k, order[1] * half + k
            picked.append(jnp.where(first, line[a], line[b]))
            block = jnp.where(first, walker[a], walker[b])
            for c in range(chunks):
                at = c * slab + k * rows
                out[at : at + rows, :] = block[:, c * LANES : (c + 1) * LANES].astype(BF16)
        tail = [p[i * chunks : (i + 1) * chunks] for i in range(2) for p in picked]
        out[chunks * slab :, :] = jnp.concatenate(tail, axis=0).astype(BF16)


def power(size):
    return size & (size - 1) == 0


def moved(me, s, size, sign):
    if power(size):
        return me ^ s if isinstance(me, int) else lax.bitwise_xor(me, jnp.int32(s))
    at = me + (s if sign > 0 else size - s)
    return at % size if isinstance(me, int) else lax.rem(at, size)


def hops(n):
    chips = n // 2
    far = list(range(chips // 2, chips)) + list(range(1, chips // 2))
    return [(0, 0)] + [(s, e) for s in far for e in range(2)] + [(0, 1)]


def arrivals(n):
    return hops(n)[:1] + hops(n)[:0:-1]


def leading(s, chips):
    top = 1 << (s.bit_length() - 1) if s else 0
    return top if power(chips) else s


def partner(blk, s, e, n, sign):
    chip = moved(lax.div(blk, 2), s, n // 2, sign)
    core = lax.rem(blk, 2)
    return 2 * chip + (core if e == 0 else 1 - core)


def fock_kernel(n, half, blk_ref, body_ref, own_ref, sib_ref, *refs):
    ins, outs = refs[:n], refs[n : 2 * n]
    prop, carried, coup, result = refs[2 * n :]
    vec_count, occupied, orbitals = own_ref.shape
    slab = outs[0].shape[0]
    rows = slab // half
    chunks = orbitals // LANES
    blk = blk_ref[0]
    exponent = jnp.zeros((2 * half * chunks, LANES), F32)
    for ref in ins:
        exponent = exponent + ref[chunks * slab :, :].astype(F32)
    growth = jnp.exp(exponent[0 : half * chunks] + exponent[half * chunks :])
    for ref, (s, e) in zip(ins, arrivals(n)):
        source = partner(blk, s, e, n, -1)
        for w in range(half):
            for c in range(chunks):
                piece = ref[c * slab + w * rows : c * slab + (w + 1) * rows, :].astype(F32)
                piece = piece * growth[w * chunks + c : w * chunks + c + 1]
                prop[w, source, :, c * LANES : (c + 1) * LANES] = piece.astype(prop.dtype)
    scaled = jnp.concatenate([prop[w, i] for w in range(half) for i in range(n)], axis=0).astype(BF16)
    carried[...] = jnp.dot(scaled, body_ref[...], preferred_element_type=F32).astype(BF16)
    batch = math.gcd(vec_count, 4)
    for c, ref in enumerate((own_ref, sib_ref)):
        for g in range(0, vec_count, batch):
            left = ref[g : g + batch].reshape(batch * occupied, orbitals)
            s = lax.dot_general(left, carried[...], (((1,), (1,)), ((), ())), preferred_element_type=F32).astype(BF16)
            for k in range(batch):
                at = (c * vec_count + g + k) * occupied
                for w in range(half):
                    coup[w * occupied : (w + 1) * occupied, at : at + occupied] = s[
                        k * occupied : (k + 1) * occupied, w * occupied : (w + 1) * occupied
                    ]
    tile = 256 if orbitals % 256 == 0 else orbitals
    depth = vec_count * occupied
    for t in range(0, orbitals, tile):
        total = jnp.dot(
            coup[:, :depth],
            own_ref[:, :, t : t + tile].reshape(depth, tile),
            preferred_element_type=F32,
        )
        total = total + jnp.dot(
            coup[:, depth:],
            sib_ref[:, :, t : t + tile].reshape(depth, tile),
            preferred_element_type=F32,
        )
        for w in range(half):
            for i in range(n):
                at = w * occupied + i * rows
                result[w, i, :, t : t + tile] = total[at : at + rows].astype(result.dtype)
    for out, (s, e) in zip(outs, hops(n)):
        to = partner(blk, s, e, n, 1)
        for w in range(half):
            out[w * rows : (w + 1) * rows, :] = result[w, to].astype(BF16)


def sum_kernel(n, keep, cap, groups, core_ref, pick_ref, *refs):
    ins, outs = refs[:n], refs[n:]
    slab, orbitals = ins[0].shape
    half = keep // 2
    rows = slab // half
    halves = []
    for e in range(2):
        same = [ref for ref, (_, other) in zip(ins, hops(n)) if other == e]
        total = same[0][...].astype(F32)
        for ref in same[1:]:
            total = total + ref[...].astype(F32)
        halves.append(total)
    first = core_ref[0] == 0
    whole = [jnp.where(first, halves[0], halves[1]), jnp.where(first, halves[1], halves[0])]
    walker = [whole[m // half][(m % half) * rows : (m % half + 1) * rows] for m in range(keep)]
    for s, out in enumerate(outs):
        source = s if power(groups) else (groups - s) % groups
        for k in range(cap):
            value = jnp.zeros((rows, orbitals), F32)
            for m in range(k, keep, cap):
                mine = pick_ref[source * keep + m : source * keep + m + 1, :]
                value = jnp.where(wide_mask(mine, orbitals), walker[m], value)
            out[k * rows : (k + 1) * rows, :] = value.astype(BF16)


def deal_kernel(order, keep, cap, me_ref, target_ref, weights_ref, total_ref, *refs):
    groups = len(order)
    ins, (out_any, blocks, wide, held, sems) = refs[:groups], refs[groups:]
    rows, slots, orbitals = wide.shape
    live = groups * keep
    for s, ref in zip(order, ins):
        base = moved(me_ref[0], s, groups, -1) * cap
        for k in range(cap):
            blocks[base + k] = ref[k * rows : (k + 1) * rows, :].astype(F32)
    blocks[groups * cap] = jnp.zeros((rows, orbitals), F32)
    places = []
    for slot in range(slots):
        t = target_ref[slot]
        alive = t < live
        at = jnp.where(alive, lax.rem(t, groups) * cap + lax.rem(lax.div(t, groups), cap), groups * cap)
        weight = jnp.where(alive, weights_ref[slot], F32(0.0))
        factor = jnp.full((1, LANES), weight * live, F32) / total_ref[0:1, :]
        places.append((at, factor[:, 0:1]))
    step = rows // sems.shape[0]
    copies = []
    for h in range(sems.shape[0]):
        band = slice(h * step, (h + 1) * step)
        for slot, (at, factor) in enumerate(places):
            wide[band, slot, :] = blocks[at, band, :] * factor
        held[band] = wide[band].astype(BF16)
        copies.append(pltpu.make_async_copy(held.at[band], out_any.at[band], sems.at[h]))
        copies[-1].start()
    for copy in copies:
        copy.wait()


def call(kernel, outs, scalars, held, arrays, scratch, name, flops=0, vmem=VMEM, place=pltpu.VMEM):
    smem = pl.BlockSpec(memory_space=pltpu.SMEM)
    full = pl.BlockSpec(memory_space=pltpu.VMEM)
    size = sum(x.size * x.dtype.itemsize for x in list(arrays) + list(outs))
    return pl.pallas_call(
        kernel,
        out_shape=outs,
        in_specs=[smem] * len(scalars) + [pl.BlockSpec(memory_space=pl.ANY)] * len(held) + [full] * len(arrays),
        out_specs=[pl.BlockSpec(memory_space=place)] * len(outs),
        scratch_shapes=scratch,
        compiler_params=pltpu.CompilerParams(vmem_limit_bytes=vmem * 2**20),
        cost_estimate=pl.CostEstimate(flops=flops, bytes_accessed=size, transcendentals=0),
        name=name,
    )(*scalars, *held, *arrays)


def body(walkers, one_body, fields, field_diag, chol, weights, target):
    rows, slots, orbitals = walkers.shape
    vec_count, occupied, _ = chol.shape
    n, groups = lax.axis_size("blk"), lax.axis_size("grp")
    keep = slots // 2
    half = keep // 2
    cap = -(-slots // groups)
    slab = half * rows
    shape = jax.ShapeDtypeStruct
    grp = lax.axis_index("grp").reshape(1)
    blk = lax.axis_index("blk").reshape(1)
    core = lax.rem(blk, 2)

    def to_list(x, s):
        return lax.ppermute(x, "grp", [(i, moved(i, s, groups, 1)) for i in range(groups)]) if s else x

    def to_block(x, s, e):
        if not s and not e:
            return x
        return lax.ppermute(x, "blk", [(i, 2 * moved(i // 2, s, n // 2, 1) + (i % 2 ^ e)) for i in range(n)])

    order = [0] + sorted(range(1, groups), key=lambda s: (s & 1, -s))
    chunks = orbitals // LANES
    sibling = to_block(chol, 0, 1)
    width = orbitals + tail_blocks(cap * (2 * chunks + 1) + 3, cap * rows) * LANES
    routed = call(
        functools.partial(route_kernel, keep, cap),
        [shape((cap * rows, width), BF16)] * groups,
        [grp],
        [target, weights, walkers, fields, field_diag],
        [],
        [
            pltpu.SMEM(target.shape, target.dtype),
            pltpu.SMEM(weights.shape, weights.dtype),
            pltpu.VMEM(walkers.shape, walkers.dtype),
            pltpu.VMEM(fields.shape, fields.dtype),
            pltpu.VMEM(field_diag.shape, field_diag.dtype),
            pltpu.VMEM((rows, slots, orbitals), F32),
            pltpu.VMEM((groups * cap + 1, rows, orbitals), F32),
            pltpu.VMEM((slots, 2 * chunks + 4, LANES), F32),
            pltpu.VMEM((groups * cap + 1, 2 * chunks + 4, LANES), F32),
            pltpu.SemaphoreType.DMA((5,)),
        ],
        "route",
        vmem=ROUTE_VMEM,
    )
    (kept,) = call(
        stage_kernel,
        [shape(routed[0].shape, BF16)],
        [],
        [routed[0]],
        [],
        [pltpu.SemaphoreType.DMA((1,))],
        "keep",
    )
    (own,) = call(
        stage_kernel,
        [shape(chol.shape, chol.dtype)],
        [],
        [chol, kept],
        [],
        [pltpu.SemaphoreType.DMA((1,))],
        "stage",
        vmem=STAGE_VMEM,
    )
    routed = [to_list(routed[s], s) if s else kept for s in order]
    payload = shape((chunks * slab + 2 * half * chunks, LANES), BF16)
    same, other, weight_sum, pick = call(
        functools.partial(merge_kernel, order, keep, cap, orbitals),
        [payload, payload, shape((8, LANES), F32), shape((groups * keep, LANES), F32)],
        [core],
        [own],
        routed,
        [],
        "merge",
    )
    (held_body,) = call(
        stage_kernel,
        [shape(one_body.shape, one_body.dtype)],
        [],
        [one_body, weight_sum],
        [],
        [pltpu.SemaphoreType.DMA((1,))],
        "hold",
    )
    gathered = {}
    for s, e in arrivals(n):
        if leading(s, n // 2) == s:
            gathered[s, e] = to_block(other if e else same, s, e)
    for s, e in arrivals(n):
        top = leading(s, n // 2)
        if top != s:
            gathered[s, e] = to_block(gathered[top, e], s ^ top, 0)
    gathered = [gathered[hop] for hop in arrivals(n)]
    held = F32 if rows % 16 else BF16
    parts = call(
        functools.partial(fock_kernel, n, half),
        [shape((slab, orbitals), BF16)] * n,
        [blk],
        [],
        [held_body, own, sibling] + gathered,
        [
            pltpu.VMEM((half, n, rows, orbitals), held),
            pltpu.VMEM((half * occupied, orbitals), BF16),
            pltpu.VMEM((half * occupied, 2 * vec_count * occupied), BF16),
            pltpu.VMEM((half, n, rows, orbitals), held),
        ],
        "fock",
        flops=2 * n * slab * orbitals * (orbitals + 4 * vec_count * occupied),
    )
    backs = [to_block(x, s, e) for x, (s, e) in zip(parts, hops(n))]
    back = call(
        functools.partial(sum_kernel, n, keep, cap, groups),
        [shape((cap * rows, orbitals), BF16)] * groups,
        [core],
        [],
        [pick] + backs,
        [],
        "sum",
    )
    back = [to_list(back[s], s) for s in order]
    (out,) = call(
        functools.partial(deal_kernel, order, keep, cap),
        [shape(walkers.shape, BF16)],
        [grp, target, weights],
        [],
        [weight_sum] + back,
        [
            pltpu.VMEM((groups * cap + 1, rows, orbitals), F32),
            pltpu.VMEM(walkers.shape, F32),
            pltpu.VMEM(walkers.shape, BF16),
            pltpu.SemaphoreType.DMA((2,)),
        ],
        "deal",
        place=pl.ANY,
    )
    return out


def solution(mesh):
    in_specs = (
        P("blk", "grp", None),
        P(),
        P("grp", "blk"),
        P("blk", None),
        P("blk", None, None),
        P("grp"),
        P("grp"),
    )
    out_specs = P("blk", "grp", None)
    return jax.shard_map(body, mesh=mesh, in_specs=in_specs, out_specs=out_specs, check_vma=False)
```

```python
import functools
import math
import jax
import jax.numpy as jnp
from jax import lax
from jax.experimental import pallas as pl
from jax.experimental.pallas import tpu as pltpu
from jax.sharding import PartitionSpec as P

F32 = jnp.float32
BF16 = jnp.bfloat16
LANES = 128
VMEM = 24
ROUTE_VMEM = 56
STAGE_VMEM = 48


def terms(value, count):
    out = []
    for _ in range(count):
        term = value.astype(BF16).astype(F32)
        out.append(term)
        value = value - term
    return out


def tail_blocks(count, slab):
    return -(-count // slab)


def write_tail(out_ref, start, lines):
    slab = out_ref.shape[0]
    for b in range(tail_blocks(lines.shape[0], slab)):
        part = lines[b * slab : (b + 1) * slab]
        if part.shape[0] < slab:
            part = jnp.concatenate([part, jnp.zeros((slab - part.shape[0], LANES), F32)], axis=0)
        out_ref[:, start + b * LANES : start + (b + 1) * LANES] = part.astype(BF16)


def read_tail(ref, start, count):
    parts = [ref[:, c : c + LANES].astype(F32) for c in range(start, ref.shape[1], LANES)]
    whole = parts[0] if len(parts) == 1 else jnp.concatenate(parts, axis=0)
    return whole[0:count]


def wide_mask(line, width):
    return jnp.concatenate([line] * (width // LANES), axis=1) > 0


def stage_kernel(*refs):
    sems = refs[-1]
    count = sems.shape[0]
    copies = [pltpu.make_async_copy(refs[i], refs[i - count - 1], sems.at[i]) for i in range(count)]
    for copy in copies:
        copy.start()
    for copy in copies:
        copy.wait()


def route_kernel(keep, cap, me_ref, target_any, weights_any, walkers_any, fields_any, diag_any, *refs):
    *outs, target_ref, weights_ref, walkers_ref, fields_ref, diag_ref, wide, blocks, parts, lines, sems = refs
    pairs = (
        (walkers_any, walkers_ref),
        (target_any, target_ref),
        (weights_any, weights_ref),
        (fields_any, fields_ref),
        (diag_any, diag_ref),
    )
    copies = [pltpu.make_async_copy(a, b, sems.at[i]) for i, (a, b) in enumerate(pairs)]
    for copy in copies:
        copy.start()
    rows, slots, orbitals = walkers_ref.shape
    vec_count = fields_ref.shape[1]
    chunks = orbitals // LANES
    groups = len(outs)
    live = groups * keep
    blocks[...] = jnp.zeros(blocks.shape, F32)
    lines[...] = jnp.zeros(lines.shape, F32)
    for copy in copies:
        copy.wait()
    wide[...] = walkers_ref[...].astype(F32)
    exponent = fields_ref[:, 0:1] * diag_ref[0:1, :]
    for g in range(1, vec_count):
        exponent = exponent + fields_ref[:, g : g + 1] * diag_ref[g : g + 1, :]
    for i, term in enumerate(terms(exponent, 2)):
        for c in range(chunks):
            parts[:, i * chunks + c, :] = term[:, c * LANES : (c + 1) * LANES]
    weight = F32(0.0)
    for slot in range(slots):
        t = target_ref[slot]
        alive = t < live
        weight = weight + jnp.where(alive, weights_ref[slot], F32(0.0))
        turn = lax.div(t, groups)
        at = jnp.where(alive, lax.rem(t, groups) * cap + lax.rem(turn, cap), groups * cap)
        blocks[at] = wide[:, slot, :]
        parts[slot, 2 * chunks : 2 * chunks + 1, :] = jnp.full((1, LANES), (turn + 1).astype(F32), F32)
        lines[at] = parts[slot]
    sums = terms(jnp.full((1, LANES), weight, F32), 3)
    for s, out in enumerate(outs):
        base = moved(me_ref[0], s, groups, 1) * cap
        out[:, 0:orbitals] = jnp.concatenate([blocks[base + k] for k in range(cap)], axis=0).astype(BF16)
        tail = [lines[base + k][0 : 2 * chunks + 1] for k in range(cap)]
        write_tail(out, orbitals, jnp.concatenate(tail + sums, axis=0))


def merge_kernel(order, keep, cap, orbitals, core_ref, when, *refs):
    ins, (same_ref, other_ref, same2_ref, other2_ref, weight_ref, pick_ref) = refs[: len(order)], refs[len(order) :]
    half = keep // 2
    rows = ins[0].shape[0] // cap
    slab = half * rows
    chunks = orbitals // LANES
    each = 2 * chunks + 1
    weight = jnp.zeros((1, LANES), F32)
    walker = [jnp.zeros((rows, orbitals), F32)] * keep
    line = [jnp.zeros((2 * chunks, LANES), F32)] * keep
    for s, ref in zip(order, ins):
        tail = read_tail(ref, orbitals, cap * each + 3)
        weight = weight + (tail[cap * each : cap * each + 1] + tail[cap * each + 1 : cap * each + 2] + tail[cap * each + 2 :])
        for k in range(cap):
            flag = tail[(k + 1) * each - 1 : (k + 1) * each]
            block = ref[k * rows : (k + 1) * rows, 0:orbitals].astype(F32)
            part = tail[k * each : (k + 1) * each - 1]
            for m in range(k, keep, cap):
                mine = jnp.where(flag == m + 1, F32(1.0), F32(0.0))
                pick_ref[s * keep + m : s * keep + m + 1, :] = mine
                walker[m] = jnp.where(wide_mask(mine, orbitals), block, walker[m])
                line[m] = jnp.where(mine > 0, part, line[m])
    weight_ref[...] = jnp.broadcast_to(weight, weight_ref.shape)
    first = core_ref[0] == 0
    for out, order in ((same_ref, (0, 1)), (other_ref, (1, 0))):
        picked = []
        for k in range(half):
            a, b = order[0] * half + k, order[1] * half + k
            picked.append(jnp.where(first, line[a], line[b]))
            block = jnp.where(first, walker[a], walker[b])
            for c in range(chunks):
                at = c * slab + k * rows
                out[at : at + rows, :] = block[:, c * LANES : (c + 1) * LANES].astype(BF16)
        tail = [p[i * chunks : (i + 1) * chunks] for i in range(2) for p in picked]
        out[chunks * slab :, :] = jnp.concatenate(tail, axis=0).astype(BF16)
    same2_ref[...] = same_ref[...]
    other2_ref[...] = other_ref[...]


def power(size):
    return size & (size - 1) == 0


def moved(me, s, size, sign):
    if power(size):
        return me ^ s if isinstance(me, int) else lax.bitwise_xor(me, jnp.int32(s))
    at = me + (s if sign > 0 else size - s)
    return at % size if isinstance(me, int) else lax.rem(at, size)


def hops(n):
    chips = n // 2
    far = list(range(chips // 2, chips)) + list(range(1, chips // 2))
    return [(0, 0)] + [(s, e) for s in far for e in range(2)] + [(0, 1)]


def after_kernel(source_ref, when_ref, out_ref):
    out_ref[...] = source_ref[...]


def arrivals(n):
    return hops(n)[:1] + hops(n)[:0:-1]


def leading(s, chips):
    top = 1 << (s.bit_length() - 1) if s else 0
    return top if power(chips) else s


def partner(blk, s, e, n, sign):
    chip = moved(lax.div(blk, 2), s, n // 2, sign)
    core = lax.rem(blk, 2)
    return 2 * chip + (core if e == 0 else 1 - core)


def fock_kernel(n, half, blk_ref, body_ref, own_ref, sib_ref, *refs):
    ins, outs = refs[:n], refs[n : 2 * n]
    prop, carried, coup, result = refs[2 * n :]
    vec_count, occupied, orbitals = own_ref.shape
    slab = outs[0].shape[0]
    rows = slab // half
    chunks = orbitals // LANES
    blk = blk_ref[0]
    exponent = jnp.zeros((2 * half * chunks, LANES), F32)
    for ref in ins:
        exponent = exponent + ref[chunks * slab :, :].astype(F32)
    growth = jnp.exp(exponent[0 : half * chunks] + exponent[half * chunks :])
    for ref, (s, e) in zip(ins, arrivals(n)):
        source = partner(blk, s, e, n, -1)
        for w in range(half):
            for c in range(chunks):
                piece = ref[c * slab + w * rows : c * slab + (w + 1) * rows, :].astype(F32)
                piece = piece * growth[w * chunks + c : w * chunks + c + 1]
                prop[w, source, :, c * LANES : (c + 1) * LANES] = piece.astype(prop.dtype)
    scaled = jnp.concatenate([prop[w, i] for w in range(half) for i in range(n)], axis=0).astype(BF16)
    carried[...] = jnp.dot(scaled, body_ref[...], preferred_element_type=F32).astype(BF16)
    batch = math.gcd(vec_count, 4)
    for c, ref in enumerate((own_ref, sib_ref)):
        for g in range(0, vec_count, batch):
            left = ref[g : g + batch].reshape(batch * occupied, orbitals)
            s = lax.dot_general(left, carried[...], (((1,), (1,)), ((), ())), preferred_element_type=F32).astype(BF16)
            for k in range(batch):
                at = (c * vec_count + g + k) * occupied
                for w in range(half):
                    coup[w * occupied : (w + 1) * occupied, at : at + occupied] = s[
                        k * occupied : (k + 1) * occupied, w * occupied : (w + 1) * occupied
                    ]
    tile = 256 if orbitals % 256 == 0 else orbitals
    depth = vec_count * occupied
    for t in range(0, orbitals, tile):
        total = jnp.dot(
            coup[:, :depth],
            own_ref[:, :, t : t + tile].reshape(depth, tile),
            preferred_element_type=F32,
        )
        total = total + jnp.dot(
            coup[:, depth:],
            sib_ref[:, :, t : t + tile].reshape(depth, tile),
            preferred_element_type=F32,
        )
        for w in range(half):
            for i in range(n):
                at = w * occupied + i * rows
                result[w, i, :, t : t + tile] = total[at : at + rows].astype(result.dtype)
    for out, (s, e) in zip(outs, hops(n)):
        to = partner(blk, s, e, n, 1)
        for w in range(half):
            out[w * rows : (w + 1) * rows, :] = result[w, to].astype(BF16)


def sum_kernel(n, keep, cap, groups, core_ref, pick_ref, *refs):
    ins, outs = refs[:n], refs[n:]
    slab, orbitals = ins[0].shape
    half = keep // 2
    rows = slab // half
    halves = []
    for e in range(2):
        same = [ref for ref, (_, other) in zip(ins, hops(n)) if other == e]
        total = same[0][...].astype(F32)
        for ref in same[1:]:
            total = total + ref[...].astype(F32)
        halves.append(total)
    first = core_ref[0] == 0
    whole = [jnp.where(first, halves[0], halves[1]), jnp.where(first, halves[1], halves[0])]
    walker = [whole[m // half][(m % half) * rows : (m % half + 1) * rows] for m in range(keep)]
    for s, out in enumerate(outs):
        source = s if power(groups) else (groups - s) % groups
        for k in range(cap):
            value = jnp.zeros((rows, orbitals), F32)
            for m in range(k, keep, cap):
                mine = pick_ref[source * keep + m : source * keep + m + 1, :]
                value = jnp.where(wide_mask(mine, orbitals), walker[m], value)
            out[k * rows : (k + 1) * rows, :] = value.astype(BF16)


def deal_kernel(order, keep, cap, me_ref, target_ref, weights_ref, total_ref, *refs):
    groups = len(order)
    ins, (out_any, blocks, wide, held, sems) = refs[:groups], refs[groups:]
    rows, slots, orbitals = wide.shape
    live = groups * keep
    for s, ref in zip(order, ins):
        base = moved(me_ref[0], s, groups, -1) * cap
        for k in range(cap):
            blocks[base + k] = ref[k * rows : (k + 1) * rows, :].astype(F32)
    blocks[groups * cap] = jnp.zeros((rows, orbitals), F32)
    places = []
    for slot in range(slots):
        t = target_ref[slot]
        alive = t < live
        at = jnp.where(alive, lax.rem(t, groups) * cap + lax.rem(lax.div(t, groups), cap), groups * cap)
        weight = jnp.where(alive, weights_ref[slot], F32(0.0))
        factor = jnp.full((1, LANES), weight * live, F32) / total_ref[0:1, :]
        places.append((at, factor[:, 0:1]))
    step = rows // sems.shape[0]
    copies = []
    for h in range(sems.shape[0]):
        band = slice(h * step, (h + 1) * step)
        for slot, (at, factor) in enumerate(places):
            wide[band, slot, :] = blocks[at, band, :] * factor
        held[band] = wide[band].astype(BF16)
        copies.append(pltpu.make_async_copy(held.at[band], out_any.at[band], sems.at[h]))
        copies[-1].start()
    for copy in copies:
        copy.wait()


def call(kernel, outs, scalars, held, arrays, scratch, name, flops=0, vmem=VMEM, place=pltpu.VMEM):
    smem = pl.BlockSpec(memory_space=pltpu.SMEM)
    full = pl.BlockSpec(memory_space=pltpu.VMEM)
    size = sum(x.size * x.dtype.itemsize for x in list(arrays) + list(outs))
    return pl.pallas_call(
        kernel,
        out_shape=outs,
        in_specs=[smem] * len(scalars) + [pl.BlockSpec(memory_space=pl.ANY)] * len(held) + [full] * len(arrays),
        out_specs=[pl.BlockSpec(memory_space=place)] * len(outs),
        scratch_shapes=scratch,
        compiler_params=pltpu.CompilerParams(vmem_limit_bytes=vmem * 2**20),
        cost_estimate=pl.CostEstimate(flops=flops, bytes_accessed=size, transcendentals=0),
        name=name,
    )(*scalars, *held, *arrays)


def body(walkers, one_body, fields, field_diag, chol, weights, target):
    rows, slots, orbitals = walkers.shape
    vec_count, occupied, _ = chol.shape
    n, groups = lax.axis_size("blk"), lax.axis_size("grp")
    keep = slots // 2
    half = keep // 2
    cap = -(-slots // groups)
    slab = half * rows
    shape = jax.ShapeDtypeStruct
    grp = lax.axis_index("grp").reshape(1)
    blk = lax.axis_index("blk").reshape(1)
    core = lax.rem(blk, 2)

    def to_list(x, s):
        return lax.ppermute(x, "grp", [(i, moved(i, s, groups, 1)) for i in range(groups)]) if s else x

    def to_block(x, s, e):
        if not s and not e:
            return x
        return lax.ppermute(x, "blk", [(i, 2 * moved(i // 2, s, n // 2, 1) + (i % 2 ^ e)) for i in range(n)])

    order = [0] + sorted(range(1, groups), key=lambda s: (s & 1, -s))
    chunks = orbitals // LANES
    sibling = to_block(chol, 0, 1)
    width = orbitals + tail_blocks(cap * (2 * chunks + 1) + 3, cap * rows) * LANES
    routed = call(
        functools.partial(route_kernel, keep, cap),
        [shape((cap * rows, width), BF16)] * groups,
        [grp],
        [target, weights, walkers, fields, field_diag],
        [],
        [
            pltpu.SMEM(target.shape, target.dtype),
            pltpu.SMEM(weights.shape, weights.dtype),
            pltpu.VMEM(walkers.shape, walkers.dtype),
            pltpu.VMEM(fields.shape, fields.dtype),
            pltpu.VMEM(field_diag.shape, field_diag.dtype),
            pltpu.VMEM((rows, slots, orbitals), F32),
            pltpu.VMEM((groups * cap + 1, rows, orbitals), F32),
            pltpu.VMEM((slots, 2 * chunks + 4, LANES), F32),
            pltpu.VMEM((groups * cap + 1, 2 * chunks + 4, LANES), F32),
            pltpu.SemaphoreType.DMA((5,)),
        ],
        "route",
        vmem=ROUTE_VMEM,
    )
    (kept,) = call(
        stage_kernel,
        [shape(routed[0].shape, BF16)],
        [],
        [routed[0]],
        [],
        [pltpu.SemaphoreType.DMA((1,))],
        "keep",
    )
    (own,) = call(
        stage_kernel,
        [shape(chol.shape, chol.dtype)],
        [],
        [chol, kept],
        [],
        [pltpu.SemaphoreType.DMA((1,))],
        "stage",
        vmem=STAGE_VMEM,
    )
    routed = [to_list(routed[s], s) if s else kept for s in order]
    payload = shape((chunks * slab + 2 * half * chunks, LANES), BF16)
    same, other, same2, other2, weight_sum, pick = call(
        functools.partial(merge_kernel, order, keep, cap, orbitals),
        [payload] * 4 + [shape((8, LANES), F32), shape((groups * keep, LANES), F32)],
        [core],
        [own],
        routed,
        [],
        "merge",
    )
    (held_body,) = call(
        stage_kernel,
        [shape(one_body.shape, one_body.dtype)],
        [],
        [one_body, weight_sum],
        [],
        [pltpu.SemaphoreType.DMA((1,))],
        "hold",
    )
    relayed = {leading(s, n // 2) for s, _ in hops(n) if leading(s, n // 2) != s}
    gathered = {}
    for s, e in hops(n):
        if s in relayed:
            gathered[s, e] = to_block(other if e else same, s, e)
    for s, e in hops(n):
        if leading(s, n // 2) == s and s not in relayed and (s, e) != (0, 1):
            gathered[s, e] = to_block(other2 if e else same2, s, e)
    for s, e in hops(n):
        top = leading(s, n // 2)
        if top != s:
            gathered[s, e] = to_block(gathered[top, e], s ^ top, 0)
    late = gathered.get((1, 1), same2)
    (last,) = call(after_kernel, [payload], [], [], [other2, late], [], "after")
    gathered[0, 1] = to_block(last, 0, 1)
    gathered = [gathered[hop] for hop in arrivals(n)]
    held = F32 if rows % 16 else BF16
    parts = call(
        functools.partial(fock_kernel, n, half),
        [shape((slab, orbitals), BF16)] * n,
        [blk],
        [],
        [held_body, own, sibling] + gathered,
        [
            pltpu.VMEM((half, n, rows, orbitals), held),
            pltpu.VMEM((half * occupied, orbitals), BF16),
            pltpu.VMEM((half * occupied, 2 * vec_count * occupied), BF16),
            pltpu.VMEM((half, n, rows, orbitals), held),
        ],
        "fock",
        flops=2 * n * slab * orbitals * (orbitals + 4 * vec_count * occupied),
    )
    backs = [to_block(x, s, e) for x, (s, e) in zip(parts, hops(n))]
    back = call(
        functools.partial(sum_kernel, n, keep, cap, groups),
        [shape((cap * rows, orbitals), BF16)] * groups,
        [core],
        [],
        [pick] + backs,
        [],
        "sum",
    )
    back = [to_list(back[s], s) for s in order]
    (out,) = call(
        functools.partial(deal_kernel, order, keep, cap),
        [shape(walkers.shape, BF16)],
        [grp, target, weights],
        [],
        [weight_sum] + back,
        [
            pltpu.VMEM((groups * cap + 1, rows, orbitals), F32),
            pltpu.VMEM(walkers.shape, F32),
            pltpu.VMEM(walkers.shape, BF16),
            pltpu.SemaphoreType.DMA((2,)),
        ],
        "deal",
        place=pl.ANY,
    )
    return out


def solution(mesh):
    in_specs = (
        P("blk", "grp", None),
        P(),
        P("grp", "blk"),
        P("blk", None),
        P("blk", None, None),
        P("grp"),
        P("grp"),
    )
    out_specs = P("blk", "grp", None)
    return jax.shard_map(body, mesh=mesh, in_specs=in_specs, out_specs=out_specs, check_vma=False)
```

```python
import functools
import math
import jax
import jax.numpy as jnp
from jax import lax
from jax.experimental import pallas as pl
from jax.experimental.pallas import tpu as pltpu
from jax.sharding import PartitionSpec as P

F32 = jnp.float32
BF16 = jnp.bfloat16
LANES = 128
VMEM = 24
ROUTE_VMEM = 56
STAGE_VMEM = 48


def terms(value, count):
    out = []
    for _ in range(count):
        term = value.astype(BF16).astype(F32)
        out.append(term)
        value = value - term
    return out


def tail_blocks(count, slab):
    return -(-count // slab)


def write_tail(out_ref, start, lines):
    slab = out_ref.shape[0]
    for b in range(tail_blocks(lines.shape[0], slab)):
        part = lines[b * slab : (b + 1) * slab]
        if part.shape[0] < slab:
            part = jnp.concatenate([part, jnp.zeros((slab - part.shape[0], LANES), F32)], axis=0)
        out_ref[:, start + b * LANES : start + (b + 1) * LANES] = part.astype(BF16)


def read_tail(ref, start, count):
    parts = [ref[:, c : c + LANES].astype(F32) for c in range(start, ref.shape[1], LANES)]
    whole = parts[0] if len(parts) == 1 else jnp.concatenate(parts, axis=0)
    return whole[0:count]


def wide_mask(line, width):
    return jnp.concatenate([line] * (width // LANES), axis=1) > 0


def stage_kernel(*refs):
    sems = refs[-1]
    count = sems.shape[0]
    copies = [pltpu.make_async_copy(refs[i], refs[i - count - 1], sems.at[i]) for i in range(count)]
    for copy in copies:
        copy.start()
    for copy in copies:
        copy.wait()


def route_kernel(keep, cap, me_ref, target_any, weights_any, walkers_any, fields_any, diag_any, *refs):
    *outs, target_ref, weights_ref, walkers_ref, fields_ref, diag_ref, wide, blocks, parts, lines, sems = refs
    pairs = (
        (walkers_any, walkers_ref),
        (target_any, target_ref),
        (weights_any, weights_ref),
        (fields_any, fields_ref),
        (diag_any, diag_ref),
    )
    copies = [pltpu.make_async_copy(a, b, sems.at[i]) for i, (a, b) in enumerate(pairs)]
    for copy in copies:
        copy.start()
    rows, slots, orbitals = walkers_ref.shape
    vec_count = fields_ref.shape[1]
    chunks = orbitals // LANES
    groups = len(outs)
    live = groups * keep
    blocks[...] = jnp.zeros(blocks.shape, F32)
    lines[...] = jnp.zeros(lines.shape, F32)
    for copy in copies:
        copy.wait()
    wide[...] = walkers_ref[...].astype(F32)
    exponent = fields_ref[:, 0:1] * diag_ref[0:1, :]
    for g in range(1, vec_count):
        exponent = exponent + fields_ref[:, g : g + 1] * diag_ref[g : g + 1, :]
    for i, term in enumerate(terms(exponent, 2)):
        for c in range(chunks):
            parts[:, i * chunks + c, :] = term[:, c * LANES : (c + 1) * LANES]
    weight = F32(0.0)
    for slot in range(slots):
        t = target_ref[slot]
        alive = t < live
        weight = weight + jnp.where(alive, weights_ref[slot], F32(0.0))
        turn = lax.div(t, groups)
        at = jnp.where(alive, lax.rem(t, groups) * cap + lax.rem(turn, cap), groups * cap)
        blocks[at] = wide[:, slot, :]
        parts[slot, 2 * chunks : 2 * chunks + 1, :] = jnp.full((1, LANES), (turn + 1).astype(F32), F32)
        lines[at] = parts[slot]
    sums = terms(jnp.full((1, LANES), weight, F32), 3)
    for s, out in enumerate(outs):
        base = moved(me_ref[0], s, groups, 1) * cap
        out[:, 0:orbitals] = jnp.concatenate([blocks[base + k] for k in range(cap)], axis=0).astype(BF16)
        tail = [lines[base + k][0 : 2 * chunks + 1] for k in range(cap)]
        write_tail(out, orbitals, jnp.concatenate(tail + sums, axis=0))


def merge_kernel(order, keep, cap, orbitals, core_ref, when, *refs):
    ins, (same_ref, other_ref, same2_ref, other2_ref, weight_ref, pick_ref) = refs[: len(order)], refs[len(order) :]
    half = keep // 2
    rows = ins[0].shape[0] // cap
    slab = half * rows
    chunks = orbitals // LANES
    each = 2 * chunks + 1
    weight = jnp.zeros((1, LANES), F32)
    walker = [jnp.zeros((rows, orbitals), F32)] * keep
    line = [jnp.zeros((2 * chunks, LANES), F32)] * keep
    for s, ref in zip(order, ins):
        tail = read_tail(ref, orbitals, cap * each + 3)
        weight = weight + (tail[cap * each : cap * each + 1] + tail[cap * each + 1 : cap * each + 2] + tail[cap * each + 2 :])
        for k in range(cap):
            flag = tail[(k + 1) * each - 1 : (k + 1) * each]
            block = ref[k * rows : (k + 1) * rows, 0:orbitals].astype(F32)
            part = tail[k * each : (k + 1) * each - 1]
            for m in range(k, keep, cap):
                mine = jnp.where(flag == m + 1, F32(1.0), F32(0.0))
                pick_ref[s * keep + m : s * keep + m + 1, :] = mine
                walker[m] = jnp.where(wide_mask(mine, orbitals), block, walker[m])
                line[m] = jnp.where(mine > 0, part, line[m])
    weight_ref[...] = jnp.broadcast_to(weight, weight_ref.shape)
    first = core_ref[0] == 0
    for out, order in ((same_ref, (0, 1)), (other_ref, (1, 0))):
        picked = []
        for k in range(half):
            a, b = order[0] * half + k, order[1] * half + k
            picked.append(jnp.where(first, line[a], line[b]))
            block = jnp.where(first, walker[a], walker[b])
            for c in range(chunks):
                at = c * slab + k * rows
                out[at : at + rows, :] = block[:, c * LANES : (c + 1) * LANES].astype(BF16)
        tail = [p[i * chunks : (i + 1) * chunks] for i in range(2) for p in picked]
        out[chunks * slab :, :] = jnp.concatenate(tail, axis=0).astype(BF16)
    same2_ref[...] = same_ref[...]
    other2_ref[...] = other_ref[...]


def power(size):
    return size & (size - 1) == 0


def moved(me, s, size, sign):
    if power(size):
        return me ^ s if isinstance(me, int) else lax.bitwise_xor(me, jnp.int32(s))
    at = me + (s if sign > 0 else size - s)
    return at % size if isinstance(me, int) else lax.rem(at, size)


def hops(n):
    chips = n // 2
    far = list(range(chips // 2, chips)) + list(range(1, chips // 2))
    return [(0, 0)] + [(s, e) for s in far for e in range(2)] + [(0, 1)]


def after_kernel(source_ref, when_ref, out_ref):
    out_ref[...] = source_ref[...]


def arrivals(n):
    return hops(n)[:1] + hops(n)[:0:-1]


def leading(s, e, chips):
    return 1 << (s.bit_length() - 1) if s and e and power(chips) else s


def returns(n):
    return [(s, e) for s, e in hops(n) if leading(s, e, n // 2) == s]


def add_kernel(count, *refs):
    outs = refs[len(refs) - 1 - count :]
    ins = refs[: len(refs) - 1 - count]
    total = ins[count][...].astype(F32)
    for ref in ins[count + 1 :]:
        total = total + ref[...].astype(F32)
    outs[0][...] = total.astype(BF16)
    for i in range(count):
        outs[1 + i][...] = ins[i][...]


def partner(blk, s, e, n, sign):
    chip = moved(lax.div(blk, 2), s, n // 2, sign)
    core = lax.rem(blk, 2)
    return 2 * chip + (core if e == 0 else 1 - core)


def fock_kernel(n, half, blk_ref, body_ref, own_ref, sib_ref, *refs):
    ins, outs = refs[:n], refs[n : 2 * n]
    prop, carried, coup, result = refs[2 * n :]
    vec_count, occupied, orbitals = own_ref.shape
    slab = outs[0].shape[0]
    rows = slab // half
    chunks = orbitals // LANES
    blk = blk_ref[0]
    exponent = jnp.zeros((2 * half * chunks, LANES), F32)
    for ref in ins:
        exponent = exponent + ref[chunks * slab :, :].astype(F32)
    growth = jnp.exp(exponent[0 : half * chunks] + exponent[half * chunks :])
    for ref, (s, e) in zip(ins, arrivals(n)):
        source = partner(blk, s, e, n, -1)
        for w in range(half):
            for c in range(chunks):
                piece = ref[c * slab + w * rows : c * slab + (w + 1) * rows, :].astype(F32)
                piece = piece * growth[w * chunks + c : w * chunks + c + 1]
                prop[w, source, :, c * LANES : (c + 1) * LANES] = piece.astype(prop.dtype)
    scaled = jnp.concatenate([prop[w, i] for w in range(half) for i in range(n)], axis=0).astype(BF16)
    carried[...] = jnp.dot(scaled, body_ref[...], preferred_element_type=F32).astype(BF16)
    batch = math.gcd(vec_count, 4)
    for c, ref in enumerate((own_ref, sib_ref)):
        for g in range(0, vec_count, batch):
            left = ref[g : g + batch].reshape(batch * occupied, orbitals)
            s = lax.dot_general(left, carried[...], (((1,), (1,)), ((), ())), preferred_element_type=F32).astype(BF16)
            for k in range(batch):
                at = (c * vec_count + g + k) * occupied
                for w in range(half):
                    coup[w * occupied : (w + 1) * occupied, at : at + occupied] = s[
                        k * occupied : (k + 1) * occupied, w * occupied : (w + 1) * occupied
                    ]
    tile = 256 if orbitals % 256 == 0 else orbitals
    depth = vec_count * occupied
    for t in range(0, orbitals, tile):
        total = jnp.dot(
            coup[:, :depth],
            own_ref[:, :, t : t + tile].reshape(depth, tile),
            preferred_element_type=F32,
        )
        total = total + jnp.dot(
            coup[:, depth:],
            sib_ref[:, :, t : t + tile].reshape(depth, tile),
            preferred_element_type=F32,
        )
        for w in range(half):
            for i in range(n):
                at = w * occupied + i * rows
                result[w, i, :, t : t + tile] = total[at : at + rows].astype(result.dtype)
    for out, (s, e) in zip(outs, hops(n)):
        to = partner(blk, s, e, n, 1)
        for w in range(half):
            out[w * rows : (w + 1) * rows, :] = result[w, to].astype(BF16)


def sum_kernel(n, keep, cap, groups, core_ref, pick_ref, *refs):
    known = returns(n)
    ins, outs = refs[: len(known)], refs[len(known) :]
    slab, orbitals = ins[0].shape
    half = keep // 2
    rows = slab // half
    halves = []
    for e in range(2):
        same = [ref for ref, (_, other) in zip(ins, known) if other == e]
        total = same[0][...].astype(F32)
        for ref in same[1:]:
            total = total + ref[...].astype(F32)
        halves.append(total)
    first = core_ref[0] == 0
    whole = [jnp.where(first, halves[0], halves[1]), jnp.where(first, halves[1], halves[0])]
    walker = [whole[m // half][(m % half) * rows : (m % half + 1) * rows] for m in range(keep)]
    for s, out in enumerate(outs):
        source = s if power(groups) else (groups - s) % groups
        for k in range(cap):
            value = jnp.zeros((rows, orbitals), F32)
            for m in range(k, keep, cap):
                mine = pick_ref[source * keep + m : source * keep + m + 1, :]
                value = jnp.where(wide_mask(mine, orbitals), walker[m], value)
            out[k * rows : (k + 1) * rows, :] = value.astype(BF16)


def deal_kernel(order, keep, cap, me_ref, target_ref, weights_ref, total_ref, *refs):
    groups = len(order)
    ins, (out_any, blocks, wide, held, sems) = refs[:groups], refs[groups:]
    rows, slots, orbitals = wide.shape
    live = groups * keep
    for s, ref in zip(order, ins):
        base = moved(me_ref[0], s, groups, -1) * cap
        for k in range(cap):
            blocks[base + k] = ref[k * rows : (k + 1) * rows, :].astype(F32)
    blocks[groups * cap] = jnp.zeros((rows, orbitals), F32)
    places = []
    for slot in range(slots):
        t = target_ref[slot]
        alive = t < live
        at = jnp.where(alive, lax.rem(t, groups) * cap + lax.rem(lax.div(t, groups), cap), groups * cap)
        weight = jnp.where(alive, weights_ref[slot], F32(0.0))
        factor = jnp.full((1, LANES), weight * live, F32) / total_ref[0:1, :]
        places.append((at, factor[:, 0:1]))
    step = rows // sems.shape[0]
    copies = []
    for h in range(sems.shape[0]):
        band = slice(h * step, (h + 1) * step)
        for slot, (at, factor) in enumerate(places):
            wide[band, slot, :] = blocks[at, band, :] * factor
        held[band] = wide[band].astype(BF16)
        copies.append(pltpu.make_async_copy(held.at[band], out_any.at[band], sems.at[h]))
        copies[-1].start()
    for copy in copies:
        copy.wait()


def call(kernel, outs, scalars, held, arrays, scratch, name, flops=0, vmem=VMEM, place=pltpu.VMEM):
    smem = pl.BlockSpec(memory_space=pltpu.SMEM)
    full = pl.BlockSpec(memory_space=pltpu.VMEM)
    size = sum(x.size * x.dtype.itemsize for x in list(arrays) + list(outs))
    return pl.pallas_call(
        kernel,
        out_shape=outs,
        in_specs=[smem] * len(scalars) + [pl.BlockSpec(memory_space=pl.ANY)] * len(held) + [full] * len(arrays),
        out_specs=[pl.BlockSpec(memory_space=place)] * len(outs),
        scratch_shapes=scratch,
        compiler_params=pltpu.CompilerParams(vmem_limit_bytes=vmem * 2**20),
        cost_estimate=pl.CostEstimate(flops=flops, bytes_accessed=size, transcendentals=0),
        name=name,
    )(*scalars, *held, *arrays)


def body(walkers, one_body, fields, field_diag, chol, weights, target):
    rows, slots, orbitals = walkers.shape
    vec_count, occupied, _ = chol.shape
    n, groups = lax.axis_size("blk"), lax.axis_size("grp")
    keep = slots // 2
    half = keep // 2
    cap = -(-slots // groups)
    slab = half * rows
    shape = jax.ShapeDtypeStruct
    grp = lax.axis_index("grp").reshape(1)
    blk = lax.axis_index("blk").reshape(1)
    core = lax.rem(blk, 2)

    def to_list(x, s):
        return lax.ppermute(x, "grp", [(i, moved(i, s, groups, 1)) for i in range(groups)]) if s else x

    def to_block(x, s, e):
        if not s and not e:
            return x
        return lax.ppermute(x, "blk", [(i, 2 * moved(i // 2, s, n // 2, 1) + (i % 2 ^ e)) for i in range(n)])

    order = [0] + sorted(range(1, groups), key=lambda s: (s & 1, -s))
    chunks = orbitals // LANES
    sibling = to_block(chol, 0, 1)
    width = orbitals + tail_blocks(cap * (2 * chunks + 1) + 3, cap * rows) * LANES
    routed = call(
        functools.partial(route_kernel, keep, cap),
        [shape((cap * rows, width), BF16)] * groups,
        [grp],
        [target, weights, walkers, fields, field_diag],
        [],
        [
            pltpu.SMEM(target.shape, target.dtype),
            pltpu.SMEM(weights.shape, weights.dtype),
            pltpu.VMEM(walkers.shape, walkers.dtype),
            pltpu.VMEM(fields.shape, fields.dtype),
            pltpu.VMEM(field_diag.shape, field_diag.dtype),
            pltpu.VMEM((rows, slots, orbitals), F32),
            pltpu.VMEM((groups * cap + 1, rows, orbitals), F32),
            pltpu.VMEM((slots, 2 * chunks + 4, LANES), F32),
            pltpu.VMEM((groups * cap + 1, 2 * chunks + 4, LANES), F32),
            pltpu.SemaphoreType.DMA((5,)),
        ],
        "route",
        vmem=ROUTE_VMEM,
    )
    (kept,) = call(
        stage_kernel,
        [shape(routed[0].shape, BF16)],
        [],
        [routed[0]],
        [],
        [pltpu.SemaphoreType.DMA((1,))],
        "keep",
    )
    (own,) = call(
        stage_kernel,
        [shape(chol.shape, chol.dtype)],
        [],
        [chol, kept],
        [],
        [pltpu.SemaphoreType.DMA((1,))],
        "stage",
        vmem=STAGE_VMEM,
    )
    routed = [to_list(routed[s], s) if s else kept for s in order]
    payload = shape((chunks * slab + 2 * half * chunks, LANES), BF16)
    same, other, same2, other2, weight_sum, pick = call(
        functools.partial(merge_kernel, order, keep, cap, orbitals),
        [payload] * 4 + [shape((8, LANES), F32), shape((groups * keep, LANES), F32)],
        [core],
        [own],
        routed,
        [],
        "merge",
    )
    (held_body,) = call(
        stage_kernel,
        [shape(one_body.shape, one_body.dtype)],
        [],
        [one_body, weight_sum],
        [],
        [pltpu.SemaphoreType.DMA((1,))],
        "hold",
    )
    chips = n // 2
    gathered = {}
    for s, e in [hop for hop in hops(n) if hop[1]] + [hop for hop in hops(n) if not hop[1]]:
        if leading(s, e, chips) == s and 2 * s >= chips:
            gathered[s, e] = to_block(other if e else same, s, e)
    for s, e in hops(n):
        if leading(s, e, chips) == s and 2 * s < chips and (s, e) != (0, 1):
            gathered[s, e] = to_block(other2 if e else same2, s, e)
    for s, e in hops(n):
        top = leading(s, e, chips)
        if top != s:
            gathered[s, e] = to_block(gathered[top, e], s ^ top, 0)
    (last,) = call(after_kernel, [payload], [], [], [other2, gathered.get((chips // 2, 0), same2)], [], "after")
    gathered[0, 1] = to_block(last, 0, 1)
    gathered = [gathered[hop] for hop in arrivals(n)]
    held = F32 if rows % 16 else BF16
    parts = call(
        functools.partial(fock_kernel, n, half),
        [shape((slab, orbitals), BF16)] * n,
        [blk],
        [],
        [held_body, own, sibling] + gathered,
        [
            pltpu.VMEM((half, n, rows, orbitals), held),
            pltpu.VMEM((half * occupied, orbitals), BF16),
            pltpu.VMEM((half * occupied, 2 * vec_count * occupied), BF16),
            pltpu.VMEM((half, n, rows, orbitals), held),
        ],
        "fock",
        flops=2 * n * slab * orbitals * (orbitals + 4 * vec_count * occupied),
    )
    parts = dict(zip(hops(n), parts))
    for s, e in returns(n):
        via = [hop for hop in hops(n) if hop[1] == e and hop[0] != s and leading(*hop, chips) == s]
        if via:
            later = [hop for hop in returns(n) if hop[0] < s and hop != (0, 0) and (hop[1] == e or 2 * hop[0] < chips)]
            out = call(
                functools.partial(add_kernel, len(later)),
                [shape((slab, orbitals), BF16)] * (1 + len(later)),
                [],
                [],
                [parts[hop] for hop in later] + [parts[s, e]] + [to_block(parts[hop], hop[0] ^ s, 0) for hop in via],
                [],
                "add",
            )
            parts.update(zip([(s, e)] + later, out))
    backs = [to_block(parts[hop], *hop) for hop in returns(n)]
    back = call(
        functools.partial(sum_kernel, n, keep, cap, groups),
        [shape((cap * rows, orbitals), BF16)] * groups,
        [core],
        [],
        [pick] + backs,
        [],
        "sum",
    )
    back = [to_list(back[s], s) for s in order]
    (out,) = call(
        functools.partial(deal_kernel, order, keep, cap),
        [shape(walkers.shape, BF16)],
        [grp, target, weights],
        [],
        [weight_sum] + back,
        [
            pltpu.VMEM((groups * cap + 1, rows, orbitals), F32),
            pltpu.VMEM(walkers.shape, F32),
            pltpu.VMEM(walkers.shape, BF16),
            pltpu.SemaphoreType.DMA((2,)),
        ],
        "deal",
        place=pl.ANY,
    )
    return out


def solution(mesh):
    in_specs = (
        P("blk", "grp", None),
        P(),
        P("grp", "blk"),
        P("blk", None),
        P("blk", None, None),
        P("grp"),
        P("grp"),
    )
    out_specs = P("blk", "grp", None)
    return jax.shard_map(body, mesh=mesh, in_specs=in_specs, out_specs=out_specs, check_vma=False)
```

```python
import functools
import math
import jax
import jax.numpy as jnp
from jax import lax
from jax.experimental import pallas as pl
from jax.experimental.pallas import tpu as pltpu
from jax.sharding import PartitionSpec as P

F32 = jnp.float32
BF16 = jnp.bfloat16
LANES = 128
VMEM = 24
ROUTE_VMEM = 56
STAGE_VMEM = 48


def terms(value, count):
    out = []
    for _ in range(count):
        term = value.astype(BF16).astype(F32)
        out.append(term)
        value = value - term
    return out


def tail_blocks(count, slab):
    return -(-count // slab)


def write_tail(out_ref, start, lines):
    slab = out_ref.shape[0]
    for b in range(tail_blocks(lines.shape[0], slab)):
        part = lines[b * slab : (b + 1) * slab]
        if part.shape[0] < slab:
            part = jnp.concatenate([part, jnp.zeros((slab - part.shape[0], LANES), F32)], axis=0)
        out_ref[:, start + b * LANES : start + (b + 1) * LANES] = part.astype(BF16)


def read_tail(ref, start, count):
    parts = [ref[:, c : c + LANES].astype(F32) for c in range(start, ref.shape[1], LANES)]
    whole = parts[0] if len(parts) == 1 else jnp.concatenate(parts, axis=0)
    return whole[0:count]


def wide_mask(line, width):
    return jnp.concatenate([line] * (width // LANES), axis=1) > 0


def stage_kernel(*refs):
    sems = refs[-1]
    count = sems.shape[0]
    copies = [pltpu.make_async_copy(refs[i], refs[i - count - 1], sems.at[i]) for i in range(count)]
    for copy in copies:
        copy.start()
    for copy in copies:
        copy.wait()


def route_kernel(keep, cap, me_ref, target_any, weights_any, walkers_any, fields_any, diag_any, *refs):
    *outs, target_ref, weights_ref, walkers_ref, fields_ref, diag_ref, wide, blocks, parts, lines, sems = refs
    pairs = (
        (walkers_any, walkers_ref),
        (target_any, target_ref),
        (weights_any, weights_ref),
        (fields_any, fields_ref),
        (diag_any, diag_ref),
    )
    copies = [pltpu.make_async_copy(a, b, sems.at[i]) for i, (a, b) in enumerate(pairs)]
    for copy in copies:
        copy.start()
    rows, slots, orbitals = walkers_ref.shape
    vec_count = fields_ref.shape[1]
    chunks = orbitals // LANES
    groups = len(outs)
    live = groups * keep
    blocks[...] = jnp.zeros(blocks.shape, F32)
    lines[...] = jnp.zeros(lines.shape, F32)
    for copy in copies:
        copy.wait()
    wide[...] = walkers_ref[...].astype(F32)
    exponent = fields_ref[:, 0:1] * diag_ref[0:1, :]
    for g in range(1, vec_count):
        exponent = exponent + fields_ref[:, g : g + 1] * diag_ref[g : g + 1, :]
    for i, term in enumerate(terms(exponent, 2)):
        for c in range(chunks):
            parts[:, i * chunks + c, :] = term[:, c * LANES : (c + 1) * LANES]
    weight = F32(0.0)
    for slot in range(slots):
        t = target_ref[slot]
        alive = t < live
        weight = weight + jnp.where(alive, weights_ref[slot], F32(0.0))
        turn = lax.div(t, groups)
        at = jnp.where(alive, lax.rem(t, groups) * cap + lax.rem(turn, cap), groups * cap)
        blocks[at] = wide[:, slot, :]
        parts[slot, 2 * chunks : 2 * chunks + 1, :] = jnp.full((1, LANES), (turn + 1).astype(F32), F32)
        lines[at] = parts[slot]
    sums = terms(jnp.full((1, LANES), weight, F32), 3)
    for s, out in enumerate(outs):
        base = moved(me_ref[0], s, groups, 1) * cap
        out[:, 0:orbitals] = jnp.concatenate([blocks[base + k] for k in range(cap)], axis=0).astype(BF16)
        tail = [lines[base + k][0 : 2 * chunks + 1] for k in range(cap)]
        write_tail(out, orbitals, jnp.concatenate(tail + sums, axis=0))


def merge_kernel(order, keep, cap, orbitals, core_ref, when, *refs):
    ins, (same_ref, other_ref, same2_ref, other2_ref, weight_ref, pick_ref) = refs[: len(order)], refs[len(order) :]
    half = keep // 2
    rows = ins[0].shape[0] // cap
    slab = half * rows
    chunks = orbitals // LANES
    each = 2 * chunks + 1
    weight = jnp.zeros((1, LANES), F32)
    walker = [jnp.zeros((rows, orbitals), F32)] * keep
    line = [jnp.zeros((2 * chunks, LANES), F32)] * keep
    for s, ref in zip(order, ins):
        tail = read_tail(ref, orbitals, cap * each + 3)
        weight = weight + (tail[cap * each : cap * each + 1] + tail[cap * each + 1 : cap * each + 2] + tail[cap * each + 2 :])
        for k in range(cap):
            flag = tail[(k + 1) * each - 1 : (k + 1) * each]
            block = ref[k * rows : (k + 1) * rows, 0:orbitals].astype(F32)
            part = tail[k * each : (k + 1) * each - 1]
            for m in range(k, keep, cap):
                mine = jnp.where(flag == m + 1, F32(1.0), F32(0.0))
                pick_ref[s * keep + m : s * keep + m + 1, :] = mine
                walker[m] = jnp.where(wide_mask(mine, orbitals), block, walker[m])
                line[m] = jnp.where(mine > 0, part, line[m])
    weight_ref[...] = jnp.broadcast_to(weight, weight_ref.shape)
    first = core_ref[0] == 0
    for out, order in ((same_ref, (0, 1)), (other_ref, (1, 0))):
        picked = []
        for k in range(half):
            a, b = order[0] * half + k, order[1] * half + k
            picked.append(jnp.where(first, line[a], line[b]))
            block = jnp.where(first, walker[a], walker[b])
            for c in range(chunks):
                at = c * slab + k * rows
                out[at : at + rows, :] = block[:, c * LANES : (c + 1) * LANES].astype(BF16)
        tail = [p[i * chunks : (i + 1) * chunks] for i in range(2) for p in picked]
        out[chunks * slab :, :] = jnp.concatenate(tail, axis=0).astype(BF16)
    same2_ref[...] = same_ref[...]
    other2_ref[...] = other_ref[...]


def power(size):
    return size & (size - 1) == 0


def moved(me, s, size, sign):
    if power(size):
        return me ^ s if isinstance(me, int) else lax.bitwise_xor(me, jnp.int32(s))
    at = me + (s if sign > 0 else size - s)
    return at % size if isinstance(me, int) else lax.rem(at, size)


def hops(n):
    chips = n // 2
    far = list(range(chips // 2, chips)) + list(range(1, chips // 2))
    return [(0, 0)] + [(s, e) for s in far for e in range(2)] + [(0, 1)]


def after_kernel(source_ref, when_ref, out_ref):
    out_ref[...] = source_ref[...]


def arrivals(n):
    return hops(n)


def leading(s, e, chips):
    return 1 << (s.bit_length() - 1) if s and e and power(chips) else s


def returns(n):
    return [(s, e) for s, e in hops(n) if leading(s, e, n // 2) == s]


def add_kernel(count, *refs):
    outs = refs[len(refs) - 1 - count :]
    ins = refs[: len(refs) - 1 - count]
    total = ins[count][...].astype(F32)
    for ref in ins[count + 1 :]:
        total = total + ref[...].astype(F32)
    outs[0][...] = total.astype(BF16)
    for i in range(count):
        outs[1 + i][...] = ins[i][...]


def partner(blk, s, e, n, sign):
    chip = moved(lax.div(blk, 2), s, n // 2, sign)
    core = lax.rem(blk, 2)
    return 2 * chip + (core if e == 0 else 1 - core)


def fock_kernel(n, half, blk_ref, body_ref, own_ref, sib_ref, *refs):
    ins, outs = refs[:n], refs[n : 2 * n]
    prop, carried, coup, result = refs[2 * n :]
    vec_count, occupied, orbitals = own_ref.shape
    slab = outs[0].shape[0]
    rows = slab // half
    chunks = orbitals // LANES
    blk = blk_ref[0]
    exponent = jnp.zeros((2 * half * chunks, LANES), F32)
    for ref in ins:
        exponent = exponent + ref[chunks * slab :, :].astype(F32)
    growth = jnp.exp(exponent[0 : half * chunks] + exponent[half * chunks :])
    for ref, (s, e) in zip(ins, arrivals(n)):
        source = partner(blk, s, e, n, -1)
        for w in range(half):
            for c in range(chunks):
                piece = ref[c * slab + w * rows : c * slab + (w + 1) * rows, :].astype(F32)
                piece = piece * growth[w * chunks + c : w * chunks + c + 1]
                prop[w, source, :, c * LANES : (c + 1) * LANES] = piece.astype(prop.dtype)
    scaled = jnp.concatenate([prop[w, i] for w in range(half) for i in range(n)], axis=0).astype(BF16)
    carried[...] = jnp.dot(scaled, body_ref[...], preferred_element_type=F32).astype(BF16)
    batch = math.gcd(vec_count, 4)
    for c, ref in enumerate((own_ref, sib_ref)):
        for g in range(0, vec_count, batch):
            left = ref[g : g + batch].reshape(batch * occupied, orbitals)
            s = lax.dot_general(left, carried[...], (((1,), (1,)), ((), ())), preferred_element_type=F32).astype(BF16)
            for k in range(batch):
                at = (c * vec_count + g + k) * occupied
                for w in range(half):
                    coup[w * occupied : (w + 1) * occupied, at : at + occupied] = s[
                        k * occupied : (k + 1) * occupied, w * occupied : (w + 1) * occupied
                    ]
    tile = 256 if orbitals % 256 == 0 else orbitals
    depth = vec_count * occupied
    for t in range(0, orbitals, tile):
        total = jnp.dot(
            coup[:, :depth],
            own_ref[:, :, t : t + tile].reshape(depth, tile),
            preferred_element_type=F32,
        )
        total = total + jnp.dot(
            coup[:, depth:],
            sib_ref[:, :, t : t + tile].reshape(depth, tile),
            preferred_element_type=F32,
        )
        for w in range(half):
            for i in range(n):
                at = w * occupied + i * rows
                result[w, i, :, t : t + tile] = total[at : at + rows].astype(result.dtype)
    for out, (s, e) in zip(outs, hops(n)):
        to = partner(blk, s, e, n, 1)
        for w in range(half):
            out[w * rows : (w + 1) * rows, :] = result[w, to].astype(BF16)


def sum_kernel(n, keep, cap, groups, core_ref, pick_ref, *refs):
    known = returns(n)
    ins, outs = refs[: len(known)], refs[len(known) :]
    slab, orbitals = ins[0].shape
    half = keep // 2
    rows = slab // half
    halves = []
    for e in range(2):
        same = [ref for ref, (_, other) in zip(ins, known) if other == e]
        total = same[0][...].astype(F32)
        for ref in same[1:]:
            total = total + ref[...].astype(F32)
        halves.append(total)
    first = core_ref[0] == 0
    whole = [jnp.where(first, halves[0], halves[1]), jnp.where(first, halves[1], halves[0])]
    walker = [whole[m // half][(m % half) * rows : (m % half + 1) * rows] for m in range(keep)]
    for s, out in enumerate(outs):
        source = s if power(groups) else (groups - s) % groups
        for k in range(cap):
            value = jnp.zeros((rows, orbitals), F32)
            for m in range(k, keep, cap):
                mine = pick_ref[source * keep + m : source * keep + m + 1, :]
                value = jnp.where(wide_mask(mine, orbitals), walker[m], value)
            out[k * rows : (k + 1) * rows, :] = value.astype(BF16)


def deal_kernel(order, keep, cap, me_ref, target_ref, weights_ref, total_ref, *refs):
    groups = len(order)
    ins, (out_any, blocks, wide, held, sems) = refs[:groups], refs[groups:]
    rows, slots, orbitals = wide.shape
    live = groups * keep
    for s, ref in zip(order, ins):
        base = moved(me_ref[0], s, groups, -1) * cap
        for k in range(cap):
            blocks[base + k] = ref[k * rows : (k + 1) * rows, :].astype(F32)
    blocks[groups * cap] = jnp.zeros((rows, orbitals), F32)
    places = []
    for slot in range(slots):
        t = target_ref[slot]
        alive = t < live
        at = jnp.where(alive, lax.rem(t, groups) * cap + lax.rem(lax.div(t, groups), cap), groups * cap)
        weight = jnp.where(alive, weights_ref[slot], F32(0.0))
        factor = jnp.full((1, LANES), weight * live, F32) / total_ref[0:1, :]
        places.append((at, factor[:, 0:1]))
    step = rows // sems.shape[0]
    copies = []
    for h in range(sems.shape[0]):
        band = slice(h * step, (h + 1) * step)
        for slot, (at, factor) in enumerate(places):
            wide[band, slot, :] = blocks[at, band, :] * factor
        held[band] = wide[band].astype(BF16)
        copies.append(pltpu.make_async_copy(held.at[band], out_any.at[band], sems.at[h]))
        copies[-1].start()
    for copy in copies:
        copy.wait()


def call(kernel, outs, scalars, held, arrays, scratch, name, flops=0, vmem=VMEM, place=pltpu.VMEM):
    smem = pl.BlockSpec(memory_space=pltpu.SMEM)
    full = pl.BlockSpec(memory_space=pltpu.VMEM)
    size = sum(x.size * x.dtype.itemsize for x in list(arrays) + list(outs))
    return pl.pallas_call(
        kernel,
        out_shape=outs,
        in_specs=[smem] * len(scalars) + [pl.BlockSpec(memory_space=pl.ANY)] * len(held) + [full] * len(arrays),
        out_specs=[pl.BlockSpec(memory_space=place)] * len(outs),
        scratch_shapes=scratch,
        compiler_params=pltpu.CompilerParams(vmem_limit_bytes=vmem * 2**20),
        cost_estimate=pl.CostEstimate(flops=flops, bytes_accessed=size, transcendentals=0),
        name=name,
    )(*scalars, *held, *arrays)


def body(walkers, one_body, fields, field_diag, chol, weights, target):
    rows, slots, orbitals = walkers.shape
    vec_count, occupied, _ = chol.shape
    n, groups = lax.axis_size("blk"), lax.axis_size("grp")
    keep = slots // 2
    half = keep // 2
    cap = -(-slots // groups)
    slab = half * rows
    shape = jax.ShapeDtypeStruct
    grp = lax.axis_index("grp").reshape(1)
    blk = lax.axis_index("blk").reshape(1)
    core = lax.rem(blk, 2)

    def to_list(x, s):
        return lax.ppermute(x, "grp", [(i, moved(i, s, groups, 1)) for i in range(groups)]) if s else x

    def to_block(x, s, e):
        if not s and not e:
            return x
        return lax.ppermute(x, "blk", [(i, 2 * moved(i // 2, s, n // 2, 1) + (i % 2 ^ e)) for i in range(n)])

    order = [0] + sorted(range(1, groups), key=lambda s: (s & 1, -s))
    chunks = orbitals // LANES
    sibling = to_block(chol, 0, 1)
    width = orbitals + tail_blocks(cap * (2 * chunks + 1) + 3, cap * rows) * LANES
    routed = call(
        functools.partial(route_kernel, keep, cap),
        [shape((cap * rows, width), BF16)] * groups,
        [grp],
        [target, weights, walkers, fields, field_diag],
        [],
        [
            pltpu.SMEM(target.shape, target.dtype),
            pltpu.SMEM(weights.shape, weights.dtype),
            pltpu.VMEM(walkers.shape, walkers.dtype),
            pltpu.VMEM(fields.shape, fields.dtype),
            pltpu.VMEM(field_diag.shape, field_diag.dtype),
            pltpu.VMEM((rows, slots, orbitals), F32),
            pltpu.VMEM((groups * cap + 1, rows, orbitals), F32),
            pltpu.VMEM((slots, 2 * chunks + 4, LANES), F32),
            pltpu.VMEM((groups * cap + 1, 2 * chunks + 4, LANES), F32),
            pltpu.SemaphoreType.DMA((5,)),
        ],
        "route",
        vmem=ROUTE_VMEM,
    )
    (kept,) = call(
        stage_kernel,
        [shape(routed[0].shape, BF16)],
        [],
        [routed[0]],
        [],
        [pltpu.SemaphoreType.DMA((1,))],
        "keep",
    )
    (own,) = call(
        stage_kernel,
        [shape(chol.shape, chol.dtype)],
        [],
        [chol, kept],
        [],
        [pltpu.SemaphoreType.DMA((1,))],
        "stage",
        vmem=STAGE_VMEM,
    )
    routed = [to_list(routed[s], s) if s else kept for s in order]
    payload = shape((chunks * slab + 2 * half * chunks, LANES), BF16)
    same, other, same2, other2, weight_sum, pick = call(
        functools.partial(merge_kernel, order, keep, cap, orbitals),
        [payload] * 4 + [shape((8, LANES), F32), shape((groups * keep, LANES), F32)],
        [core],
        [own],
        routed,
        [],
        "merge",
    )
    (held_body,) = call(
        stage_kernel,
        [shape(one_body.shape, one_body.dtype)],
        [],
        [one_body, weight_sum],
        [],
        [pltpu.SemaphoreType.DMA((1,))],
        "hold",
    )
    chips = n // 2
    gathered = {}
    for s, e in [hop for hop in hops(n) if hop[1]] + [hop for hop in hops(n) if not hop[1]]:
        if leading(s, e, chips) == s and 2 * s >= chips:
            gathered[s, e] = to_block(other if e else same, s, e)
    for s, e in hops(n):
        if leading(s, e, chips) == s and 2 * s < chips and (s, e) != (0, 1):
            gathered[s, e] = to_block(other2 if e else same2, s, e)
    for s, e in hops(n):
        top = leading(s, e, chips)
        if top != s:
            gathered[s, e] = to_block(gathered[top, e], s ^ top, 0)
    (last,) = call(after_kernel, [payload], [], [], [other2, gathered.get((1, 0), same2)], [], "after")
    gathered[0, 1] = to_block(last, 0, 1)
    gathered = [gathered[hop] for hop in arrivals(n)]
    held = F32 if rows % 16 else BF16
    parts = call(
        functools.partial(fock_kernel, n, half),
        [shape((slab, orbitals), BF16)] * n,
        [blk],
        [],
        [held_body, own, sibling] + gathered,
        [
            pltpu.VMEM((half, n, rows, orbitals), held),
            pltpu.VMEM((half * occupied, orbitals), BF16),
            pltpu.VMEM((half * occupied, 2 * vec_count * occupied), BF16),
            pltpu.VMEM((half, n, rows, orbitals), held),
        ],
        "fock",
        flops=2 * n * slab * orbitals * (orbitals + 4 * vec_count * occupied),
    )
    parts = dict(zip(hops(n), parts))
    for s, e in returns(n):
        via = [hop for hop in hops(n) if hop[1] == e and hop[0] != s and leading(*hop, chips) == s]
        if via:
            later = [hop for hop in returns(n) if hop[0] < s and hop != (0, 0) and (hop[1] == e or 2 * hop[0] < chips)]
            out = call(
                functools.partial(add_kernel, len(later)),
                [shape((slab, orbitals), BF16)] * (1 + len(later)),
                [],
                [],
                [parts[hop] for hop in later] + [parts[s, e]] + [to_block(parts[hop], hop[0] ^ s, 0) for hop in via],
                [],
                "add",
            )
            parts.update(zip([(s, e)] + later, out))
    backs = [to_block(parts[hop], *hop) for hop in returns(n)]
    back = call(
        functools.partial(sum_kernel, n, keep, cap, groups),
        [shape((cap * rows, orbitals), BF16)] * groups,
        [core],
        [],
        [pick] + backs,
        [],
        "sum",
    )
    back = [to_list(back[s], s) for s in order]
    (out,) = call(
        functools.partial(deal_kernel, order, keep, cap),
        [shape(walkers.shape, BF16)],
        [grp, target, weights],
        [],
        [weight_sum] + back,
        [
            pltpu.VMEM((groups * cap + 1, rows, orbitals), F32),
            pltpu.VMEM(walkers.shape, F32),
            pltpu.VMEM(walkers.shape, BF16),
            pltpu.SemaphoreType.DMA((2,)),
        ],
        "deal",
        place=pl.ANY,
    )
    return out


def solution(mesh):
    in_specs = (
        P("blk", "grp", None),
        P(),
        P("grp", "blk"),
        P("blk", None),
        P("blk", None, None),
        P("grp"),
        P("grp"),
    )
    out_specs = P("blk", "grp", None)
    return jax.shard_map(body, mesh=mesh, in_specs=in_specs, out_specs=out_specs, check_vma=False)
```

```python
import functools
import math
import jax
import jax.numpy as jnp
from jax import lax
from jax.experimental import pallas as pl
from jax.experimental.pallas import tpu as pltpu
from jax.sharding import PartitionSpec as P

F32 = jnp.float32
BF16 = jnp.bfloat16
LANES = 128
VMEM = 24
ROUTE_VMEM = 56
STAGE_VMEM = 48


def terms(value, count):
    out = []
    for _ in range(count):
        term = value.astype(BF16).astype(F32)
        out.append(term)
        value = value - term
    return out


def tail_blocks(count, slab):
    return -(-count // slab)


def write_tail(out_ref, start, lines):
    slab = out_ref.shape[0]
    for b in range(tail_blocks(lines.shape[0], slab)):
        part = lines[b * slab : (b + 1) * slab]
        if part.shape[0] < slab:
            part = jnp.concatenate([part, jnp.zeros((slab - part.shape[0], LANES), F32)], axis=0)
        out_ref[:, start + b * LANES : start + (b + 1) * LANES] = part.astype(BF16)


def read_tail(ref, start, count):
    parts = [ref[:, c : c + LANES].astype(F32) for c in range(start, ref.shape[1], LANES)]
    whole = parts[0] if len(parts) == 1 else jnp.concatenate(parts, axis=0)
    return whole[0:count]


def wide_mask(line, width):
    return jnp.concatenate([line] * (width // LANES), axis=1) > 0


def stage_kernel(*refs):
    sems = refs[-1]
    count = sems.shape[0]
    copies = [pltpu.make_async_copy(refs[i], refs[i - count - 1], sems.at[i]) for i in range(count)]
    for copy in copies:
        copy.start()
    for copy in copies:
        copy.wait()


def route_kernel(keep, cap, me_ref, target_any, weights_any, walkers_any, fields_any, diag_any, *refs):
    *outs, target_ref, weights_ref, walkers_ref, fields_ref, diag_ref, wide, blocks, parts, lines, sems = refs
    pairs = (
        (walkers_any, walkers_ref),
        (target_any, target_ref),
        (weights_any, weights_ref),
        (fields_any, fields_ref),
        (diag_any, diag_ref),
    )
    copies = [pltpu.make_async_copy(a, b, sems.at[i]) for i, (a, b) in enumerate(pairs)]
    for copy in copies:
        copy.start()
    rows, slots, orbitals = walkers_ref.shape
    vec_count = fields_ref.shape[1]
    chunks = orbitals // LANES
    groups = len(outs)
    live = groups * keep
    blocks[...] = jnp.zeros(blocks.shape, F32)
    lines[...] = jnp.zeros(lines.shape, F32)
    for copy in copies:
        copy.wait()
    wide[...] = walkers_ref[...].astype(F32)
    exponent = fields_ref[:, 0:1] * diag_ref[0:1, :]
    for g in range(1, vec_count):
        exponent = exponent + fields_ref[:, g : g + 1] * diag_ref[g : g + 1, :]
    for i, term in enumerate(terms(exponent, 2)):
        for c in range(chunks):
            parts[:, i * chunks + c, :] = term[:, c * LANES : (c + 1) * LANES]
    weight = F32(0.0)
    for slot in range(slots):
        t = target_ref[slot]
        alive = t < live
        weight = weight + jnp.where(alive, weights_ref[slot], F32(0.0))
        turn = lax.div(t, groups)
        at = jnp.where(alive, lax.rem(t, groups) * cap + lax.rem(turn, cap), groups * cap)
        blocks[at] = wide[:, slot, :]
        parts[slot, 2 * chunks : 2 * chunks + 1, :] = jnp.full((1, LANES), (turn + 1).astype(F32), F32)
        lines[at] = parts[slot]
    sums = terms(jnp.full((1, LANES), weight, F32), 3)
    for s, out in enumerate(outs):
        base = moved(me_ref[0], s, groups, 1) * cap
        out[:, 0:orbitals] = jnp.concatenate([blocks[base + k] for k in range(cap)], axis=0).astype(BF16)
        tail = [lines[base + k][0 : 2 * chunks + 1] for k in range(cap)]
        write_tail(out, orbitals, jnp.concatenate(tail + sums, axis=0))


def merge_kernel(order, keep, cap, orbitals, core_ref, when, *refs):
    ins, (same_ref, other_ref, same2_ref, other2_ref, weight_ref, pick_ref) = refs[: len(order)], refs[len(order) :]
    half = keep // 2
    rows = ins[0].shape[0] // cap
    slab = half * rows
    chunks = orbitals // LANES
    each = 2 * chunks + 1
    weight = jnp.zeros((1, LANES), F32)
    walker = [jnp.zeros((rows, orbitals), F32)] * keep
    line = [jnp.zeros((2 * chunks, LANES), F32)] * keep
    for s, ref in zip(order, ins):
        tail = read_tail(ref, orbitals, cap * each + 3)
        weight = weight + (tail[cap * each : cap * each + 1] + tail[cap * each + 1 : cap * each + 2] + tail[cap * each + 2 :])
        for k in range(cap):
            flag = tail[(k + 1) * each - 1 : (k + 1) * each]
            block = ref[k * rows : (k + 1) * rows, 0:orbitals].astype(F32)
            part = tail[k * each : (k + 1) * each - 1]
            for m in range(k, keep, cap):
                mine = jnp.where(flag == m + 1, F32(1.0), F32(0.0))
                pick_ref[s * keep + m : s * keep + m + 1, :] = mine
                walker[m] = jnp.where(wide_mask(mine, orbitals), block, walker[m])
                line[m] = jnp.where(mine > 0, part, line[m])
    weight_ref[...] = jnp.broadcast_to(weight, weight_ref.shape)
    first = core_ref[0] == 0
    for out, order in ((same_ref, (0, 1)), (other_ref, (1, 0))):
        picked = []
        for k in range(half):
            a, b = order[0] * half + k, order[1] * half + k
            picked.append(jnp.where(first, line[a], line[b]))
            block = jnp.where(first, walker[a], walker[b])
            for c in range(chunks):
                at = c * slab + k * rows
                out[at : at + rows, :] = block[:, c * LANES : (c + 1) * LANES].astype(BF16)
        tail = [p[i * chunks : (i + 1) * chunks] for i in range(2) for p in picked]
        out[chunks * slab :, :] = jnp.concatenate(tail, axis=0).astype(BF16)
    same2_ref[...] = same_ref[...]
    other2_ref[...] = other_ref[...]


def power(size):
    return size & (size - 1) == 0


def moved(me, s, size, sign):
    if power(size):
        return me ^ s if isinstance(me, int) else lax.bitwise_xor(me, jnp.int32(s))
    at = me + (s if sign > 0 else size - s)
    return at % size if isinstance(me, int) else lax.rem(at, size)


def hops(n):
    chips = n // 2
    far = list(range(chips // 2, chips)) + list(range(1, chips // 2))
    return [(0, 0)] + [(s, e) for s in far for e in range(2)] + [(0, 1)]


def arrivals(n):
    return hops(n)


def leading(s, e, chips):
    return 1 << (s.bit_length() - 1) if s and e and power(chips) else s


def returns(n):
    return [(s, e) for s, e in hops(n) if leading(s, e, n // 2) == s]


def add_kernel(count, *refs):
    outs = refs[len(refs) - 1 - count :]
    ins = refs[: len(refs) - 1 - count]
    total = ins[count][...].astype(F32)
    for ref in ins[count + 1 :]:
        total = total + ref[...].astype(F32)
    outs[0][...] = total.astype(BF16)
    for i in range(count):
        outs[1 + i][...] = ins[i][...]


def partner(blk, s, e, n, sign):
    chip = moved(lax.div(blk, 2), s, n // 2, sign)
    core = lax.rem(blk, 2)
    return 2 * chip + (core if e == 0 else 1 - core)


def fock_kernel(n, half, blk_ref, body_ref, own_ref, sib_ref, *refs):
    ins, outs = refs[:n], refs[n : 2 * n]
    prop, carried, coup, result = refs[2 * n :]
    vec_count, occupied, orbitals = own_ref.shape
    slab = outs[0].shape[0]
    rows = slab // half
    chunks = orbitals // LANES
    blk = blk_ref[0]
    exponent = jnp.zeros((2 * half * chunks, LANES), F32)
    for ref in ins:
        exponent = exponent + ref[chunks * slab :, :].astype(F32)
    growth = jnp.exp(exponent[0 : half * chunks] + exponent[half * chunks :])
    for ref, (s, e) in zip(ins, arrivals(n)):
        source = partner(blk, s, e, n, -1)
        for w in range(half):
            for c in range(chunks):
                piece = ref[c * slab + w * rows : c * slab + (w + 1) * rows, :].astype(F32)
                piece = piece * growth[w * chunks + c : w * chunks + c + 1]
                prop[w, source, :, c * LANES : (c + 1) * LANES] = piece.astype(prop.dtype)
    scaled = jnp.concatenate([prop[w, i] for w in range(half) for i in range(n)], axis=0).astype(BF16)
    carried[...] = jnp.dot(scaled, body_ref[...], preferred_element_type=F32).astype(BF16)
    batch = vec_count
    for c, ref in enumerate((own_ref, sib_ref)):
        for g in range(0, vec_count, batch):
            left = ref[g : g + batch].reshape(batch * occupied, orbitals)
            s = lax.dot_general(left, carried[...], (((1,), (1,)), ((), ())), preferred_element_type=F32).astype(BF16)
            for k in range(batch):
                at = (c * vec_count + g + k) * occupied
                for w in range(half):
                    coup[w * occupied : (w + 1) * occupied, at : at + occupied] = s[
                        k * occupied : (k + 1) * occupied, w * occupied : (w + 1) * occupied
                    ]
    tile = 256 if orbitals % 256 == 0 else orbitals
    depth = vec_count * occupied
    for t in range(0, orbitals, tile):
        total = jnp.dot(
            coup[:, :depth],
            own_ref[:, :, t : t + tile].reshape(depth, tile),
            preferred_element_type=F32,
        )
        total = total + jnp.dot(
            coup[:, depth:],
            sib_ref[:, :, t : t + tile].reshape(depth, tile),
            preferred_element_type=F32,
        )
        for w in range(half):
            for i in range(n):
                at = w * occupied + i * rows
                result[w, i, :, t : t + tile] = total[at : at + rows].astype(result.dtype)
    for out, (s, e) in zip(outs, hops(n)):
        to = partner(blk, s, e, n, 1)
        for w in range(half):
            out[w * rows : (w + 1) * rows, :] = result[w, to].astype(BF16)


def sum_kernel(n, keep, cap, groups, core_ref, pick_ref, *refs):
    known = returns(n)
    ins, outs = refs[: len(known)], refs[len(known) :]
    slab, orbitals = ins[0].shape
    half = keep // 2
    rows = slab // half
    halves = []
    for e in range(2):
        same = [ref for ref, (_, other) in zip(ins, known) if other == e]
        total = same[0][...].astype(F32)
        for ref in same[1:]:
            total = total + ref[...].astype(F32)
        halves.append(total)
    first = core_ref[0] == 0
    whole = [jnp.where(first, halves[0], halves[1]), jnp.where(first, halves[1], halves[0])]
    walker = [whole[m // half][(m % half) * rows : (m % half + 1) * rows] for m in range(keep)]
    for s, out in enumerate(outs):
        source = s if power(groups) else (groups - s) % groups
        for k in range(cap):
            value = jnp.zeros((rows, orbitals), F32)
            for m in range(k, keep, cap):
                mine = pick_ref[source * keep + m : source * keep + m + 1, :]
                value = jnp.where(wide_mask(mine, orbitals), walker[m], value)
            out[k * rows : (k + 1) * rows, :] = value.astype(BF16)


def deal_kernel(order, keep, cap, me_ref, target_ref, weights_ref, total_ref, *refs):
    groups = len(order)
    ins, (out_any, blocks, wide, held, sems) = refs[:groups], refs[groups:]
    rows, slots, orbitals = wide.shape
    live = groups * keep
    for s, ref in zip(order, ins):
        base = moved(me_ref[0], s, groups, -1) * cap
        for k in range(cap):
            blocks[base + k] = ref[k * rows : (k + 1) * rows, :].astype(F32)
    blocks[groups * cap] = jnp.zeros((rows, orbitals), F32)
    places = []
    for slot in range(slots):
        t = target_ref[slot]
        alive = t < live
        at = jnp.where(alive, lax.rem(t, groups) * cap + lax.rem(lax.div(t, groups), cap), groups * cap)
        weight = jnp.where(alive, weights_ref[slot], F32(0.0))
        factor = jnp.full((1, LANES), weight * live, F32) / total_ref[0:1, :]
        places.append((at, factor[:, 0:1]))
    step = rows // sems.shape[0]
    copies = []
    for h in range(sems.shape[0]):
        band = slice(h * step, (h + 1) * step)
        for slot, (at, factor) in enumerate(places):
            wide[band, slot, :] = blocks[at, band, :] * factor
        held[band] = wide[band].astype(BF16)
        copies.append(pltpu.make_async_copy(held.at[band], out_any.at[band], sems.at[h]))
        copies[-1].start()
    for copy in copies:
        copy.wait()


def call(kernel, outs, scalars, held, arrays, scratch, name, flops=0, vmem=VMEM, place=pltpu.VMEM):
    smem = pl.BlockSpec(memory_space=pltpu.SMEM)
    full = pl.BlockSpec(memory_space=pltpu.VMEM)
    size = sum(x.size * x.dtype.itemsize for x in list(arrays) + list(outs))
    return pl.pallas_call(
        kernel,
        out_shape=outs,
        in_specs=[smem] * len(scalars) + [pl.BlockSpec(memory_space=pl.ANY)] * len(held) + [full] * len(arrays),
        out_specs=[pl.BlockSpec(memory_space=place)] * len(outs),
        scratch_shapes=scratch,
        compiler_params=pltpu.CompilerParams(vmem_limit_bytes=vmem * 2**20),
        cost_estimate=pl.CostEstimate(flops=flops, bytes_accessed=size, transcendentals=0),
        name=name,
    )(*scalars, *held, *arrays)


def body(walkers, one_body, fields, field_diag, chol, weights, target):
    rows, slots, orbitals = walkers.shape
    vec_count, occupied, _ = chol.shape
    n, groups = lax.axis_size("blk"), lax.axis_size("grp")
    keep = slots // 2
    half = keep // 2
    cap = -(-slots // groups)
    slab = half * rows
    shape = jax.ShapeDtypeStruct
    grp = lax.axis_index("grp").reshape(1)
    blk = lax.axis_index("blk").reshape(1)
    core = lax.rem(blk, 2)

    def to_list(x, s):
        return lax.ppermute(x, "grp", [(i, moved(i, s, groups, 1)) for i in range(groups)]) if s else x

    def to_block(x, s, e):
        if not s and not e:
            return x
        return lax.ppermute(x, "blk", [(i, 2 * moved(i // 2, s, n // 2, 1) + (i % 2 ^ e)) for i in range(n)])

    order = [0] + sorted(range(1, groups), key=lambda s: (s & 1, -s))
    chunks = orbitals // LANES
    sibling = to_block(chol, 0, 1)
    width = orbitals + tail_blocks(cap * (2 * chunks + 1) + 3, cap * rows) * LANES
    routed = call(
        functools.partial(route_kernel, keep, cap),
        [shape((cap * rows, width), BF16)] * groups,
        [grp],
        [target, weights, walkers, fields, field_diag],
        [],
        [
            pltpu.SMEM(target.shape, target.dtype),
            pltpu.SMEM(weights.shape, weights.dtype),
            pltpu.VMEM(walkers.shape, walkers.dtype),
            pltpu.VMEM(fields.shape, fields.dtype),
            pltpu.VMEM(field_diag.shape, field_diag.dtype),
            pltpu.VMEM((rows, slots, orbitals), F32),
            pltpu.VMEM((groups * cap + 1, rows, orbitals), F32),
            pltpu.VMEM((slots, 2 * chunks + 4, LANES), F32),
            pltpu.VMEM((groups * cap + 1, 2 * chunks + 4, LANES), F32),
            pltpu.SemaphoreType.DMA((5,)),
        ],
        "route",
        vmem=ROUTE_VMEM,
    )
    (kept,) = call(
        stage_kernel,
        [shape(routed[0].shape, BF16)],
        [],
        [routed[0]],
        [],
        [pltpu.SemaphoreType.DMA((1,))],
        "keep",
    )
    (own,) = call(
        stage_kernel,
        [shape(chol.shape, chol.dtype)],
        [],
        [chol, kept],
        [],
        [pltpu.SemaphoreType.DMA((1,))],
        "stage",
        vmem=STAGE_VMEM,
    )
    routed = [to_list(routed[s], s) if s else kept for s in order]
    routed[1], sibling = lax.optimization_barrier((routed[1], sibling))
    payload = shape((chunks * slab + 2 * half * chunks, LANES), BF16)
    same, other, same2, other2, weight_sum, pick = call(
        functools.partial(merge_kernel, order, keep, cap, orbitals),
        [payload] * 4 + [shape((8, LANES), F32), shape((groups * keep, LANES), F32)],
        [core],
        [own],
        routed,
        [],
        "merge",
    )
    (held_body,) = call(
        stage_kernel,
        [shape(one_body.shape, one_body.dtype)],
        [],
        [one_body, weight_sum],
        [],
        [pltpu.SemaphoreType.DMA((1,))],
        "hold",
    )
    chips = n // 2
    gathered = {}
    for s, e in [hop for hop in hops(n) if hop[1]] + [hop for hop in hops(n) if not hop[1]]:
        if leading(s, e, chips) == s and 2 * s >= chips:
            gathered[s, e] = to_block(other if e else same, s, e)
    for s, e in hops(n):
        if leading(s, e, chips) == s and 2 * s < chips and (s, e) not in ((0, 1), (1, 1)):
            gathered[s, e] = to_block(other2 if e else same2, s, e)
    first = (chips // 2, 1)
    gathered[first], later = lax.optimization_barrier((gathered[first], other2))
    gathered[1, 0], latest = lax.optimization_barrier((gathered[1, 0], later))
    for s, e in hops(n):
        top = leading(s, e, chips)
        if top != s:
            gathered[s, e] = to_block(gathered[top, e], s ^ top, 0)
    gathered[1, 1] = to_block(later, 1, 1)
    gathered[0, 1] = to_block(latest, 0, 1)
    gathered = [gathered[hop] for hop in arrivals(n)]
    held = F32 if rows % 16 else BF16
    parts = call(
        functools.partial(fock_kernel, n, half),
        [shape((slab, orbitals), BF16)] * n,
        [blk],
        [],
        [held_body, own, sibling] + gathered,
        [
            pltpu.VMEM((half, n, rows, orbitals), held),
            pltpu.VMEM((half * occupied, orbitals), BF16),
            pltpu.VMEM((half * occupied, 2 * vec_count * occupied), BF16),
            pltpu.VMEM((half, n, rows, orbitals), held),
        ],
        "fock",
        flops=2 * n * slab * orbitals * (orbitals + 4 * vec_count * occupied),
    )
    parts = dict(zip(hops(n), parts))
    for s, e in returns(n):
        via = [hop for hop in hops(n) if hop[1] == e and hop[0] != s and leading(*hop, chips) == s]
        if via:
            later = [hop for hop in returns(n) if hop[0] < s and hop != (0, 0) and (hop[1] == e or 2 * hop[0] < chips)]
            out = call(
                functools.partial(add_kernel, len(later)),
                [shape((slab, orbitals), BF16)] * (1 + len(later)),
                [],
                [],
                [parts[hop] for hop in later] + [parts[s, e]] + [to_block(parts[hop], hop[0] ^ s, 0) for hop in via],
                [],
                "add",
            )
            parts.update(zip([(s, e)] + later, out))
    backs = [to_block(parts[hop], *hop) for hop in returns(n)]
    back = call(
        functools.partial(sum_kernel, n, keep, cap, groups),
        [shape((cap * rows, orbitals), BF16)] * groups,
        [core],
        [],
        [pick] + backs,
        [],
        "sum",
    )
    back = [to_list(back[s], s) for s in order]
    (out,) = call(
        functools.partial(deal_kernel, order, keep, cap),
        [shape(walkers.shape, BF16)],
        [grp, target, weights],
        [],
        [weight_sum] + back,
        [
            pltpu.VMEM((groups * cap + 1, rows, orbitals), F32),
            pltpu.VMEM(walkers.shape, F32),
            pltpu.VMEM(walkers.shape, BF16),
            pltpu.SemaphoreType.DMA((2,)),
        ],
        "deal",
        place=pl.ANY,
    )
    return out


def solution(mesh):
    in_specs = (
        P("blk", "grp", None),
        P(),
        P("grp", "blk"),
        P("blk", None),
        P("blk", None, None),
        P("grp"),
        P("grp"),
    )
    out_specs = P("blk", "grp", None)
    return jax.shard_map(body, mesh=mesh, in_specs=in_specs, out_specs=out_specs, check_vma=False)
```

```python
import functools
import math
import jax
import jax.numpy as jnp
from jax import lax
from jax.experimental import pallas as pl
from jax.experimental.pallas import tpu as pltpu
from jax.sharding import PartitionSpec as P

F32 = jnp.float32
BF16 = jnp.bfloat16
LANES = 128
VMEM = 24
ROUTE_VMEM = 56
STAGE_VMEM = 48


def terms(value, count):
    out = []
    for _ in range(count):
        term = value.astype(BF16).astype(F32)
        out.append(term)
        value = value - term
    return out


def tail_blocks(count, slab):
    return -(-count // slab)


def write_tail(out_ref, start, lines):
    slab = out_ref.shape[0]
    for b in range(tail_blocks(lines.shape[0], slab)):
        part = lines[b * slab : (b + 1) * slab]
        if part.shape[0] < slab:
            part = jnp.concatenate([part, jnp.zeros((slab - part.shape[0], LANES), F32)], axis=0)
        out_ref[:, start + b * LANES : start + (b + 1) * LANES] = part.astype(BF16)


def read_tail(ref, start, count):
    parts = [ref[:, c : c + LANES].astype(F32) for c in range(start, ref.shape[1], LANES)]
    whole = parts[0] if len(parts) == 1 else jnp.concatenate(parts, axis=0)
    return whole[0:count]


def wide_mask(line, width):
    return jnp.concatenate([line] * (width // LANES), axis=1) > 0


def stage_kernel(*refs):
    sems = refs[-1]
    count = sems.shape[0]
    copies = [pltpu.make_async_copy(refs[i], refs[i - count - 1], sems.at[i]) for i in range(count)]
    for copy in copies:
        copy.start()
    for copy in copies:
        copy.wait()


def route_kernel(keep, cap, me_ref, target_any, weights_any, walkers_any, fields_any, diag_any, *refs):
    *outs, target_ref, weights_ref, walkers_ref, fields_ref, diag_ref, wide, blocks, parts, lines, sems = refs
    pairs = (
        (walkers_any, walkers_ref),
        (target_any, target_ref),
        (weights_any, weights_ref),
        (fields_any, fields_ref),
        (diag_any, diag_ref),
    )
    copies = [pltpu.make_async_copy(a, b, sems.at[i]) for i, (a, b) in enumerate(pairs)]
    for copy in copies:
        copy.start()
    rows, slots, orbitals = walkers_ref.shape
    vec_count = fields_ref.shape[1]
    chunks = orbitals // LANES
    groups = len(outs)
    live = groups * keep
    blocks[...] = jnp.zeros(blocks.shape, F32)
    lines[...] = jnp.zeros(lines.shape, F32)
    for copy in copies:
        copy.wait()
    wide[...] = walkers_ref[...].astype(F32)
    exponent = fields_ref[:, 0:1] * diag_ref[0:1, :]
    for g in range(1, vec_count):
        exponent = exponent + fields_ref[:, g : g + 1] * diag_ref[g : g + 1, :]
    for i, term in enumerate(terms(exponent, 2)):
        for c in range(chunks):
            parts[:, i * chunks + c, :] = term[:, c * LANES : (c + 1) * LANES]
    weight = F32(0.0)
    for slot in range(slots):
        t = target_ref[slot]
        alive = t < live
        weight = weight + jnp.where(alive, weights_ref[slot], F32(0.0))
        turn = lax.div(t, groups)
        at = jnp.where(alive, lax.rem(t, groups) * cap + lax.rem(turn, cap), groups * cap)
        blocks[at] = wide[:, slot, :]
        parts[slot, 2 * chunks : 2 * chunks + 1, :] = jnp.full((1, LANES), (turn + 1).astype(F32), F32)
        lines[at] = parts[slot]
    sums = terms(jnp.full((1, LANES), weight, F32), 3)
    for s, out in enumerate(outs):
        base = moved(me_ref[0], s, groups, 1) * cap
        out[:, 0:orbitals] = jnp.concatenate([blocks[base + k] for k in range(cap)], axis=0).astype(BF16)
        tail = [lines[base + k][0 : 2 * chunks + 1] for k in range(cap)]
        write_tail(out, orbitals, jnp.concatenate(tail + sums, axis=0))


def merge_kernel(order, keep, cap, orbitals, core_ref, when, *refs):
    ins, (same_ref, other_ref, same2_ref, other2_ref, weight_ref, pick_ref) = refs[: len(order)], refs[len(order) :]
    half = keep // 2
    rows = ins[0].shape[0] // cap
    slab = half * rows
    chunks = orbitals // LANES
    each = 2 * chunks + 1
    weight = jnp.zeros((1, LANES), F32)
    walker = [jnp.zeros((rows, orbitals), F32)] * keep
    line = [jnp.zeros((2 * chunks, LANES), F32)] * keep
    for s, ref in zip(order, ins):
        tail = read_tail(ref, orbitals, cap * each + 3)
        weight = weight + (tail[cap * each : cap * each + 1] + tail[cap * each + 1 : cap * each + 2] + tail[cap * each + 2 :])
        for k in range(cap):
            flag = tail[(k + 1) * each - 1 : (k + 1) * each]
            block = ref[k * rows : (k + 1) * rows, 0:orbitals].astype(F32)
            part = tail[k * each : (k + 1) * each - 1]
            for m in range(k, keep, cap):
                mine = jnp.where(flag == m + 1, F32(1.0), F32(0.0))
                pick_ref[s * keep + m : s * keep + m + 1, :] = mine
                walker[m] = jnp.where(wide_mask(mine, orbitals), block, walker[m])
                line[m] = jnp.where(mine > 0, part, line[m])
    weight_ref[...] = jnp.broadcast_to(weight, weight_ref.shape)
    first = core_ref[0] == 0
    for out, order in ((same_ref, (0, 1)), (other_ref, (1, 0))):
        picked = []
        for k in range(half):
            a, b = order[0] * half + k, order[1] * half + k
            picked.append(jnp.where(first, line[a], line[b]))
            block = jnp.where(first, walker[a], walker[b])
            for c in range(chunks):
                at = c * slab + k * rows
                out[at : at + rows, :] = block[:, c * LANES : (c + 1) * LANES].astype(BF16)
        tail = [p[i * chunks : (i + 1) * chunks] for i in range(2) for p in picked]
        out[chunks * slab :, :] = jnp.concatenate(tail, axis=0).astype(BF16)
    same2_ref[...] = same_ref[...]
    other2_ref[...] = other_ref[...]


def power(size):
    return size & (size - 1) == 0


def moved(me, s, size, sign):
    if power(size):
        return me ^ s if isinstance(me, int) else lax.bitwise_xor(me, jnp.int32(s))
    at = me + (s if sign > 0 else size - s)
    return at % size if isinstance(me, int) else lax.rem(at, size)


def hops(n):
    chips = n // 2
    far = list(range(chips // 2, chips)) + list(range(1, chips // 2))
    return [(0, 0)] + [(s, e) for s in far for e in range(2)] + [(0, 1)]


def arrivals(n):
    return hops(n)


def leading(s, e, chips):
    return 1 << (s.bit_length() - 1) if s and e and power(chips) else s


def returns(n):
    return [(s, e) for s, e in hops(n) if leading(s, e, n // 2) == s]


def add_kernel(count, *refs):
    outs = refs[len(refs) - 1 - count :]
    ins = refs[: len(refs) - 1 - count]
    total = ins[count][...].astype(F32)
    for ref in ins[count + 1 :]:
        total = total + ref[...].astype(F32)
    outs[0][...] = total.astype(BF16)
    for i in range(count):
        outs[1 + i][...] = ins[i][...]


def partner(blk, s, e, n, sign):
    chip = moved(lax.div(blk, 2), s, n // 2, sign)
    core = lax.rem(blk, 2)
    return 2 * chip + (core if e == 0 else 1 - core)


def fock_kernel(n, half, blk_ref, body_ref, own_ref, sib_ref, *refs):
    ins, outs = refs[:n], refs[n : 2 * n]
    prop, carried, coup, result = refs[2 * n :]
    vec_count, occupied, orbitals = own_ref.shape
    slab = outs[0].shape[0]
    rows = slab // half
    chunks = orbitals // LANES
    blk = blk_ref[0]
    exponent = jnp.zeros((2 * half * chunks, LANES), F32)
    for ref in ins:
        exponent = exponent + ref[chunks * slab :, :].astype(F32)
    growth = jnp.exp(exponent[0 : half * chunks] + exponent[half * chunks :])
    for ref, (s, e) in zip(ins, arrivals(n)):
        source = partner(blk, s, e, n, -1)
        for w in range(half):
            for c in range(chunks):
                piece = ref[c * slab + w * rows : c * slab + (w + 1) * rows, :].astype(F32)
                piece = piece * growth[w * chunks + c : w * chunks + c + 1]
                prop[w, source, :, c * LANES : (c + 1) * LANES] = piece.astype(prop.dtype)
    scaled = jnp.concatenate([prop[w, i] for w in range(half) for i in range(n)], axis=0).astype(BF16)
    carried[...] = jnp.dot(scaled, body_ref[...], preferred_element_type=F32).astype(BF16)
    batch = math.gcd(vec_count, 4)
    for c, ref in enumerate((own_ref, sib_ref)):
        for g in range(0, vec_count, batch):
            left = ref[g : g + batch].reshape(batch * occupied, orbitals)
            s = lax.dot_general(left, carried[...], (((1,), (1,)), ((), ())), preferred_element_type=F32).astype(BF16)
            for k in range(batch):
                at = (c * vec_count + g + k) * occupied
                for w in range(half):
                    coup[w * occupied : (w + 1) * occupied, at : at + occupied] = s[
                        k * occupied : (k + 1) * occupied, w * occupied : (w + 1) * occupied
                    ]
    tile = 256 if orbitals % 256 == 0 else orbitals
    depth = vec_count * occupied
    for t in range(0, orbitals, tile):
        total = jnp.dot(
            coup[:, :depth],
            own_ref[:, :, t : t + tile].reshape(depth, tile),
            preferred_element_type=F32,
        )
        total = total + jnp.dot(
            coup[:, depth:],
            sib_ref[:, :, t : t + tile].reshape(depth, tile),
            preferred_element_type=F32,
        )
        for w in range(half):
            for i in range(n):
                at = w * occupied + i * rows
                result[w, i, :, t : t + tile] = total[at : at + rows].astype(result.dtype)
    for out, (s, e) in zip(outs, hops(n)):
        to = partner(blk, s, e, n, 1)
        for w in range(half):
            out[w * rows : (w + 1) * rows, :] = result[w, to].astype(BF16)


def sum_kernel(n, keep, cap, groups, core_ref, pick_ref, *refs):
    known = returns(n)
    ins, outs = refs[: len(known)], refs[len(known) :]
    slab, orbitals = ins[0].shape
    half = keep // 2
    rows = slab // half
    halves = []
    for e in range(2):
        same = [ref for ref, (_, other) in zip(ins, known) if other == e]
        total = same[0][...].astype(F32)
        for ref in same[1:]:
            total = total + ref[...].astype(F32)
        halves.append(total)
    first = core_ref[0] == 0
    whole = [jnp.where(first, halves[0], halves[1]), jnp.where(first, halves[1], halves[0])]
    walker = [whole[m // half][(m % half) * rows : (m % half + 1) * rows] for m in range(keep)]
    for s, out in enumerate(outs):
        source = s if power(groups) else (groups - s) % groups
        for k in range(cap):
            value = jnp.zeros((rows, orbitals), F32)
            for m in range(k, keep, cap):
                mine = pick_ref[source * keep + m : source * keep + m + 1, :]
                value = jnp.where(wide_mask(mine, orbitals), walker[m], value)
            out[k * rows : (k + 1) * rows, :] = value.astype(BF16)


def deal_kernel(order, keep, cap, me_ref, target_ref, weights_ref, total_ref, *refs):
    groups = len(order)
    ins, (out_any, blocks, wide, held, sems) = refs[:groups], refs[groups:]
    rows, slots, orbitals = wide.shape
    live = groups * keep
    for s, ref in zip(order, ins):
        base = moved(me_ref[0], s, groups, -1) * cap
        for k in range(cap):
            blocks[base + k] = ref[k * rows : (k + 1) * rows, :].astype(F32)
    blocks[groups * cap] = jnp.zeros((rows, orbitals), F32)
    places = []
    for slot in range(slots):
        t = target_ref[slot]
        alive = t < live
        at = jnp.where(alive, lax.rem(t, groups) * cap + lax.rem(lax.div(t, groups), cap), groups * cap)
        weight = jnp.where(alive, weights_ref[slot], F32(0.0))
        factor = jnp.full((1, LANES), weight * live, F32) / total_ref[0:1, :]
        places.append((at, factor[:, 0:1]))
    step = rows // sems.shape[0]
    copies = []
    for h in range(sems.shape[0]):
        band = slice(h * step, (h + 1) * step)
        for slot, (at, factor) in enumerate(places):
            wide[band, slot, :] = blocks[at, band, :] * factor
        held[band] = wide[band].astype(BF16)
        copies.append(pltpu.make_async_copy(held.at[band], out_any.at[band], sems.at[h]))
        copies[-1].start()
    for copy in copies:
        copy.wait()


def call(kernel, outs, scalars, held, arrays, scratch, name, flops=0, vmem=VMEM, place=pltpu.VMEM):
    smem = pl.BlockSpec(memory_space=pltpu.SMEM)
    full = pl.BlockSpec(memory_space=pltpu.VMEM)
    size = sum(x.size * x.dtype.itemsize for x in list(arrays) + list(outs))
    return pl.pallas_call(
        kernel,
        out_shape=outs,
        in_specs=[smem] * len(scalars) + [pl.BlockSpec(memory_space=pl.ANY)] * len(held) + [full] * len(arrays),
        out_specs=[pl.BlockSpec(memory_space=place)] * len(outs),
        scratch_shapes=scratch,
        compiler_params=pltpu.CompilerParams(vmem_limit_bytes=vmem * 2**20),
        cost_estimate=pl.CostEstimate(flops=flops, bytes_accessed=size, transcendentals=0),
        name=name,
    )(*scalars, *held, *arrays)


def body(walkers, one_body, fields, field_diag, chol, weights, target):
    rows, slots, orbitals = walkers.shape
    vec_count, occupied, _ = chol.shape
    n, groups = lax.axis_size("blk"), lax.axis_size("grp")
    keep = slots // 2
    half = keep // 2
    cap = -(-slots // groups)
    slab = half * rows
    shape = jax.ShapeDtypeStruct
    grp = lax.axis_index("grp").reshape(1)
    blk = lax.axis_index("blk").reshape(1)
    core = lax.rem(blk, 2)

    def to_list(x, s):
        return lax.ppermute(x, "grp", [(i, moved(i, s, groups, 1)) for i in range(groups)]) if s else x

    def to_block(x, s, e):
        if not s and not e:
            return x
        return lax.ppermute(x, "blk", [(i, 2 * moved(i // 2, s, n // 2, 1) + (i % 2 ^ e)) for i in range(n)])

    order = [0] + sorted(range(1, groups), key=lambda s: (s & 1, -s))
    chunks = orbitals // LANES
    sibling = to_block(chol, 0, 1)
    width = orbitals + tail_blocks(cap * (2 * chunks + 1) + 3, cap * rows) * LANES
    routed = call(
        functools.partial(route_kernel, keep, cap),
        [shape((cap * rows, width), BF16)] * groups,
        [grp],
        [target, weights, walkers, fields, field_diag],
        [],
        [
            pltpu.SMEM(target.shape, target.dtype),
            pltpu.SMEM(weights.shape, weights.dtype),
            pltpu.VMEM(walkers.shape, walkers.dtype),
            pltpu.VMEM(fields.shape, fields.dtype),
            pltpu.VMEM(field_diag.shape, field_diag.dtype),
            pltpu.VMEM((rows, slots, orbitals), F32),
            pltpu.VMEM((groups * cap + 1, rows, orbitals), F32),
            pltpu.VMEM((slots, 2 * chunks + 4, LANES), F32),
            pltpu.VMEM((groups * cap + 1, 2 * chunks + 4, LANES), F32),
            pltpu.SemaphoreType.DMA((5,)),
        ],
        "route",
        vmem=ROUTE_VMEM,
    )
    (kept,) = call(
        stage_kernel,
        [shape(routed[0].shape, BF16)],
        [],
        [routed[0]],
        [],
        [pltpu.SemaphoreType.DMA((1,))],
        "keep",
    )
    (own,) = call(
        stage_kernel,
        [shape(chol.shape, chol.dtype)],
        [],
        [chol, kept],
        [],
        [pltpu.SemaphoreType.DMA((1,))],
        "stage",
        vmem=STAGE_VMEM,
    )
    routed = [to_list(routed[s], s) if s else kept for s in order]
    routed[1], sibling = lax.optimization_barrier((routed[1], sibling))
    payload = shape((chunks * slab + 2 * half * chunks, LANES), BF16)
    same, other, same2, other2, weight_sum, pick = call(
        functools.partial(merge_kernel, order, keep, cap, orbitals),
        [payload] * 4 + [shape((8, LANES), F32), shape((groups * keep, LANES), F32)],
        [core],
        [own],
        routed,
        [],
        "merge",
    )
    (held_body,) = call(
        stage_kernel,
        [shape(one_body.shape, one_body.dtype)],
        [],
        [one_body, weight_sum],
        [],
        [pltpu.SemaphoreType.DMA((1,))],
        "hold",
    )
    chips = n // 2
    gathered = {}
    for s, e in [hop for hop in hops(n) if hop[1]] + [hop for hop in hops(n) if not hop[1]]:
        if leading(s, e, chips) == s and 2 * s >= chips:
            gathered[s, e] = to_block(other if e else same, s, e)
    for s, e in hops(n):
        if leading(s, e, chips) == s and 2 * s < chips and (s, e) not in ((0, 1), (1, 1)):
            gathered[s, e] = to_block(other2 if e else same2, s, e)
    first = (chips // 2, 1)
    gathered[first], later = lax.optimization_barrier((gathered[first], other2))
    gathered[1, 0], latest = lax.optimization_barrier((gathered[1, 0], later))
    for s, e in hops(n):
        top = leading(s, e, chips)
        if top != s:
            gathered[s, e] = to_block(gathered[top, e], s ^ top, 0)
    gathered[1, 1] = to_block(later, 1, 1)
    gathered[0, 1] = to_block(latest, 0, 1)
    gathered = [gathered[hop] for hop in arrivals(n)]
    held = F32 if rows % 16 else BF16
    parts = call(
        functools.partial(fock_kernel, n, half),
        [shape((slab, orbitals), BF16)] * n,
        [blk],
        [],
        [held_body, own, sibling] + gathered,
        [
            pltpu.VMEM((half, n, rows, orbitals), held),
            pltpu.VMEM((half * occupied, orbitals), BF16),
            pltpu.VMEM((half * occupied, 2 * vec_count * occupied), BF16),
            pltpu.VMEM((half, n, rows, orbitals), held),
        ],
        "fock",
        flops=2 * n * slab * orbitals * (orbitals + 4 * vec_count * occupied),
    )
    parts = dict(zip(hops(n), parts))
    for s, e in returns(n):
        via = [hop for hop in hops(n) if hop[1] == e and hop[0] != s and leading(*hop, chips) == s]
        if via:
            later = [hop for hop in returns(n) if hop[0] < s and hop != (0, 0) and (hop[1] == e or 2 * hop[0] < chips)]
            out = call(
                functools.partial(add_kernel, len(later)),
                [shape((slab, orbitals), BF16)] * (1 + len(later)),
                [],
                [],
                [parts[hop] for hop in later] + [parts[s, e]] + [to_block(parts[hop], hop[0] ^ s, 0) for hop in via],
                [],
                "add",
            )
            parts.update(zip([(s, e)] + later, out))
    backs = [to_block(parts[hop], *hop) for hop in returns(n)]
    back = call(
        functools.partial(sum_kernel, n, keep, cap, groups),
        [shape((cap * rows, orbitals), BF16)] * groups,
        [core],
        [],
        [pick] + backs,
        [],
        "sum",
    )
    back = [to_list(back[s], s) for s in order]
    (out,) = call(
        functools.partial(deal_kernel, order, keep, cap),
        [shape(walkers.shape, BF16)],
        [grp, target, weights],
        [],
        [weight_sum] + back,
        [
            pltpu.VMEM((groups * cap + 1, rows, orbitals), F32),
            pltpu.VMEM(walkers.shape, F32),
            pltpu.VMEM(walkers.shape, BF16),
            pltpu.SemaphoreType.DMA((2,)),
        ],
        "deal",
        place=pl.ANY,
    )
    return out


def solution(mesh):
    in_specs = (
        P("blk", "grp", None),
        P(),
        P("grp", "blk"),
        P("blk", None),
        P("blk", None, None),
        P("grp"),
        P("grp"),
    )
    out_specs = P("blk", "grp", None)
    return jax.shard_map(body, mesh=mesh, in_specs=in_specs, out_specs=out_specs, check_vma=False)
```

```python
import functools
import math
import jax
import jax.numpy as jnp
from jax import lax
from jax.experimental import pallas as pl
from jax.experimental.pallas import tpu as pltpu
from jax.sharding import PartitionSpec as P

F32 = jnp.float32
BF16 = jnp.bfloat16
LANES = 128
VMEM = 24
ROUTE_VMEM = 56
STAGE_VMEM = 48


def terms(value, count):
    out = []
    for _ in range(count):
        term = value.astype(BF16).astype(F32)
        out.append(term)
        value = value - term
    return out


def tail_blocks(count, slab):
    return -(-count // slab)


def write_tail(out_ref, start, lines):
    slab = out_ref.shape[0]
    for b in range(tail_blocks(lines.shape[0], slab)):
        part = lines[b * slab : (b + 1) * slab]
        if part.shape[0] < slab:
            part = jnp.concatenate([part, jnp.zeros((slab - part.shape[0], LANES), F32)], axis=0)
        out_ref[:, start + b * LANES : start + (b + 1) * LANES] = part.astype(BF16)


def read_tail(ref, start, count):
    parts = [ref[:, c : c + LANES].astype(F32) for c in range(start, ref.shape[1], LANES)]
    whole = parts[0] if len(parts) == 1 else jnp.concatenate(parts, axis=0)
    return whole[0:count]


def wide_mask(line, width):
    return jnp.concatenate([line] * (width // LANES), axis=1) > 0


def stage_kernel(*refs):
    sems = refs[-1]
    count = sems.shape[0]
    copies = [pltpu.make_async_copy(refs[i], refs[i - count - 1], sems.at[i]) for i in range(count)]
    for copy in copies:
        copy.start()
    for copy in copies:
        copy.wait()


def route_kernel(keep, cap, me_ref, target_any, weights_any, walkers_any, fields_any, diag_any, *refs):
    *outs, target_ref, weights_ref, walkers_ref, fields_ref, diag_ref, wide, blocks, parts, lines, sems = refs
    pairs = (
        (walkers_any, walkers_ref),
        (target_any, target_ref),
        (weights_any, weights_ref),
        (fields_any, fields_ref),
        (diag_any, diag_ref),
    )
    copies = [pltpu.make_async_copy(a, b, sems.at[i]) for i, (a, b) in enumerate(pairs)]
    for copy in copies:
        copy.start()
    rows, slots, orbitals = walkers_ref.shape
    vec_count = fields_ref.shape[1]
    chunks = orbitals // LANES
    groups = len(outs)
    live = groups * keep
    blocks[...] = jnp.zeros(blocks.shape, F32)
    lines[...] = jnp.zeros(lines.shape, F32)
    for copy in copies:
        copy.wait()
    wide[...] = walkers_ref[...].astype(F32)
    exponent = fields_ref[:, 0:1] * diag_ref[0:1, :]
    for g in range(1, vec_count):
        exponent = exponent + fields_ref[:, g : g + 1] * diag_ref[g : g + 1, :]
    for i, term in enumerate(terms(exponent, 2)):
        for c in range(chunks):
            parts[:, i * chunks + c, :] = term[:, c * LANES : (c + 1) * LANES]
    weight = F32(0.0)
    for slot in range(slots):
        t = target_ref[slot]
        alive = t < live
        weight = weight + jnp.where(alive, weights_ref[slot], F32(0.0))
        turn = lax.div(t, groups)
        at = jnp.where(alive, lax.rem(t, groups) * cap + lax.rem(turn, cap), groups * cap)
        blocks[at] = wide[:, slot, :]
        parts[slot, 2 * chunks : 2 * chunks + 1, :] = jnp.full((1, LANES), (turn + 1).astype(F32), F32)
        lines[at] = parts[slot]
    sums = terms(jnp.full((1, LANES), weight, F32), 3)
    for s, out in enumerate(outs):
        base = moved(me_ref[0], s, groups, 1) * cap
        out[:, 0:orbitals] = jnp.concatenate([blocks[base + k] for k in range(cap)], axis=0).astype(BF16)
        tail = [lines[base + k][0 : 2 * chunks + 1] for k in range(cap)]
        write_tail(out, orbitals, jnp.concatenate(tail + sums, axis=0))


def merge_kernel(order, keep, cap, orbitals, core_ref, when, *refs):
    ins, (same_ref, other_ref, same2_ref, other2_ref, weight_ref, pick_ref) = refs[: len(order)], refs[len(order) :]
    half = keep // 2
    rows = ins[0].shape[0] // cap
    slab = half * rows
    chunks = orbitals // LANES
    each = 2 * chunks + 1
    weight = jnp.zeros((1, LANES), F32)
    walker = [jnp.zeros((rows, orbitals), F32)] * keep
    line = [jnp.zeros((2 * chunks, LANES), F32)] * keep
    for s, ref in zip(order, ins):
        tail = read_tail(ref, orbitals, cap * each + 3)
        weight = weight + (tail[cap * each : cap * each + 1] + tail[cap * each + 1 : cap * each + 2] + tail[cap * each + 2 :])
        for k in range(cap):
            flag = tail[(k + 1) * each - 1 : (k + 1) * each]
            block = ref[k * rows : (k + 1) * rows, 0:orbitals].astype(F32)
            part = tail[k * each : (k + 1) * each - 1]
            for m in range(k, keep, cap):
                mine = jnp.where(flag == m + 1, F32(1.0), F32(0.0))
                pick_ref[s * keep + m : s * keep + m + 1, :] = mine
                walker[m] = jnp.where(wide_mask(mine, orbitals), block, walker[m])
                line[m] = jnp.where(mine > 0, part, line[m])
    weight_ref[...] = jnp.broadcast_to(weight, weight_ref.shape)
    first = core_ref[0] == 0
    for out, order in ((same_ref, (0, 1)), (other_ref, (1, 0))):
        picked = []
        for k in range(half):
            a, b = order[0] * half + k, order[1] * half + k
            picked.append(jnp.where(first, line[a], line[b]))
            block = jnp.where(first, walker[a], walker[b])
            for c in range(chunks):
                at = c * slab + k * rows
                out[at : at + rows, :] = block[:, c * LANES : (c + 1) * LANES].astype(BF16)
        tail = [p[i * chunks : (i + 1) * chunks] for i in range(2) for p in picked]
        out[chunks * slab :, :] = jnp.concatenate(tail, axis=0).astype(BF16)
    same2_ref[...] = same_ref[...]
    other2_ref[...] = other_ref[...]


def power(size):
    return size & (size - 1) == 0


def moved(me, s, size, sign):
    if power(size):
        return me ^ s if isinstance(me, int) else lax.bitwise_xor(me, jnp.int32(s))
    at = me + (s if sign > 0 else size - s)
    return at % size if isinstance(me, int) else lax.rem(at, size)


def hops(n):
    chips = n // 2
    far = list(range(chips // 2, chips)) + list(range(1, chips // 2))
    return [(0, 0)] + [(s, e) for s in far for e in range(2)] + [(0, 1)]


def after_kernel(source_ref, when_ref, out_ref):
    out_ref[...] = source_ref[...]


def arrivals(n):
    return hops(n)[:1] + hops(n)[:0:-1]


def leading(s, e, chips):
    return 1 << (s.bit_length() - 1) if s and e and power(chips) else s


def returns(n):
    return [(s, e) for s, e in hops(n) if leading(s, e, n // 2) == s]


def add_kernel(count, *refs):
    outs = refs[len(refs) - 1 - count :]
    ins = refs[: len(refs) - 1 - count]
    total = ins[count][...].astype(F32)
    for ref in ins[count + 1 :]:
        total = total + ref[...].astype(F32)
    outs[0][...] = total.astype(BF16)
    for i in range(count):
        outs[1 + i][...] = ins[i][...]


def partner(blk, s, e, n, sign):
    chip = moved(lax.div(blk, 2), s, n // 2, sign)
    core = lax.rem(blk, 2)
    return 2 * chip + (core if e == 0 else 1 - core)


def fock_kernel(n, half, blk_ref, body_ref, own_ref, sib_ref, *refs):
    ins, outs = refs[:n], refs[n : 2 * n]
    prop, carried, coup, result = refs[2 * n :]
    vec_count, occupied, orbitals = own_ref.shape
    slab = outs[0].shape[0]
    rows = slab // half
    chunks = orbitals // LANES
    blk = blk_ref[0]
    exponent = jnp.zeros((2 * half * chunks, LANES), F32)
    for ref in ins:
        exponent = exponent + ref[chunks * slab :, :].astype(F32)
    growth = jnp.exp(exponent[0 : half * chunks] + exponent[half * chunks :])
    for ref, (s, e) in zip(ins, arrivals(n)):
        source = partner(blk, s, e, n, -1)
        for w in range(half):
            for c in range(chunks):
                piece = ref[c * slab + w * rows : c * slab + (w + 1) * rows, :].astype(F32)
                piece = piece * growth[w * chunks + c : w * chunks + c + 1]
                prop[w, source, :, c * LANES : (c + 1) * LANES] = piece.astype(prop.dtype)
    scaled = jnp.concatenate([prop[w, i] for w in range(half) for i in range(n)], axis=0).astype(BF16)
    carried[...] = jnp.dot(scaled, body_ref[...], preferred_element_type=F32).astype(BF16)
    batch = math.gcd(vec_count, 4)
    for c, ref in enumerate((own_ref, sib_ref)):
        for g in range(0, vec_count, batch):
            left = ref[g : g + batch].reshape(batch * occupied, orbitals)
            s = lax.dot_general(left, carried[...], (((1,), (1,)), ((), ())), preferred_element_type=F32).astype(BF16)
            for k in range(batch):
                at = (c * vec_count + g + k) * occupied
                for w in range(half):
                    coup[w * occupied : (w + 1) * occupied, at : at + occupied] = s[
                        k * occupied : (k + 1) * occupied, w * occupied : (w + 1) * occupied
                    ]
    tile = 256 if orbitals % 256 == 0 else orbitals
    depth = vec_count * occupied
    for t in range(0, orbitals, tile):
        total = jnp.dot(
            coup[:, :depth],
            own_ref[:, :, t : t + tile].reshape(depth, tile),
            preferred_element_type=F32,
        )
        total = total + jnp.dot(
            coup[:, depth:],
            sib_ref[:, :, t : t + tile].reshape(depth, tile),
            preferred_element_type=F32,
        )
        for w in range(half):
            for i in range(n):
                at = w * occupied + i * rows
                result[w, i, :, t : t + tile] = total[at : at + rows].astype(result.dtype)
    for out, (s, e) in zip(outs, hops(n)):
        to = partner(blk, s, e, n, 1)
        for w in range(half):
            out[w * rows : (w + 1) * rows, :] = result[w, to].astype(BF16)


def sum_kernel(n, keep, cap, groups, core_ref, pick_ref, *refs):
    known = returns(n)
    ins, outs = refs[: len(known)], refs[len(known) :]
    slab, orbitals = ins[0].shape
    half = keep // 2
    rows = slab // half
    halves = []
    for e in range(2):
        same = [ref for ref, (_, other) in zip(ins, known) if other == e]
        total = same[0][...].astype(F32)
        for ref in same[1:]:
            total = total + ref[...].astype(F32)
        halves.append(total)
    first = core_ref[0] == 0
    whole = [jnp.where(first, halves[0], halves[1]), jnp.where(first, halves[1], halves[0])]
    walker = [whole[m // half][(m % half) * rows : (m % half + 1) * rows] for m in range(keep)]
    for s, out in enumerate(outs):
        source = s if power(groups) else (groups - s) % groups
        for k in range(cap):
            value = jnp.zeros((rows, orbitals), F32)
            for m in range(k, keep, cap):
                mine = pick_ref[source * keep + m : source * keep + m + 1, :]
                value = jnp.where(wide_mask(mine, orbitals), walker[m], value)
            out[k * rows : (k + 1) * rows, :] = value.astype(BF16)


def deal_kernel(order, keep, cap, me_ref, target_ref, weights_ref, total_ref, *refs):
    groups = len(order)
    ins, (out_any, blocks, wide, held, sems) = refs[:groups], refs[groups:]
    rows, slots, orbitals = wide.shape
    live = groups * keep
    for s, ref in zip(order, ins):
        base = moved(me_ref[0], s, groups, -1) * cap
        for k in range(cap):
            blocks[base + k] = ref[k * rows : (k + 1) * rows, :].astype(F32)
    blocks[groups * cap] = jnp.zeros((rows, orbitals), F32)
    places = []
    for slot in range(slots):
        t = target_ref[slot]
        alive = t < live
        at = jnp.where(alive, lax.rem(t, groups) * cap + lax.rem(lax.div(t, groups), cap), groups * cap)
        weight = jnp.where(alive, weights_ref[slot], F32(0.0))
        factor = jnp.full((1, LANES), weight * live, F32) / total_ref[0:1, :]
        places.append((at, factor[:, 0:1]))
    step = rows // sems.shape[0]
    copies = []
    for h in range(sems.shape[0]):
        band = slice(h * step, (h + 1) * step)
        for slot, (at, factor) in enumerate(places):
            wide[band, slot, :] = blocks[at, band, :] * factor
        held[band] = wide[band].astype(BF16)
        copies.append(pltpu.make_async_copy(held.at[band], out_any.at[band], sems.at[h]))
        copies[-1].start()
    for copy in copies:
        copy.wait()


def call(kernel, outs, scalars, held, arrays, scratch, name, flops=0, vmem=VMEM, place=pltpu.VMEM):
    smem = pl.BlockSpec(memory_space=pltpu.SMEM)
    full = pl.BlockSpec(memory_space=pltpu.VMEM)
    size = sum(x.size * x.dtype.itemsize for x in list(arrays) + list(outs))
    return pl.pallas_call(
        kernel,
        out_shape=outs,
        in_specs=[smem] * len(scalars) + [pl.BlockSpec(memory_space=pl.ANY)] * len(held) + [full] * len(arrays),
        out_specs=[pl.BlockSpec(memory_space=place)] * len(outs),
        scratch_shapes=scratch,
        compiler_params=pltpu.CompilerParams(vmem_limit_bytes=vmem * 2**20),
        cost_estimate=pl.CostEstimate(flops=flops, bytes_accessed=size, transcendentals=0),
        name=name,
    )(*scalars, *held, *arrays)


def body(walkers, one_body, fields, field_diag, chol, weights, target):
    rows, slots, orbitals = walkers.shape
    vec_count, occupied, _ = chol.shape
    n, groups = lax.axis_size("blk"), lax.axis_size("grp")
    keep = slots // 2
    half = keep // 2
    cap = -(-slots // groups)
    slab = half * rows
    shape = jax.ShapeDtypeStruct
    grp = lax.axis_index("grp").reshape(1)
    blk = lax.axis_index("blk").reshape(1)
    core = lax.rem(blk, 2)

    def to_list(x, s):
        return lax.ppermute(x, "grp", [(i, moved(i, s, groups, 1)) for i in range(groups)]) if s else x

    def to_block(x, s, e):
        if not s and not e:
            return x
        return lax.ppermute(x, "blk", [(i, 2 * moved(i // 2, s, n // 2, 1) + (i % 2 ^ e)) for i in range(n)])

    order = [0] + sorted(range(1, groups), key=lambda s: (s & 1, -s))
    chunks = orbitals // LANES
    sibling = to_block(chol, 0, 1)
    width = orbitals + tail_blocks(cap * (2 * chunks + 1) + 3, cap * rows) * LANES
    routed = call(
        functools.partial(route_kernel, keep, cap),
        [shape((cap * rows, width), BF16)] * groups,
        [grp],
        [target, weights, walkers, fields, field_diag],
        [],
        [
            pltpu.SMEM(target.shape, target.dtype),
            pltpu.SMEM(weights.shape, weights.dtype),
            pltpu.VMEM(walkers.shape, walkers.dtype),
            pltpu.VMEM(fields.shape, fields.dtype),
            pltpu.VMEM(field_diag.shape, field_diag.dtype),
            pltpu.VMEM((rows, slots, orbitals), F32),
            pltpu.VMEM((groups * cap + 1, rows, orbitals), F32),
            pltpu.VMEM((slots, 2 * chunks + 4, LANES), F32),
            pltpu.VMEM((groups * cap + 1, 2 * chunks + 4, LANES), F32),
            pltpu.SemaphoreType.DMA((5,)),
        ],
        "route",
        vmem=ROUTE_VMEM,
    )
    (kept,) = call(
        stage_kernel,
        [shape(routed[0].shape, BF16)],
        [],
        [routed[0]],
        [],
        [pltpu.SemaphoreType.DMA((1,))],
        "keep",
    )
    (own,) = call(
        stage_kernel,
        [shape(chol.shape, chol.dtype)],
        [],
        [chol, kept],
        [],
        [pltpu.SemaphoreType.DMA((1,))],
        "stage",
        vmem=STAGE_VMEM,
    )
    routed = [to_list(routed[s], s) if s else kept for s in order]
    routed[1], sibling = lax.optimization_barrier((routed[1], sibling))
    payload = shape((chunks * slab + 2 * half * chunks, LANES), BF16)
    same, other, same2, other2, weight_sum, pick = call(
        functools.partial(merge_kernel, order, keep, cap, orbitals),
        [payload] * 4 + [shape((8, LANES), F32), shape((groups * keep, LANES), F32)],
        [core],
        [own],
        routed,
        [],
        "merge",
    )
    (held_body,) = call(
        stage_kernel,
        [shape(one_body.shape, one_body.dtype)],
        [],
        [one_body, weight_sum],
        [],
        [pltpu.SemaphoreType.DMA((1,))],
        "hold",
    )
    chips = n // 2
    gathered = {}
    for s, e in [hop for hop in hops(n) if hop[1]] + [hop for hop in hops(n) if not hop[1]]:
        if leading(s, e, chips) == s and 2 * s >= chips:
            gathered[s, e] = to_block(other if e else same, s, e)
    for s, e in hops(n):
        if leading(s, e, chips) == s and 2 * s < chips and (s, e) != (0, 1):
            gathered[s, e] = to_block(other2 if e else same2, s, e)
    for s, e in hops(n):
        top = leading(s, e, chips)
        if top != s:
            gathered[s, e] = to_block(gathered[top, e], s ^ top, 0)
    (last,) = call(after_kernel, [payload], [], [], [other2, gathered.get((chips // 2, 0), same2)], [], "after")
    gathered[0, 1] = to_block(last, 0, 1)
    gathered = [gathered[hop] for hop in arrivals(n)]
    held = F32 if rows % 16 else BF16
    parts = call(
        functools.partial(fock_kernel, n, half),
        [shape((slab, orbitals), BF16)] * n,
        [blk],
        [],
        [held_body, own, sibling] + gathered,
        [
            pltpu.VMEM((half, n, rows, orbitals), held),
            pltpu.VMEM((half * occupied, orbitals), BF16),
            pltpu.VMEM((half * occupied, 2 * vec_count * occupied), BF16),
            pltpu.VMEM((half, n, rows, orbitals), held),
        ],
        "fock",
        flops=2 * n * slab * orbitals * (orbitals + 4 * vec_count * occupied),
    )
    parts = dict(zip(hops(n), parts))
    for s, e in returns(n):
        via = [hop for hop in hops(n) if hop[1] == e and hop[0] != s and leading(*hop, chips) == s]
        if via:
            later = [hop for hop in returns(n) if hop[0] < s and hop != (0, 0) and (hop[1] == e or 2 * hop[0] < chips)]
            out = call(
                functools.partial(add_kernel, len(later)),
                [shape((slab, orbitals), BF16)] * (1 + len(later)),
                [],
                [],
                [parts[hop] for hop in later] + [parts[s, e]] + [to_block(parts[hop], hop[0] ^ s, 0) for hop in via],
                [],
                "add",
            )
            parts.update(zip([(s, e)] + later, out))
    backs = [to_block(parts[hop], *hop) for hop in returns(n)]
    back = call(
        functools.partial(sum_kernel, n, keep, cap, groups),
        [shape((cap * rows, orbitals), BF16)] * groups,
        [core],
        [],
        [pick] + backs,
        [],
        "sum",
    )
    back = [to_list(back[s], s) for s in order]
    (out,) = call(
        functools.partial(deal_kernel, order, keep, cap),
        [shape(walkers.shape, BF16)],
        [grp, target, weights],
        [],
        [weight_sum] + back,
        [
            pltpu.VMEM((groups * cap + 1, rows, orbitals), F32),
            pltpu.VMEM(walkers.shape, F32),
            pltpu.VMEM(walkers.shape, BF16),
            pltpu.SemaphoreType.DMA((2,)),
        ],
        "deal",
        place=pl.ANY,
    )
    return out


def solution(mesh):
    in_specs = (
        P("blk", "grp", None),
        P(),
        P("grp", "blk"),
        P("blk", None),
        P("blk", None, None),
        P("grp"),
        P("grp"),
    )
    out_specs = P("blk", "grp", None)
    return jax.shard_map(body, mesh=mesh, in_specs=in_specs, out_specs=out_specs, check_vma=False)
```

```python
import functools
import math
import jax
import jax.numpy as jnp
from jax import lax
from jax.experimental import pallas as pl
from jax.experimental.pallas import tpu as pltpu
from jax.sharding import PartitionSpec as P

F32 = jnp.float32
BF16 = jnp.bfloat16
LANES = 128
VMEM = 24
ROUTE_VMEM = 56
STAGE_VMEM = 48


def terms(value, count):
    out = []
    for _ in range(count):
        term = value.astype(BF16).astype(F32)
        out.append(term)
        value = value - term
    return out


def tail_blocks(count, slab):
    return -(-count // slab)


def write_tail(out_ref, start, lines):
    slab = out_ref.shape[0]
    for b in range(tail_blocks(lines.shape[0], slab)):
        part = lines[b * slab : (b + 1) * slab]
        if part.shape[0] < slab:
            part = jnp.concatenate([part, jnp.zeros((slab - part.shape[0], LANES), F32)], axis=0)
        out_ref[:, start + b * LANES : start + (b + 1) * LANES] = part.astype(BF16)


def read_tail(ref, start, count):
    parts = [ref[:, c : c + LANES].astype(F32) for c in range(start, ref.shape[1], LANES)]
    whole = parts[0] if len(parts) == 1 else jnp.concatenate(parts, axis=0)
    return whole[0:count]


def wide_mask(line, width):
    return jnp.concatenate([line] * (width // LANES), axis=1) > 0


def stage_kernel(*refs):
    sems = refs[-1]
    count = sems.shape[0]
    copies = [pltpu.make_async_copy(refs[i], refs[i - count - 1], sems.at[i]) for i in range(count)]
    for copy in copies:
        copy.start()
    for copy in copies:
        copy.wait()


def route_kernel(keep, cap, me_ref, target_any, weights_any, walkers_any, fields_any, diag_any, *refs):
    *outs, target_ref, weights_ref, walkers_ref, fields_ref, diag_ref, wide, blocks, parts, lines, sems = refs
    pairs = (
        (walkers_any, walkers_ref),
        (target_any, target_ref),
        (weights_any, weights_ref),
        (fields_any, fields_ref),
        (diag_any, diag_ref),
    )
    copies = [pltpu.make_async_copy(a, b, sems.at[i]) for i, (a, b) in enumerate(pairs)]
    for copy in copies:
        copy.start()
    rows, slots, orbitals = walkers_ref.shape
    vec_count = fields_ref.shape[1]
    chunks = orbitals // LANES
    groups = len(outs)
    live = groups * keep
    blocks[...] = jnp.zeros(blocks.shape, F32)
    lines[...] = jnp.zeros(lines.shape, F32)
    for copy in copies:
        copy.wait()
    wide[...] = walkers_ref[...].astype(F32)
    exponent = fields_ref[:, 0:1] * diag_ref[0:1, :]
    for g in range(1, vec_count):
        exponent = exponent + fields_ref[:, g : g + 1] * diag_ref[g : g + 1, :]
    for i, term in enumerate(terms(exponent, 2)):
        for c in range(chunks):
            parts[:, i * chunks + c, :] = term[:, c * LANES : (c + 1) * LANES]
    weight = F32(0.0)
    for slot in range(slots):
        t = target_ref[slot]
        alive = t < live
        weight = weight + jnp.where(alive, weights_ref[slot], F32(0.0))
        turn = lax.div(t, groups)
        at = jnp.where(alive, lax.rem(t, groups) * cap + lax.rem(turn, cap), groups * cap)
        blocks[at] = wide[:, slot, :]
        parts[slot, 2 * chunks : 2 * chunks + 1, :] = jnp.full((1, LANES), (turn + 1).astype(F32), F32)
        lines[at] = parts[slot]
    sums = terms(jnp.full((1, LANES), weight, F32), 3)
    for s, out in enumerate(outs):
        base = moved(me_ref[0], s, groups, 1) * cap
        out[:, 0:orbitals] = jnp.concatenate([blocks[base + k] for k in range(cap)], axis=0).astype(BF16)
        tail = [lines[base + k][0 : 2 * chunks + 1] for k in range(cap)]
        write_tail(out, orbitals, jnp.concatenate(tail + sums, axis=0))


def merge_kernel(order, keep, cap, orbitals, core_ref, when, *refs):
    ins, (same_ref, other_ref, same2_ref, other2_ref, weight_ref, pick_ref) = refs[: len(order)], refs[len(order) :]
    half = keep // 2
    rows = ins[0].shape[0] // cap
    slab = half * rows
    chunks = orbitals // LANES
    each = 2 * chunks + 1
    weight = jnp.zeros((1, LANES), F32)
    walker = [jnp.zeros((rows, orbitals), F32)] * keep
    line = [jnp.zeros((2 * chunks, LANES), F32)] * keep
    for s, ref in zip(order, ins):
        tail = read_tail(ref, orbitals, cap * each + 3)
        weight = weight + (tail[cap * each : cap * each + 1] + tail[cap * each + 1 : cap * each + 2] + tail[cap * each + 2 :])
        for k in range(cap):
            flag = tail[(k + 1) * each - 1 : (k + 1) * each]
            block = ref[k * rows : (k + 1) * rows, 0:orbitals].astype(F32)
            part = tail[k * each : (k + 1) * each - 1]
            for m in range(k, keep, cap):
                mine = jnp.where(flag == m + 1, F32(1.0), F32(0.0))
                pick_ref[s * keep + m : s * keep + m + 1, :] = mine
                walker[m] = jnp.where(wide_mask(mine, orbitals), block, walker[m])
                line[m] = jnp.where(mine > 0, part, line[m])
    weight_ref[...] = jnp.broadcast_to(weight, weight_ref.shape)
    first = core_ref[0] == 0
    for out, order in ((same_ref, (0, 1)), (other_ref, (1, 0))):
        picked = []
        for k in range(half):
            a, b = order[0] * half + k, order[1] * half + k
            picked.append(jnp.where(first, line[a], line[b]))
            block = jnp.where(first, walker[a], walker[b])
            for c in range(chunks):
                at = c * slab + k * rows
                out[at : at + rows, :] = block[:, c * LANES : (c + 1) * LANES].astype(BF16)
        tail = [p[i * chunks : (i + 1) * chunks] for i in range(2) for p in picked]
        out[chunks * slab :, :] = jnp.concatenate(tail, axis=0).astype(BF16)
    same2_ref[...] = same_ref[...]
    other2_ref[...] = other_ref[...]


def power(size):
    return size & (size - 1) == 0


def moved(me, s, size, sign):
    if power(size):
        return me ^ s if isinstance(me, int) else lax.bitwise_xor(me, jnp.int32(s))
    at = me + (s if sign > 0 else size - s)
    return at % size if isinstance(me, int) else lax.rem(at, size)


def hops(n):
    chips = n // 2
    far = list(range(chips // 2, chips)) + list(range(1, chips // 2))
    return [(0, 0)] + [(s, e) for s in far for e in range(2)] + [(0, 1)]


def after_kernel(source_ref, when_ref, out_ref):
    out_ref[...] = source_ref[...]


def arrivals(n):
    return hops(n)[:1] + hops(n)[:0:-1]


def leading(s, e, chips):
    return 1 << (s.bit_length() - 1) if s and e and power(chips) else s


def returns(n):
    return [(s, e) for s, e in hops(n) if leading(s, e, n // 2) == s]


def add_kernel(count, *refs):
    outs = refs[len(refs) - 1 - count :]
    ins = refs[: len(refs) - 1 - count]
    total = ins[count][...].astype(F32)
    for ref in ins[count + 1 :]:
        total = total + ref[...].astype(F32)
    outs[0][...] = total.astype(BF16)
    for i in range(count):
        outs[1 + i][...] = ins[i][...]


def partner(blk, s, e, n, sign):
    chip = moved(lax.div(blk, 2), s, n // 2, sign)
    core = lax.rem(blk, 2)
    return 2 * chip + (core if e == 0 else 1 - core)


def fock_kernel(n, half, blk_ref, body_ref, own_ref, sib_ref, *refs):
    ins, outs = refs[:n], refs[n : 2 * n]
    prop, carried, coup, result = refs[2 * n :]
    vec_count, occupied, orbitals = own_ref.shape
    slab = outs[0].shape[0]
    rows = slab // half
    chunks = orbitals // LANES
    blk = blk_ref[0]
    exponent = jnp.zeros((2 * half * chunks, LANES), F32)
    for ref in ins:
        exponent = exponent + ref[chunks * slab :, :].astype(F32)
    growth = jnp.exp(exponent[0 : half * chunks] + exponent[half * chunks :])
    for ref, (s, e) in zip(ins, arrivals(n)):
        source = partner(blk, s, e, n, -1)
        for w in range(half):
            for c in range(chunks):
                piece = ref[c * slab + w * rows : c * slab + (w + 1) * rows, :].astype(F32)
                piece = piece * growth[w * chunks + c : w * chunks + c + 1]
                prop[w, source, :, c * LANES : (c + 1) * LANES] = piece.astype(prop.dtype)
    scaled = jnp.concatenate([prop[w, i] for w in range(half) for i in range(n)], axis=0).astype(BF16)
    carried[...] = jnp.dot(scaled, body_ref[...], preferred_element_type=F32).astype(BF16)
    batch = math.gcd(vec_count, 4)
    for c, ref in enumerate((own_ref, sib_ref)):
        for g in range(0, vec_count, batch):
            left = ref[g : g + batch].reshape(batch * occupied, orbitals)
            s = lax.dot_general(left, carried[...], (((1,), (1,)), ((), ())), preferred_element_type=F32).astype(BF16)
            for k in range(batch):
                at = (c * vec_count + g + k) * occupied
                for w in range(half):
                    coup[w * occupied : (w + 1) * occupied, at : at + occupied] = s[
                        k * occupied : (k + 1) * occupied, w * occupied : (w + 1) * occupied
                    ]
    tile = 256 if orbitals % 256 == 0 else orbitals
    depth = vec_count * occupied
    for t in range(0, orbitals, tile):
        total = jnp.dot(
            coup[:, :depth],
            own_ref[:, :, t : t + tile].reshape(depth, tile),
            preferred_element_type=F32,
        )
        total = total + jnp.dot(
            coup[:, depth:],
            sib_ref[:, :, t : t + tile].reshape(depth, tile),
            preferred_element_type=F32,
        )
        for w in range(half):
            for i in range(n):
                at = w * occupied + i * rows
                result[w, i, :, t : t + tile] = total[at : at + rows].astype(result.dtype)
    for out, (s, e) in zip(outs, hops(n)):
        to = partner(blk, s, e, n, 1)
        for w in range(half):
            out[w * rows : (w + 1) * rows, :] = result[w, to].astype(BF16)


def sum_kernel(n, keep, cap, groups, core_ref, pick_ref, *refs):
    known = returns(n)
    ins, outs = refs[: len(known)], refs[len(known) :]
    slab, orbitals = ins[0].shape
    half = keep // 2
    rows = slab // half
    halves = []
    for e in range(2):
        same = [ref for ref, (_, other) in zip(ins, known) if other == e]
        total = same[0][...].astype(F32)
        for ref in same[1:]:
            total = total + ref[...].astype(F32)
        halves.append(total)
    first = core_ref[0] == 0
    whole = [jnp.where(first, halves[0], halves[1]), jnp.where(first, halves[1], halves[0])]
    walker = [whole[m // half][(m % half) * rows : (m % half + 1) * rows] for m in range(keep)]
    for s, out in enumerate(outs):
        source = s if power(groups) else (groups - s) % groups
        for k in range(cap):
            value = jnp.zeros((rows, orbitals), F32)
            for m in range(k, keep, cap):
                mine = pick_ref[source * keep + m : source * keep + m + 1, :]
                value = jnp.where(wide_mask(mine, orbitals), walker[m], value)
            out[k * rows : (k + 1) * rows, :] = value.astype(BF16)


def deal_kernel(order, keep, cap, me_ref, target_ref, weights_ref, total_ref, *refs):
    groups = len(order)
    ins, (out_any, blocks, wide, held, sems) = refs[:groups], refs[groups:]
    rows, slots, orbitals = wide.shape
    live = groups * keep
    for s, ref in zip(order, ins):
        base = moved(me_ref[0], s, groups, -1) * cap
        for k in range(cap):
            blocks[base + k] = ref[k * rows : (k + 1) * rows, :].astype(F32)
    blocks[groups * cap] = jnp.zeros((rows, orbitals), F32)
    places = []
    for slot in range(slots):
        t = target_ref[slot]
        alive = t < live
        at = jnp.where(alive, lax.rem(t, groups) * cap + lax.rem(lax.div(t, groups), cap), groups * cap)
        weight = jnp.where(alive, weights_ref[slot], F32(0.0))
        factor = jnp.full((1, LANES), weight * live, F32) / total_ref[0:1, :]
        places.append((at, factor[:, 0:1]))
    step = rows // sems.shape[0]
    copies = []
    for h in range(sems.shape[0]):
        band = slice(h * step, (h + 1) * step)
        for slot, (at, factor) in enumerate(places):
            wide[band, slot, :] = blocks[at, band, :] * factor
        held[band] = wide[band].astype(BF16)
        copies.append(pltpu.make_async_copy(held.at[band], out_any.at[band], sems.at[h]))
        copies[-1].start()
    for copy in copies:
        copy.wait()


def call(kernel, outs, scalars, held, arrays, scratch, name, flops=0, vmem=VMEM, place=pltpu.VMEM):
    smem = pl.BlockSpec(memory_space=pltpu.SMEM)
    full = pl.BlockSpec(memory_space=pltpu.VMEM)
    size = sum(x.size * x.dtype.itemsize for x in list(arrays) + list(outs))
    return pl.pallas_call(
        kernel,
        out_shape=outs,
        in_specs=[smem] * len(scalars) + [pl.BlockSpec(memory_space=pl.ANY)] * len(held) + [full] * len(arrays),
        out_specs=[pl.BlockSpec(memory_space=place)] * len(outs),
        scratch_shapes=scratch,
        compiler_params=pltpu.CompilerParams(vmem_limit_bytes=vmem * 2**20),
        cost_estimate=pl.CostEstimate(flops=flops, bytes_accessed=size, transcendentals=0),
        name=name,
    )(*scalars, *held, *arrays)


def body(walkers, one_body, fields, field_diag, chol, weights, target):
    rows, slots, orbitals = walkers.shape
    vec_count, occupied, _ = chol.shape
    n, groups = lax.axis_size("blk"), lax.axis_size("grp")
    keep = slots // 2
    half = keep // 2
    cap = -(-slots // groups)
    slab = half * rows
    shape = jax.ShapeDtypeStruct
    grp = lax.axis_index("grp").reshape(1)
    blk = lax.axis_index("blk").reshape(1)
    core = lax.rem(blk, 2)

    def to_list(x, s):
        return lax.ppermute(x, "grp", [(i, moved(i, s, groups, 1)) for i in range(groups)]) if s else x

    def to_block(x, s, e):
        if not s and not e:
            return x
        return lax.ppermute(x, "blk", [(i, 2 * moved(i // 2, s, n // 2, 1) + (i % 2 ^ e)) for i in range(n)])

    order = [0] + sorted(range(1, groups), key=lambda s: (s & 1, -s))
    chunks = orbitals // LANES
    sibling = to_block(chol, 0, 1)
    width = orbitals + tail_blocks(cap * (2 * chunks + 1) + 3, cap * rows) * LANES
    routed = call(
        functools.partial(route_kernel, keep, cap),
        [shape((cap * rows, width), BF16)] * groups,
        [grp],
        [target, weights, walkers, fields, field_diag],
        [],
        [
            pltpu.SMEM(target.shape, target.dtype),
            pltpu.SMEM(weights.shape, weights.dtype),
            pltpu.VMEM(walkers.shape, walkers.dtype),
            pltpu.VMEM(fields.shape, fields.dtype),
            pltpu.VMEM(field_diag.shape, field_diag.dtype),
            pltpu.VMEM((rows, slots, orbitals), F32),
            pltpu.VMEM((groups * cap + 1, rows, orbitals), F32),
            pltpu.VMEM((slots, 2 * chunks + 4, LANES), F32),
            pltpu.VMEM((groups * cap + 1, 2 * chunks + 4, LANES), F32),
            pltpu.SemaphoreType.DMA((5,)),
        ],
        "route",
        vmem=ROUTE_VMEM,
    )
    (kept,) = call(
        stage_kernel,
        [shape(routed[0].shape, BF16)],
        [],
        [routed[0]],
        [],
        [pltpu.SemaphoreType.DMA((1,))],
        "keep",
    )
    (own,) = call(
        stage_kernel,
        [shape(chol.shape, chol.dtype)],
        [],
        [chol, kept],
        [],
        [pltpu.SemaphoreType.DMA((1,))],
        "stage",
        vmem=STAGE_VMEM,
    )
    routed = [to_list(routed[s], s) if s else kept for s in order]
    payload = shape((chunks * slab + 2 * half * chunks, LANES), BF16)
    same, other, same2, other2, weight_sum, pick = call(
        functools.partial(merge_kernel, order, keep, cap, orbitals),
        [payload] * 4 + [shape((8, LANES), F32), shape((groups * keep, LANES), F32)],
        [core],
        [own],
        routed,
        [],
        "merge",
    )
    (held_body,) = call(
        stage_kernel,
        [shape(one_body.shape, one_body.dtype)],
        [],
        [one_body, weight_sum],
        [],
        [pltpu.SemaphoreType.DMA((1,))],
        "hold",
    )
    chips = n // 2
    gathered = {}
    for s, e in [hop for hop in hops(n) if hop[1]] + [hop for hop in hops(n) if not hop[1]]:
        if leading(s, e, chips) == s and 2 * s >= chips:
            gathered[s, e] = to_block(other if e else same, s, e)
    for s, e in hops(n):
        if leading(s, e, chips) == s and 2 * s < chips and (s, e) != (0, 1):
            gathered[s, e] = to_block(other2 if e else same2, s, e)
    for s, e in hops(n):
        top = leading(s, e, chips)
        if top != s:
            gathered[s, e] = to_block(gathered[top, e], s ^ top, 0)
    (last,) = call(after_kernel, [payload], [], [], [other2, gathered.get((chips // 2, 0), same2)], [], "after")
    gathered[0, 1] = to_block(last, 0, 1)
    gathered = [gathered[hop] for hop in arrivals(n)]
    held = F32 if rows % 16 else BF16
    parts = call(
        functools.partial(fock_kernel, n, half),
        [shape((slab, orbitals), BF16)] * n,
        [blk],
        [],
        [held_body, own, sibling] + gathered,
        [
            pltpu.VMEM((half, n, rows, orbitals), held),
            pltpu.VMEM((half * occupied, orbitals), BF16),
            pltpu.VMEM((half * occupied, 2 * vec_count * occupied), BF16),
            pltpu.VMEM((half, n, rows, orbitals), held),
        ],
        "fock",
        flops=2 * n * slab * orbitals * (orbitals + 4 * vec_count * occupied),
    )
    parts = dict(zip(hops(n), parts))
    for s, e in returns(n):
        via = [hop for hop in hops(n) if hop[1] == e and hop[0] != s and leading(*hop, chips) == s]
        if via:
            later = [hop for hop in returns(n) if hop[0] < s and hop != (0, 0) and (hop[1] == e or 2 * hop[0] < chips)]
            out = call(
                functools.partial(add_kernel, len(later)),
                [shape((slab, orbitals), BF16)] * (1 + len(later)),
                [],
                [],
                [parts[hop] for hop in later] + [parts[s, e]] + [to_block(parts[hop], hop[0] ^ s, 0) for hop in via],
                [],
                "add",
            )
            parts.update(zip([(s, e)] + later, out))
    backs = [to_block(parts[hop], *hop) for hop in returns(n)]
    back = call(
        functools.partial(sum_kernel, n, keep, cap, groups),
        [shape((cap * rows, orbitals), BF16)] * groups,
        [core],
        [],
        [pick] + backs,
        [],
        "sum",
    )
    last_order = [0] + sorted(range(1, groups), key=lambda s: -bin(s).count("1"))
    back = [to_list(back[s], s) for s in last_order]
    (out,) = call(
        functools.partial(deal_kernel, last_order, keep, cap),
        [shape(walkers.shape, BF16)],
        [grp, target, weights],
        [],
        [weight_sum] + back,
        [
            pltpu.VMEM((groups * cap + 1, rows, orbitals), F32),
            pltpu.VMEM(walkers.shape, F32),
            pltpu.VMEM(walkers.shape, BF16),
            pltpu.SemaphoreType.DMA((2,)),
        ],
        "deal",
        place=pl.ANY,
    )
    return out


def solution(mesh):
    in_specs = (
        P("blk", "grp", None),
        P(),
        P("grp", "blk"),
        P("blk", None),
        P("blk", None, None),
        P("grp"),
        P("grp"),
    )
    out_specs = P("blk", "grp", None)
    return jax.shard_map(body, mesh=mesh, in_specs=in_specs, out_specs=out_specs, check_vma=False)
```

```python
import functools
import math
import jax
import jax.numpy as jnp
from jax import lax
from jax.experimental import pallas as pl
from jax.experimental.pallas import tpu as pltpu
from jax.sharding import PartitionSpec as P

F32 = jnp.float32
BF16 = jnp.bfloat16
LANES = 128
VMEM = 24
ROUTE_VMEM = 56
STAGE_VMEM = 48


def terms(value, count):
    out = []
    for _ in range(count):
        term = value.astype(BF16).astype(F32)
        out.append(term)
        value = value - term
    return out


def tail_blocks(count, slab):
    return -(-count // slab)


def write_tail(out_ref, start, lines):
    slab = out_ref.shape[0]
    for b in range(tail_blocks(lines.shape[0], slab)):
        part = lines[b * slab : (b + 1) * slab]
        if part.shape[0] < slab:
            part = jnp.concatenate([part, jnp.zeros((slab - part.shape[0], LANES), F32)], axis=0)
        out_ref[:, start + b * LANES : start + (b + 1) * LANES] = part.astype(BF16)


def read_tail(ref, start, count):
    parts = [ref[:, c : c + LANES].astype(F32) for c in range(start, ref.shape[1], LANES)]
    whole = parts[0] if len(parts) == 1 else jnp.concatenate(parts, axis=0)
    return whole[0:count]


def wide_mask(line, width):
    return jnp.concatenate([line] * (width // LANES), axis=1) > 0


def stage_kernel(*refs):
    sems = refs[-1]
    count = sems.shape[0]
    copies = [pltpu.make_async_copy(refs[i], refs[i - count - 1], sems.at[i]) for i in range(count)]
    for copy in copies:
        copy.start()
    for copy in copies:
        copy.wait()


def route_kernel(keep, cap, me_ref, target_any, weights_any, walkers_any, fields_any, diag_any, *refs):
    *outs, target_ref, weights_ref, walkers_ref, fields_ref, diag_ref, wide, blocks, parts, lines, sems = refs
    pairs = (
        (walkers_any, walkers_ref),
        (target_any, target_ref),
        (weights_any, weights_ref),
        (fields_any, fields_ref),
        (diag_any, diag_ref),
    )
    copies = [pltpu.make_async_copy(a, b, sems.at[i]) for i, (a, b) in enumerate(pairs)]
    for copy in copies:
        copy.start()
    rows, slots, orbitals = walkers_ref.shape
    vec_count = fields_ref.shape[1]
    chunks = orbitals // LANES
    groups = len(outs)
    live = groups * keep
    blocks[...] = jnp.zeros(blocks.shape, F32)
    lines[...] = jnp.zeros(lines.shape, F32)
    for copy in copies:
        copy.wait()
    wide[...] = walkers_ref[...].astype(F32)
    exponent = fields_ref[:, 0:1] * diag_ref[0:1, :]
    for g in range(1, vec_count):
        exponent = exponent + fields_ref[:, g : g + 1] * diag_ref[g : g + 1, :]
    for i, term in enumerate(terms(exponent, 2)):
        for c in range(chunks):
            parts[:, i * chunks + c, :] = term[:, c * LANES : (c + 1) * LANES]
    weight = F32(0.0)
    for slot in range(slots):
        t = target_ref[slot]
        alive = t < live
        weight = weight + jnp.where(alive, weights_ref[slot], F32(0.0))
        turn = lax.div(t, groups)
        at = jnp.where(alive, lax.rem(t, groups) * cap + lax.rem(turn, cap), groups * cap)
        blocks[at] = wide[:, slot, :]
        parts[slot, 2 * chunks : 2 * chunks + 1, :] = jnp.full((1, LANES), (turn + 1).astype(F32), F32)
        lines[at] = parts[slot]
    sums = terms(jnp.full((1, LANES), weight, F32), 3)
    for s, out in enumerate(outs):
        base = moved(me_ref[0], s, groups, 1) * cap
        out[:, 0:orbitals] = jnp.concatenate([blocks[base + k] for k in range(cap)], axis=0).astype(BF16)
        tail = [lines[base + k][0 : 2 * chunks + 1] for k in range(cap)]
        write_tail(out, orbitals, jnp.concatenate(tail + sums, axis=0))


def merge_kernel(order, keep, cap, orbitals, core_ref, when, *refs):
    ins, (same_ref, other_ref, same2_ref, other2_ref, weight_ref, pick_ref) = refs[: len(order)], refs[len(order) :]
    half = keep // 2
    rows = ins[0].shape[0] // cap
    slab = half * rows
    chunks = orbitals // LANES
    each = 2 * chunks + 1
    weight = jnp.zeros((1, LANES), F32)
    walker = [jnp.zeros((rows, orbitals), F32)] * keep
    line = [jnp.zeros((2 * chunks, LANES), F32)] * keep
    for s, ref in zip(order, ins):
        tail = read_tail(ref, orbitals, cap * each + 3)
        weight = weight + (tail[cap * each : cap * each + 1] + tail[cap * each + 1 : cap * each + 2] + tail[cap * each + 2 :])
        for k in range(cap):
            flag = tail[(k + 1) * each - 1 : (k + 1) * each]
            block = ref[k * rows : (k + 1) * rows, 0:orbitals].astype(F32)
            part = tail[k * each : (k + 1) * each - 1]
            for m in range(k, keep, cap):
                mine = jnp.where(flag == m + 1, F32(1.0), F32(0.0))
                pick_ref[s * keep + m : s * keep + m + 1, :] = mine
                walker[m] = jnp.where(wide_mask(mine, orbitals), block, walker[m])
                line[m] = jnp.where(mine > 0, part, line[m])
    weight_ref[...] = jnp.broadcast_to(weight, weight_ref.shape)
    first = core_ref[0] == 0
    for out, order in ((same_ref, (0, 1)), (other_ref, (1, 0))):
        picked = []
        for k in range(half):
            a, b = order[0] * half + k, order[1] * half + k
            picked.append(jnp.where(first, line[a], line[b]))
            block = jnp.where(first, walker[a], walker[b])
            for c in range(chunks):
                at = c * slab + k * rows
                out[at : at + rows, :] = block[:, c * LANES : (c + 1) * LANES].astype(BF16)
        tail = [p[i * chunks : (i + 1) * chunks] for i in range(2) for p in picked]
        out[chunks * slab :, :] = jnp.concatenate(tail, axis=0).astype(BF16)
    same2_ref[...] = same_ref[...]
    other2_ref[...] = other_ref[...]


def power(size):
    return size & (size - 1) == 0


def moved(me, s, size, sign):
    if power(size):
        return me ^ s if isinstance(me, int) else lax.bitwise_xor(me, jnp.int32(s))
    at = me + (s if sign > 0 else size - s)
    return at % size if isinstance(me, int) else lax.rem(at, size)


def hops(n):
    chips = n // 2
    far = list(range(chips // 2, chips)) + list(range(1, chips // 2))
    return [(0, 0)] + [(s, e) for s in far for e in range(2)] + [(0, 1)]


def after_kernel(source_ref, when_ref, out_ref):
    out_ref[...] = source_ref[...]


def arrivals(n):
    return hops(n)[:1] + hops(n)[:0:-1]


def leading(s, e, chips):
    return 1 << (s.bit_length() - 1) if s and e and power(chips) else s


def returns(n):
    return [(s, e) for s, e in hops(n) if leading(s, e, n // 2) == s]


def add_kernel(count, *refs):
    outs = refs[len(refs) - 1 - count :]
    ins = refs[: len(refs) - 1 - count]
    total = ins[count][...].astype(F32)
    for ref in ins[count + 1 :]:
        total = total + ref[...].astype(F32)
    outs[0][...] = total.astype(BF16)
    for i in range(count):
        outs[1 + i][...] = ins[i][...]


def partner(blk, s, e, n, sign):
    chip = moved(lax.div(blk, 2), s, n // 2, sign)
    core = lax.rem(blk, 2)
    return 2 * chip + (core if e == 0 else 1 - core)


def fock_kernel(n, half, blk_ref, body_ref, own_ref, sib_ref, *refs):
    ins, outs = refs[:n], refs[n : 2 * n]
    prop, carried, coup, result = refs[2 * n :]
    vec_count, occupied, orbitals = own_ref.shape
    slab = outs[0].shape[0]
    rows = slab // half
    chunks = orbitals // LANES
    blk = blk_ref[0]
    exponent = jnp.zeros((2 * half * chunks, LANES), F32)
    for ref in ins:
        exponent = exponent + ref[chunks * slab :, :].astype(F32)
    growth = jnp.exp(exponent[0 : half * chunks] + exponent[half * chunks :])
    for ref, (s, e) in zip(ins, arrivals(n)):
        source = partner(blk, s, e, n, -1)
        for w in range(half):
            for c in range(chunks):
                piece = ref[c * slab + w * rows : c * slab + (w + 1) * rows, :].astype(F32)
                piece = piece * growth[w * chunks + c : w * chunks + c + 1]
                prop[w, source, :, c * LANES : (c + 1) * LANES] = piece.astype(prop.dtype)
    scaled = jnp.concatenate([prop[w, i] for w in range(half) for i in range(n)], axis=0).astype(BF16)
    carried[...] = jnp.dot(scaled, body_ref[...], preferred_element_type=F32).astype(BF16)
    batch = math.gcd(vec_count, 4)
    for c, ref in enumerate((own_ref, sib_ref)):
        for g in range(0, vec_count, batch):
            left = ref[g : g + batch].reshape(batch * occupied, orbitals)
            s = lax.dot_general(left, carried[...], (((1,), (1,)), ((), ())), preferred_element_type=F32).astype(BF16)
            for k in range(batch):
                at = (c * vec_count + g + k) * occupied
                for w in range(half):
                    coup[w * occupied : (w + 1) * occupied, at : at + occupied] = s[
                        k * occupied : (k + 1) * occupied, w * occupied : (w + 1) * occupied
                    ]
    tile = 256 if orbitals % 256 == 0 else orbitals
    depth = vec_count * occupied
    for t in range(0, orbitals, tile):
        total = jnp.dot(
            coup[:, :depth],
            own_ref[:, :, t : t + tile].reshape(depth, tile),
            preferred_element_type=F32,
        )
        total = total + jnp.dot(
            coup[:, depth:],
            sib_ref[:, :, t : t + tile].reshape(depth, tile),
            preferred_element_type=F32,
        )
        for w in range(half):
            for i in range(n):
                at = w * occupied + i * rows
                result[w, i, :, t : t + tile] = total[at : at + rows].astype(result.dtype)
    for out, (s, e) in zip(outs, hops(n)):
        to = partner(blk, s, e, n, 1)
        for w in range(half):
            out[w * rows : (w + 1) * rows, :] = result[w, to].astype(BF16)


def sum_kernel(n, keep, cap, groups, core_ref, pick_ref, *refs):
    known = returns(n)
    ins, outs = refs[: len(known)], refs[len(known) :]
    slab, orbitals = ins[0].shape
    half = keep // 2
    rows = slab // half
    halves = []
    for e in range(2):
        same = [ref for ref, (_, other) in zip(ins, known) if other == e]
        total = same[0][...].astype(F32)
        for ref in same[1:]:
            total = total + ref[...].astype(F32)
        halves.append(total)
    first = core_ref[0] == 0
    whole = [jnp.where(first, halves[0], halves[1]), jnp.where(first, halves[1], halves[0])]
    walker = [whole[m // half][(m % half) * rows : (m % half + 1) * rows] for m in range(keep)]
    for s, out in enumerate(outs):
        source = s if power(groups) else (groups - s) % groups
        for k in range(cap):
            value = jnp.zeros((rows, orbitals), F32)
            for m in range(k, keep, cap):
                mine = pick_ref[source * keep + m : source * keep + m + 1, :]
                value = jnp.where(wide_mask(mine, orbitals), walker[m], value)
            out[k * rows : (k + 1) * rows, :] = value.astype(BF16)


def deal_kernel(order, keep, cap, me_ref, target_ref, weights_ref, total_ref, *refs):
    groups = len(order)
    ins, (out_any, blocks, wide, held, sems) = refs[:groups], refs[groups:]
    rows, slots, orbitals = wide.shape
    live = groups * keep
    for s, ref in zip(order, ins):
        base = moved(me_ref[0], s, groups, -1) * cap
        for k in range(cap):
            blocks[base + k] = ref[k * rows : (k + 1) * rows, :].astype(F32)
    blocks[groups * cap] = jnp.zeros((rows, orbitals), F32)
    places = []
    for slot in range(slots):
        t = target_ref[slot]
        alive = t < live
        at = jnp.where(alive, lax.rem(t, groups) * cap + lax.rem(lax.div(t, groups), cap), groups * cap)
        weight = jnp.where(alive, weights_ref[slot], F32(0.0))
        factor = jnp.full((1, LANES), weight * live, F32) / total_ref[0:1, :]
        places.append((at, factor[:, 0:1]))
    step = rows // sems.shape[0]
    copies = []
    for h in range(sems.shape[0]):
        band = slice(h * step, (h + 1) * step)
        for slot, (at, factor) in enumerate(places):
            wide[band, slot, :] = blocks[at, band, :] * factor
        held[band] = wide[band].astype(BF16)
        copies.append(pltpu.make_async_copy(held.at[band], out_any.at[band], sems.at[h]))
        copies[-1].start()
    for copy in copies:
        copy.wait()


def call(kernel, outs, scalars, held, arrays, scratch, name, flops=0, vmem=VMEM, place=pltpu.VMEM):
    smem = pl.BlockSpec(memory_space=pltpu.SMEM)
    full = pl.BlockSpec(memory_space=pltpu.VMEM)
    size = sum(x.size * x.dtype.itemsize for x in list(arrays) + list(outs))
    return pl.pallas_call(
        kernel,
        out_shape=outs,
        in_specs=[smem] * len(scalars) + [pl.BlockSpec(memory_space=pl.ANY)] * len(held) + [full] * len(arrays),
        out_specs=[pl.BlockSpec(memory_space=place)] * len(outs),
        scratch_shapes=scratch,
        compiler_params=pltpu.CompilerParams(vmem_limit_bytes=vmem * 2**20),
        cost_estimate=pl.CostEstimate(flops=flops, bytes_accessed=size, transcendentals=0),
        name=name,
    )(*scalars, *held, *arrays)


def body(walkers, one_body, fields, field_diag, chol, weights, target):
    rows, slots, orbitals = walkers.shape
    vec_count, occupied, _ = chol.shape
    n, groups = lax.axis_size("blk"), lax.axis_size("grp")
    keep = slots // 2
    half = keep // 2
    cap = -(-slots // groups)
    slab = half * rows
    shape = jax.ShapeDtypeStruct
    grp = lax.axis_index("grp").reshape(1)
    blk = lax.axis_index("blk").reshape(1)
    core = lax.rem(blk, 2)

    def to_list(x, s):
        return lax.ppermute(x, "grp", [(i, moved(i, s, groups, 1)) for i in range(groups)]) if s else x

    def to_block(x, s, e):
        if not s and not e:
            return x
        return lax.ppermute(x, "blk", [(i, 2 * moved(i // 2, s, n // 2, 1) + (i % 2 ^ e)) for i in range(n)])

    order = [0] + sorted(range(1, groups), key=lambda s: (s & 1, -s))
    chunks = orbitals // LANES
    sibling = to_block(chol, 0, 1)
    width = orbitals + tail_blocks(cap * (2 * chunks + 1) + 3, cap * rows) * LANES
    routed = call(
        functools.partial(route_kernel, keep, cap),
        [shape((cap * rows, width), BF16)] * groups,
        [grp],
        [target, weights, walkers, fields, field_diag],
        [],
        [
            pltpu.SMEM(target.shape, target.dtype),
            pltpu.SMEM(weights.shape, weights.dtype),
            pltpu.VMEM(walkers.shape, walkers.dtype),
            pltpu.VMEM(fields.shape, fields.dtype),
            pltpu.VMEM(field_diag.shape, field_diag.dtype),
            pltpu.VMEM((rows, slots, orbitals), F32),
            pltpu.VMEM((groups * cap + 1, rows, orbitals), F32),
            pltpu.VMEM((slots, 2 * chunks + 4, LANES), F32),
            pltpu.VMEM((groups * cap + 1, 2 * chunks + 4, LANES), F32),
            pltpu.SemaphoreType.DMA((5,)),
        ],
        "route",
        vmem=ROUTE_VMEM,
    )
    (kept,) = call(
        stage_kernel,
        [shape(routed[0].shape, BF16)],
        [],
        [routed[0]],
        [],
        [pltpu.SemaphoreType.DMA((1,))],
        "keep",
    )
    (own,) = call(
        stage_kernel,
        [shape(chol.shape, chol.dtype)],
        [],
        [chol, kept],
        [],
        [pltpu.SemaphoreType.DMA((1,))],
        "stage",
        vmem=STAGE_VMEM,
    )
    routed = [to_list(routed[s], s) if s else kept for s in order]
    payload = shape((chunks * slab + 2 * half * chunks, LANES), BF16)
    same, other, same2, other2, weight_sum, pick = call(
        functools.partial(merge_kernel, order, keep, cap, orbitals),
        [payload] * 4 + [shape((8, LANES), F32), shape((groups * keep, LANES), F32)],
        [core],
        [own],
        routed,
        [],
        "merge",
    )
    (held_body,) = call(
        stage_kernel,
        [shape(one_body.shape, one_body.dtype)],
        [],
        [one_body, weight_sum],
        [],
        [pltpu.SemaphoreType.DMA((1,))],
        "hold",
    )
    chips = n // 2
    gathered = {}
    for s, e in [hop for hop in hops(n) if hop[1]] + [hop for hop in hops(n) if not hop[1]]:
        if leading(s, e, chips) == s and 2 * s >= chips:
            gathered[s, e] = to_block(other if e else same, s, e)
    for s, e in hops(n):
        if leading(s, e, chips) == s and 2 * s < chips and (s, e) != (0, 1):
            gathered[s, e] = to_block(other2 if e else same2, s, e)
    for s, e in hops(n):
        top = leading(s, e, chips)
        if top != s:
            gathered[s, e] = to_block(gathered[top, e], s ^ top, 0)
    (last,) = call(after_kernel, [payload], [], [], [other2, gathered.get((chips - 1, 0), same2)], [], "after")
    gathered[0, 1] = to_block(last, 0, 1)
    gathered = [gathered[hop] for hop in arrivals(n)]
    held = F32 if rows % 16 else BF16
    parts = call(
        functools.partial(fock_kernel, n, half),
        [shape((slab, orbitals), BF16)] * n,
        [blk],
        [],
        [held_body, own, sibling] + gathered,
        [
            pltpu.VMEM((half, n, rows, orbitals), held),
            pltpu.VMEM((half * occupied, orbitals), BF16),
            pltpu.VMEM((half * occupied, 2 * vec_count * occupied), BF16),
            pltpu.VMEM((half, n, rows, orbitals), held),
        ],
        "fock",
        flops=2 * n * slab * orbitals * (orbitals + 4 * vec_count * occupied),
    )
    parts = dict(zip(hops(n), parts))
    for s, e in returns(n):
        via = [hop for hop in hops(n) if hop[1] == e and hop[0] != s and leading(*hop, chips) == s]
        if via:
            later = [hop for hop in returns(n) if hop[0] < s and hop != (0, 0) and (hop[1] == e or 2 * hop[0] < chips)]
            out = call(
                functools.partial(add_kernel, len(later)),
                [shape((slab, orbitals), BF16)] * (1 + len(later)),
                [],
                [],
                [parts[hop] for hop in later] + [parts[s, e]] + [to_block(parts[hop], hop[0] ^ s, 0) for hop in via],
                [],
                "add",
            )
            parts.update(zip([(s, e)] + later, out))
    backs = [to_block(parts[hop], *hop) for hop in returns(n)]
    back = call(
        functools.partial(sum_kernel, n, keep, cap, groups),
        [shape((cap * rows, orbitals), BF16)] * groups,
        [core],
        [],
        [pick] + backs,
        [],
        "sum",
    )
    back = [to_list(back[s], s) for s in order]
    (out,) = call(
        functools.partial(deal_kernel, order, keep, cap),
        [shape(walkers.shape, BF16)],
        [grp, target, weights],
        [],
        [weight_sum] + back,
        [
            pltpu.VMEM((groups * cap + 1, rows, orbitals), F32),
            pltpu.VMEM(walkers.shape, F32),
            pltpu.VMEM(walkers.shape, BF16),
            pltpu.SemaphoreType.DMA((2,)),
        ],
        "deal",
        place=pl.ANY,
    )
    return out


def solution(mesh):
    in_specs = (
        P("blk", "grp", None),
        P(),
        P("grp", "blk"),
        P("blk", None),
        P("blk", None, None),
        P("grp"),
        P("grp"),
    )
    out_specs = P("blk", "grp", None)
    return jax.shard_map(body, mesh=mesh, in_specs=in_specs, out_specs=out_specs, check_vma=False)
```
